128 devices in a mesh: dp: 4 (over y_lo, core), space: 32 (over z, y_hi, x).
Axes of the slice: x: 4, y: 4 (y_hi: 2, y_lo: 2; y = y_hi * 2 + y_lo), z: 4, core: 2. Of those that a mesh axis runs over, the one named last changes fastest.
Arguments:
- image_in: bfloat16 [5376, 42, 256], P(('dp', 'space')), may hold values from -46 to 46
- cotangent: bfloat16 [5376, 42, 256], P(('dp', 'space')), may hold values from -6 to 6
- regions: int32 [5376, 42], P(('dp', 'space')), may hold values from 0 to 4, as said below
- first_gain: float32 [256], replicated, may hold values from 0.5 to 1.5
- first_bias: float32 [256], replicated, may hold values from -2 to 2
- qkv_weight: bfloat16 [256, 768], replicated, may hold values from -0.375 to 0.375
- query_bias: float32 [256], replicated, may hold values from -2 to 2
- value_bias: float32 [256], replicated, may hold values from -2 to 2
- position_table: float32 [169, 8], replicated, may hold values from -4 to 4
- proj_weight: bfloat16 [256, 256], replicated, may hold values from -1 to 1
- proj_bias: float32 [256], replicated, may hold values from -2 to 2
- second_gain: float32 [256], replicated, may hold values from 0.5 to 1.5
- second_bias: float32 [256], replicated, may hold values from -2 to 2
- up_weight: bfloat16 [256, 1024], replicated, may hold values from -0.375 to 0.375
- up_bias: float32 [1024], replicated, may hold values from -2 to 2
- down_weight: bfloat16 [1024, 256], replicated, may hold values from -0.1875 to 0.1875
- down_bias: float32 [256], replicated, may hold values from -2 to 2
Outputs:
- block_out: bfloat16 [5376, 42, 256], P(('dp', 'space'))
- image_grad: bfloat16 [5376, 42, 256], P(('dp', 'space'))
- first_gain_grad: float32 [256], replicated
- first_bias_grad: float32 [256], replicated
- qkv_weight_grad: float32 [256, 768], replicated
- query_bias_grad: float32 [256], replicated
- value_bias_grad: float32 [256], replicated
- position_table_grad: float32 [169, 8], replicated
- proj_weight_grad: float32 [256, 256], replicated
- proj_bias_grad: float32 [256], replicated
- second_gain_grad: float32 [256], replicated
- second_bias_grad: float32 [256], replicated
- up_weight_grad: float32 [256, 1024], replicated
- up_bias_grad: float32 [1024], replicated
- down_weight_grad: float32 [1024, 256], replicated
- down_bias_grad: float32 [256], replicated
The draws below stay inside these ranges and needn't reach their ends.
Inputs may be any that keep to these rules, and one draw needn't show every extreme that they name: `regions`: pages of 56 rows follow each other along the rows. A page's label is 4 on its padding (some last columns of every page, and possibly some last rows), else 2 for its first 3 rows plus 1 for its first 3 columns.
All inputs are finite; a program needn't handle non-finite values.
Results may differ from the reference program's by a relative error of at most 0.017.
Values may be sent and summed in bfloat16 or wider, within the bound.
No kernel may reach another device: no remote copies, remote signals or barrier semaphores. Data moves between devices by JAX's collectives and lax.ppermute only.
A program may use at most 128 MiB of HBM per device.

```python
import math
import jax
import jax.numpy as jnp
import numpy as np
from jax import lax

D = 256
HEADS = 8
HEAD_DIM = 32
MLP = 1024
WIN = 7
SHIFT = 3
PAGE_ROWS = 56
COLS = 42
ROWS = 5376
PAGES = 96
N_DP = 4


def draw_image_in(key, part):
    key = jax.random.fold_in(key, 2)
    basic_key, row_key, chan_key = jax.random.split(key, 3)
    basic_draw = jnp.clip(jax.random.normal(basic_key, (ROWS, COLS, D), jnp.float32), -4.0, 4.0)
    row_scale = jnp.exp(jax.random.uniform(row_key, (ROWS, COLS, 1), jnp.float32, -1.2, 1.2))
    chan_scale = jnp.exp(jax.random.uniform(chan_key, (D,), jnp.float32, -1.2, 1.2))
    return (basic_draw * row_scale * chan_scale).astype(jnp.bfloat16)


def draw_regions(key, part):
    key = jax.random.fold_in(key, 1)
    height_key, width_key = jax.random.split(key)
    heights = jax.random.randint(height_key, (PAGES,), PAGE_ROWS // 2, PAGE_ROWS + 1)
    widths = jax.random.randint(width_key, (PAGES,), COLS // 2 + 1, COLS)
    row_ids = jnp.arange(ROWS, dtype=jnp.int32)
    page_ids = row_ids // PAGE_ROWS
    in_page = row_ids % PAGE_ROWS
    col_ids = jnp.arange(COLS, dtype=jnp.int32)
    padded = (in_page[:, None] >= heights[page_ids][:, None]) | (col_ids[None, :] >= widths[page_ids][:, None])
    inside = 2 * (in_page[:, None] < SHIFT).astype(jnp.int32) + (col_ids[None, :] < SHIFT).astype(jnp.int32)
    return jnp.where(padded, 4, inside).astype(jnp.int32)


def steps_of(key, extent, pieces, low, largest):
    def one(dim, blocks):
        steps = jax.random.uniform(jax.random.fold_in(jax.random.fold_in(key, 6), dim), (blocks,), jnp.float32, low / len(pieces), largest / len(pieces))
        return jnp.repeat(jnp.exp(steps), extent[dim] // blocks).reshape((-1,) + (1,) * (len(extent) - dim - 1))

    level = one(*pieces[0])
    for cut in pieces[1:]:
        level = level * one(*cut)
    return level


def noise(stream_key, extent, width, limit, cuts=(), kind=jnp.bfloat16):
    loudness = steps_of(stream_key, extent, cuts, -0.22, 0.18) if cuts else 1.0
    drawn = jax.random.normal(stream_key, extent, jnp.float32) * width * loudness
    return jnp.minimum(jnp.maximum(drawn, -limit), limit).astype(kind)


def setup_inputs(seed: int = 0) -> dict:
    keys = jax.random.split(jax.random.key(seed), 18)
    return {
        "image_in": draw_image_in(jax.random.fold_in(keys[17], 71), 0),
        "cotangent": noise(keys[1], (ROWS, COLS, D), 1.0, 6.0, ((0, 128),)),
        "regions": draw_regions(jax.random.fold_in(keys[17], 71), 0),
        "first_gain": jnp.clip(1.0 + 0.1 * jax.random.normal(keys[3], (D,), jnp.float32), 0.5, 1.5),
        "first_bias": noise(keys[4], (D,), 0.3, 2.0, (), jnp.float32),
        "qkv_weight": noise(keys[5], (D, 3 * D), D ** -0.5, 0.375),
        "query_bias": noise(keys[6], (D,), 0.3, 2.0, (), jnp.float32),
        "value_bias": noise(keys[7], (D,), 0.3, 2.0, (), jnp.float32),
        "position_table": noise(keys[8], ((2 * WIN - 1) * (2 * WIN - 1), HEADS), 1.0, 4.0, (), jnp.float32),
        "proj_weight": noise(keys[9], (D, D), (D // 8) ** -0.5, 1.0),
        "proj_bias": noise(keys[10], (D,), 0.3, 2.0, (), jnp.float32),
        "second_gain": jnp.clip(1.0 + 0.1 * jax.random.normal(keys[11], (D,), jnp.float32), 0.5, 1.5),
        "second_bias": noise(keys[12], (D,), 0.3, 2.0, (), jnp.float32),
        "up_weight": noise(keys[13], (D, MLP), D ** -0.5, 0.375),
        "up_bias": noise(keys[14], (MLP,), 0.3, 2.0, (), jnp.float32),
        "down_weight": noise(keys[15], (MLP, D), MLP ** -0.5, 0.1875),
        "down_bias": noise(keys[16], (D,), 0.3, 2.0, (), jnp.float32),
    }


@jax.custom_vjp
def low(v):
    return lax.optimization_barrier(v.astype(jnp.bfloat16)).astype(jnp.float32)

@jax.custom_vjp
def low_back(v):
    return v

def low_keep(v):
    return (low(v), None)

def low_pass(kept, grad):
    return (grad,)

def back_keep(v):
    return (v, None)

def back_low(kept, grad):
    return (low(grad),)
low.defvjp(low_keep, low_pass)
low_back.defvjp(back_keep, back_low)
epsilon = 1e-05
highest = lax.Precision.HIGHEST

def relative_index():
    position = np.arange(WIN * WIN)
    first = position // WIN
    second = position % WIN
    table = (first[:, None] - first[None, :] + WIN - 1) * (2 * WIN - 1) + second[:, None] - second[None, :] + WIN - 1
    return table.astype(np.int32)

def layer_norm(values, gain, bias):
    center = values - lax.optimization_barrier(jnp.mean(values, -1, keepdims=True))
    variance = lax.optimization_barrier(jnp.mean(center * center, -1, keepdims=True))
    return center * lax.rsqrt(variance + epsilon) * gain + bias

def windows_of(grid_field):
    groups, height, breadth = grid_field.shape[:3]
    trailing = grid_field.shape[3:]
    grid_field = grid_field.reshape((groups, height // WIN, WIN, breadth // WIN, WIN) + trailing)
    grid_field = jnp.swapaxes(grid_field, 2, 3)
    return grid_field.reshape((groups * (height // WIN) * (breadth // WIN), WIN * WIN) + trailing)

def field_of(tokens, groups, height, breadth):
    trailing = tokens.shape[2:]
    grid_field = tokens.reshape((groups, height // WIN, breadth // WIN, WIN, WIN) + trailing)
    grid_field = jnp.swapaxes(grid_field, 2, 3)
    return grid_field.reshape((groups, height, breadth) + trailing)

def reference(image_in, cotangent, regions, first_gain, first_bias, qkv_weight, query_bias, value_bias, position_table, proj_weight, proj_bias, second_gain, second_bias, up_weight, up_bias, down_weight, down_bias):
    groups = N_DP
    height = ROWS // N_DP
    breadth = COLS
    scale = 1.0 / math.sqrt(HEAD_DIM)

    def shifted(grid_field):
        grid_field = grid_field.reshape((groups, height) + grid_field.shape[1:])
        return jnp.roll(grid_field, (-SHIFT, -SHIFT), (1, 2))

    def unshifted(grid_field):
        grid_field = jnp.roll(grid_field, (SHIFT, SHIFT), (1, 2))
        return grid_field.reshape((ROWS,) + grid_field.shape[2:])
    labels = windows_of(shifted(regions))
    allowed = labels[:, :, None] == labels[:, None, :]
    window_count = labels.shape[0]
    rel_index = relative_index()

    def forward(image, gain_one, bias_one, w_qkv, bias_query, bias_value, table, w_proj, bias_proj, gain_two, bias_two, w_up, bias_up, w_down, bias_down):
        tokens = windows_of(shifted(image)).reshape(-1, D)
        first = low(layer_norm(tokens, gain_one, bias_one))
        qkv = jnp.dot(first, w_qkv, precision=highest) + jnp.concatenate([bias_query, jnp.zeros_like(bias_query), bias_value])
        qkv = low(low_back(qkv))
        queries = qkv[:, :D].reshape(window_count, WIN * WIN, HEADS, HEAD_DIM)
        key_part = qkv[:, D:2 * D].reshape(window_count, WIN * WIN, HEADS, HEAD_DIM)
        value_part = qkv[:, 2 * D:].reshape(window_count, WIN * WIN, HEADS, HEAD_DIM)
        rel_bias = jnp.transpose(table[rel_index], (2, 0, 1))
        logits = jnp.einsum('wqhd,wkhd->whqk', queries, key_part, precision=highest) * scale + rel_bias
        logits = low_back(jnp.where(allowed[:, None], logits, -1000000000.0))
        attend = low(jax.nn.softmax(logits, -1))
        mixed = jnp.einsum('whqk,wkhd->wqhd', attend, value_part, precision=highest).reshape(-1, D)
        mixed = low(low_back(mixed))
        branch = low_back(jnp.dot(mixed, w_proj, precision=highest) + bias_proj)
        resid = tokens + branch
        second = low(layer_norm(resid, gain_two, bias_two))
        inner_pre = low_back(jnp.dot(second, w_up, precision=highest) + bias_up)
        active = low(jax.nn.gelu(inner_pre, approximate=False))
        result = resid + jnp.dot(active, w_down, precision=highest) + bias_down
        return unshifted(field_of(result.reshape(window_count, WIN * WIN, D), groups, height, breadth))
    primals = (image_in.astype(jnp.float32), first_gain, first_bias, qkv_weight.astype(jnp.float32), query_bias, value_bias, position_table, proj_weight.astype(jnp.float32), proj_bias, second_gain, second_bias, up_weight.astype(jnp.float32), up_bias, down_weight.astype(jnp.float32), down_bias)
    result, pullback = jax.vjp(forward, *primals)
    gradients = pullback(cotangent.astype(jnp.float32))
    return (result.astype(jnp.bfloat16), gradients[0].astype(jnp.bfloat16), gradients[1], gradients[2], gradients[3], gradients[4], gradients[5], gradients[6], gradients[7], gradients[8], gradients[9], gradients[10], gradients[11], gradients[12], gradients[13], gradients[14])
```

```python
import math

import jax
import jax.numpy as jnp
import numpy as np
from jax import lax
from jax.experimental import pallas as pl
from jax.experimental.pallas import tpu as pltpu
from jax.sharding import PartitionSpec as P

WIN = 7
SHIFT = 3
HEADS = 8
TOKENS = WIN * WIN
PAD = 56
LANES = 64
ENTRIES = (2 * WIN - 1) * (2 * WIN - 1)
COLS = 42
WINDOWS = COLS // WIN
STRIP = WINDOWS * PAD
ROW = 48
D = 256
MLP = 1024
BF16 = jnp.bfloat16
F32 = jnp.float32
epsilon = 1e-05
neg = -1000000000.0
AXES = ("dp", "space")


def from_behind(block, axis, distance):
    devices = range(lax.axis_size(axis))
    route = [((i - distance) % len(devices), i) for i in devices]
    return lax.ppermute(block, axis, route)


def gather_matrix():
    out = np.zeros((STRIP, WIN * ROW), np.float32)
    for w in range(WINDOWS):
        for i in range(WIN):
            for j in range(WIN):
                out[w * PAD + i * WIN + j, i * ROW + (w * WIN + j + SHIFT) % COLS] = 1.0
    return out


def label_matrices():
    spread = np.zeros((COLS, WINDOWS * 2 * LANES), np.float32)
    rows = np.zeros((WIN, WINDOWS * 2 * LANES), np.float32)
    for w in range(WINDOWS):
        for copy in range(2):
            for i in range(WIN):
                for j in range(WIN):
                    col = (w * 2 + copy) * LANES + i * WIN + j
                    spread[(w * WIN + j + SHIFT) % COLS, col] = 1.0
                    rows[i, col] = 1.0
    return spread, rows


def table_onehot():
    out = np.zeros((PAD, LANES, ENTRIES), np.float32)
    for k in range(TOKENS):
        for q in range(TOKENS):
            di = q // WIN - k // WIN + WIN - 1
            dj = q % WIN - k % WIN + WIN - 1
            out[k, q, di * (2 * WIN - 1) + dj] = 1.0
    return out


def dot(a, b):
    return jnp.dot(a, b, preferred_element_type=F32)


def dot_nt(a, b):
    return lax.dot_general(a, b, (((1,), (1,)), ((), ())), preferred_element_type=F32)


def dot_tn(a, b):
    return lax.dot_general(a, b, (((0,), (0,)), ((), ())), preferred_element_type=F32)


def normalize(values):
    center = values - jnp.mean(values, -1, keepdims=True)
    variance = jnp.mean(center * center, -1, keepdims=True)
    recip_dev = lax.rsqrt(variance + epsilon)
    return center * recip_dev, recip_dev


def norm_backward(upstream, normal_part, recip_dev, gain):
    scaled = upstream * gain
    inner_mean = jnp.mean(scaled, -1, keepdims=True)
    cross_mean = jnp.mean(scaled * normal_part, -1, keepdims=True)
    return recip_dev * (scaled - inner_mean - normal_part * cross_mean)


def col_sum(values):
    return jnp.sum(values, 0, keepdims=True)


def raster_rows(ref, halo, s):
    last = s == pl.num_programs(0) - 1
    blank = jnp.zeros((ROW - COLS, D), BF16)
    rows = []
    for i in range(WIN):
        g = s * WIN + i + SHIFT
        if i < WIN - SHIFT:
            value = ref[g]
        else:
            value = jnp.where(last, halo[i - (WIN - SHIFT)], ref[jnp.minimum(g, COLS - 1)])
        rows += [value, blank]
    return jnp.concatenate(rows, 0)


def put_rows(raster, out, tail, s):
    last = s == pl.num_programs(0) - 1
    for i in range(WIN):
        value = raster[i * ROW : i * ROW + COLS]
        g = s * WIN + i + SHIFT
        if i < WIN - SHIFT:
            out[g] = value
        else:

            @pl.when(last)
            def _():
                tail[i - (WIN - SHIFT)] = value

            @pl.when(jnp.logical_not(last))
            def _():
                out[g] = value


def head_blocks(values):
    lane = lax.broadcasted_iota(jnp.int32, (LANES, D), 1) // (D // HEADS)
    return jnp.concatenate(
        [jnp.where(lane == h, values, 0.0).astype(BF16) for h in range(HEADS)], 0
    )


def pad_rows(values):
    return jnp.concatenate([values, jnp.zeros((LANES - PAD,) + values.shape[1:], values.dtype)], 0)


def heads_to_lanes(values):
    turned = values.T
    return jnp.concatenate([turned[h * LANES : (h + 1) * LANES] for h in range(HEADS)], 1)


def forward_kernel(
    image, image_halo, cot, cot_halo, labels, spread, spread_rows, gather, scatter, bias_t,
    gain_one, bias_one, w_qkv, b_qkv, w_proj, b_proj, gain_two, bias_two,
    w_up, b_up, w_down, b_down,
    block_out, tail, qkv_out, attend_out, d_mixed_out, d_resid_out, tokens_out,
    up_grad, down_grad_t, proj_grad, up_sums, sums,
    lane_labels, second_all, d_inner_all, active_all, cot_all, mixed_all, d_branch_all,
):
    s = pl.program_id(0)
    steps = pl.num_programs(0)
    scale = 1.0 / math.sqrt(D // HEADS)

    @pl.when(s == 0)
    def _():
        spread_labels = dot(labels[...], spread[...])
        for n in range(COLS // WIN):
            part = spread_labels[n * WIN : (n + 1) * WIN] * spread_rows[...]
            lane_labels[n] = jnp.broadcast_to(jnp.sum(part, 0, keepdims=True), (8, part.shape[1]))
        up_sums[...] = jnp.zeros_like(up_sums)
        sums[...] = jnp.zeros_like(sums)

    rows = pl.ds(pl.multiple_of(s * STRIP, 16), STRIP)
    tokens = dot(gather[...], raster_rows(image, image_halo, s))
    cot_f32 = dot(gather[...], raster_rows(cot, cot_halo, s))
    cot_low = cot_f32.astype(BF16)
    cot_all[rows] = cot_low
    tokens_out[...] = tokens.astype(BF16)
    normal_one, _ = normalize(tokens)
    first_low = (normal_one * gain_one[...] + bias_one[...]).astype(BF16)
    qkv = dot(first_low, w_qkv[...]) + b_qkv[...]
    qkv_out[...] = qkv.astype(BF16)

    mixed_parts = []
    for w in range(WINDOWS):
        part = qkv[w * PAD : (w + 1) * PAD]
        query_blocks = head_blocks(pad_rows(part[:, :D]))
        value_blocks = head_blocks(pad_rows(part[:, 2 * D :]))
        key_low = part[:, D : 2 * D].astype(BF16)
        logits = dot_nt(key_low, query_blocks) * scale + bias_t[...]
        lane_label = lane_labels[s, 0:1, w * 128 : (w + 1) * 128]
        key_label = jnp.broadcast_to(lane_label, (128, 128)).T[:PAD]
        same = key_label == lane_label
        same = jnp.concatenate([same] * (HEADS // 2), 1)
        logits = jnp.where(same, logits, neg)
        powers = jnp.exp(logits - jnp.max(logits, 0, keepdims=True))
        attend = powers * (1.0 / jnp.sum(powers, 0, keepdims=True))
        attend_low = pad_rows(attend).astype(BF16)
        attend_out[w] = attend_low
        mixed_parts.append(dot(heads_to_lanes(attend_low), value_blocks)[:PAD])
    mixed_low = jnp.concatenate(mixed_parts, 0).astype(BF16)
    mixed_all[rows] = mixed_low

    resid = tokens + dot(mixed_low, w_proj[...]) + b_proj[...]
    normal_two, recip_two = normalize(resid)
    second_low = (normal_two * gain_two[...] + bias_two[...]).astype(BF16)
    second_all[rows] = second_low

    result = resid + b_down[...]
    d_second = jnp.zeros((STRIP, D), F32)
    for c in range(0, MLP, D):
        cols = slice(c, c + D)
        inner = dot(second_low, w_up[:, cols]) + b_up[:, cols]
        gauss = jnp.exp(-0.5 * inner * inner)
        t = 1.0 / (1.0 + (0.3275911 * 0.7071067811865476) * jnp.abs(inner))
        poly = t * (
            0.5 * 0.254829592
            + t * (0.5 * -0.284496736 + t * (0.5 * 1.421413741 + t * (0.5 * -1.453152027 + t * (0.5 * 1.061405429))))
        )
        side = poly * gauss
        cumulative = jnp.where(inner >= 0.0, 1.0 - side, side)
        active_low = (inner * cumulative).astype(BF16)
        active_all[rows, cols] = active_low
        result = result + dot(active_low, w_down[cols])
        slope = cumulative + inner * gauss * 0.3989422804014327
        d_inner = (dot_nt(cot_low, w_down[cols]) * slope).astype(BF16)
        d_inner_all[rows, cols] = d_inner
        up_sums[0:1, cols] += col_sum(d_inner.astype(F32))
        d_second = d_second + dot_nt(d_inner, w_up[:, cols])
    put_rows(dot(scatter[...], result.astype(BF16)).astype(BF16), block_out, tail, s)

    d_resid = cot_f32 + norm_backward(d_second, normal_two, recip_two, gain_two[...])
    d_branch = d_resid.astype(BF16)
    d_branch_all[rows] = d_branch
    d_resid_out[...] = d_resid
    d_mixed_out[...] = dot_nt(d_branch, w_proj[...]).astype(BF16)
    sums[0:1] += col_sum(d_second * normal_two)
    sums[1:2] += col_sum(d_second)
    sums[2:3] += col_sum(d_branch.astype(F32))
    sums[3:4] += col_sum(cot_f32)

    @pl.when(s == steps - 1)
    def _():
        up_grad[...] = dot_tn(second_all[...], d_inner_all[...])
        down_grad_t[...] = dot_tn(cot_all[...], active_all[...])
        proj_grad[...] = dot_tn(mixed_all[...], d_branch_all[...])


def backward_kernel(
    qkv_in, attend_in, d_mixed_in, d_resid_in, tokens_in, scatter, gain_one, bias_one, w_qkv,
    image_grad, tail, qkv_grad, logit_sums, qkv_sums, sums,
    first_all, d_qkv_all,
):
    s = pl.program_id(0)
    steps = pl.num_programs(0)
    scale = 1.0 / math.sqrt(D // HEADS)

    @pl.when(s == 0)
    def _():
        logit_sums[...] = jnp.zeros_like(logit_sums)
        qkv_sums[...] = jnp.zeros_like(qkv_sums)
        sums[...] = jnp.zeros_like(sums)

    rows = pl.ds(pl.multiple_of(s * STRIP, 16), STRIP)
    qkv = qkv_in[...].astype(F32)
    d_mixed = d_mixed_in[...].astype(F32)
    parts = []
    logit_total = logit_sums[...]
    for w in range(WINDOWS):
        part = qkv[w * PAD : (w + 1) * PAD]
        query_blocks = head_blocks(pad_rows(part[:, :D]))
        key_blocks = head_blocks(pad_rows(part[:, D : 2 * D]))
        value_low = part[:, 2 * D :].astype(BF16)
        mixed_blocks = head_blocks(pad_rows(d_mixed[w * PAD : (w + 1) * PAD]))
        attend_low = attend_in[w]
        attend = attend_low.astype(F32)[:PAD]
        d_attend = dot_nt(value_low, mixed_blocks)
        cross = jnp.sum(d_attend * attend, 0, keepdims=True)
        d_logits_low = pad_rows(attend * (d_attend - cross)).astype(BF16)
        logit_total = logit_total + d_logits_low.astype(F32)[:PAD]
        d_value = dot(attend_low, mixed_blocks)[:PAD]
        d_key = dot(d_logits_low, query_blocks)[:PAD] * scale
        d_query = dot(heads_to_lanes(d_logits_low), key_blocks)[:PAD] * scale
        parts.append(jnp.concatenate([d_query, d_key, d_value], 1))
    logit_sums[...] = logit_total
    d_qkv = jnp.concatenate(parts, 0).astype(BF16)
    d_qkv_all[rows] = d_qkv
    qkv_sums[0:1] += col_sum(d_qkv.astype(F32))

    normal_one, recip_one = normalize(tokens_in[...].astype(F32))
    first_all[rows] = (normal_one * gain_one[...] + bias_one[...]).astype(BF16)
    d_first = dot_nt(d_qkv, w_qkv[...])
    sums[0:1] += col_sum(d_first * normal_one)
    sums[1:2] += col_sum(d_first)
    grad = d_resid_in[...] + norm_backward(d_first, normal_one, recip_one, gain_one[...])
    put_rows(dot(scatter[...], grad.astype(BF16)).astype(BF16), image_grad, tail, s)

    @pl.when(s == steps - 1)
    def _():
        qkv_grad[...] = dot_tn(first_all[...], d_qkv_all[...])


def whole(shape):
    return pl.BlockSpec(shape, lambda s: (0,) * len(shape))


def strips(shape):
    return pl.BlockSpec(shape, lambda s: (s,) + (0,) * (len(shape) - 1))


def struct(shape, dtype):
    return jax.ShapeDtypeStruct(shape, dtype)


params = pltpu.CompilerParams(
    vmem_limit_bytes=56 * 1024 * 1024, dimension_semantics=("arbitrary",)
)


def run_forward(*args):
    n = COLS // WIN
    total = n * STRIP
    return pl.pallas_call(
        forward_kernel,
        grid=(n,),
        in_specs=[whole(a.shape) for a in args],
        out_specs=[
            whole((COLS, COLS, D)),
            whole((SHIFT, COLS, D)),
            strips((STRIP, 3 * D)),
            strips((WINDOWS, LANES, HEADS * LANES)),
            strips((STRIP, D)),
            strips((STRIP, D)),
            strips((STRIP, D)),
            whole((D, MLP)),
            whole((D, MLP)),
            whole((D, D)),
            whole((8, MLP)),
            whole((8, D)),
        ],
        out_shape=[
            struct((COLS, COLS, D), BF16),
            struct((SHIFT, COLS, D), BF16),
            struct((total, 3 * D), BF16),
            struct((n * WINDOWS, LANES, HEADS * LANES), BF16),
            struct((total, D), BF16),
            struct((total, D), F32),
            struct((total, D), BF16),
            struct((D, MLP), F32),
            struct((D, MLP), F32),
            struct((D, D), F32),
            struct((8, MLP), F32),
            struct((8, D), F32),
        ],
        scratch_shapes=[
            pltpu.VMEM((n, 8, WINDOWS * 2 * LANES), F32),
            pltpu.VMEM((total, D), BF16),
            pltpu.VMEM((total, MLP), BF16),
            pltpu.VMEM((total, MLP), BF16),
            pltpu.VMEM((total, D), BF16),
            pltpu.VMEM((total, D), BF16),
            pltpu.VMEM((total, D), BF16),
        ],
        compiler_params=params,
        name="forward_and_mlp_backward",
    )(*args)


def run_backward(*args):
    n = COLS // WIN
    total = n * STRIP
    in_specs = [
        strips((STRIP, 3 * D)),
        strips((WINDOWS, LANES, HEADS * LANES)),
        strips((STRIP, D)),
        strips((STRIP, D)),
        strips((STRIP, D)),
    ] + [whole(a.shape) for a in args[5:]]
    return pl.pallas_call(
        backward_kernel,
        grid=(n,),
        in_specs=in_specs,
        out_specs=[
            whole((COLS, COLS, D)),
            whole((SHIFT, COLS, D)),
            whole((D, 3 * D)),
            whole((PAD, HEADS * LANES)),
            whole((8, 3 * D)),
            whole((8, D)),
        ],
        out_shape=[
            struct((COLS, COLS, D), BF16),
            struct((SHIFT, COLS, D), BF16),
            struct((D, 3 * D), F32),
            struct((PAD, HEADS * LANES), F32),
            struct((8, 3 * D), F32),
            struct((8, D), F32),
        ],
        scratch_shapes=[
            pltpu.VMEM((total, D), BF16),
            pltpu.VMEM((total, 3 * D), BF16),
        ],
        compiler_params=params,
        name="attention_backward",
    )(*args)


def coords(index):
    dp, space = divmod(index, 32)
    return {"c": dp % 2, "y": dp // 2 + 2 * ((space // 4) % 2), "x": space % 4, "z": space // 8}


def index_of(c, y, x, z):
    return ((y % 2) * 2 + c) * 32 + z * 8 + (y // 2) * 4 + x


STEPS = (
    ("c", "c", 0),
    ("y", "x", 0),
    ("x", "z", 0),
    ("z", "y", 0),
    ("y", "x", 1),
    ("x", "z", 1),
    ("z", "y", 1),
)
HALVINGS = 4


def partners(step):
    out = []
    for i in range(128):
        at = coords(i)
        axis = step[at["c"]]
        to = dict(at)
        to[axis] = at[axis] ^ (1 << step[2])
        out.append((i, index_of(**to)))
    return out


def own_bit(step, at):
    bits = [(at[step[core]] >> step[2]) & 1 for core in range(2)]
    return jnp.where(at["c"] == 0, bits[0], bits[1])


def sum_everywhere(rows):
    me = lax.axis_index(AXES)
    at = coords(me)
    kept = []
    for step in STEPS[:HALVINGS]:
        half = rows.shape[0] // 2
        keep = own_bit(step, at)
        send = lax.dynamic_slice_in_dim(rows, (1 - keep) * half, half, 0).astype(BF16)
        got = lax.ppermute(send, AXES, partners(step))
        rows = lax.dynamic_slice_in_dim(rows, keep * half, half, 0) + got.astype(F32)
        kept.append(keep)
    low = rows.astype(BF16)
    for step in STEPS[HALVINGS:]:
        got = lax.ppermute(low, AXES, partners(step))
        low = (low.astype(F32) + got.astype(F32)).astype(BF16)
    for step, keep in zip(reversed(STEPS[:HALVINGS]), reversed(kept)):
        got = lax.ppermute(low, AXES, partners(step))
        first = jnp.where(keep == 0, low, got)
        second = jnp.where(keep == 0, got, low)
        low = jnp.concatenate([first, second], 0)
    return low


def body(
    image_in, cotangent, regions, first_gain, first_bias, qkv_weight, query_bias, value_bias,
    position_table, proj_weight, proj_bias, second_gain, second_bias, up_weight, up_bias,
    down_weight, down_bias,
):
    arrived = from_behind(
        (image_in[:SHIFT], cotangent[:SHIFT], regions[:SHIFT].astype(BF16)), "space", -1
    )
    labels = jnp.concatenate([regions[SHIFT:].astype(BF16), arrived[2]], 0)
    gather = gather_matrix()
    spread, spread_rows = label_matrices()
    onehot = jnp.asarray(table_onehot().reshape(PAD * LANES, ENTRIES))
    bias_t = lax.dot_general(
        position_table, onehot, (((0,), (1,)), ((), ())), precision=lax.Precision.HIGHEST
    )
    bias_t = jnp.transpose(bias_t.reshape(HEADS, PAD, LANES), (1, 0, 2)).reshape(PAD, HEADS * LANES)
    blank = np.where(np.arange(PAD) < TOKENS, 0.0, neg).astype(np.float32)[:, None]
    bias_t = bias_t + blank
    b_qkv = jnp.concatenate([query_bias, jnp.zeros_like(query_bias), value_bias])
    scatter = jnp.asarray(gather.T, BF16)
    (
        block_out, out_tail, qkv, attend, d_mixed, d_resid, tokens,
        up_grad, down_grad_t, proj_grad, up_sums, sums_two,
    ) = run_forward(
        image_in, arrived[0], cotangent, arrived[1], labels,
        jnp.asarray(spread, BF16), jnp.asarray(spread_rows), jnp.asarray(gather, BF16), scatter, bias_t,
        first_gain[None], first_bias[None], qkv_weight, b_qkv[None], proj_weight, proj_bias[None],
        second_gain[None], second_bias[None], up_weight, up_bias[None], down_weight, down_bias[None],
    )
    image_grad, grad_tail, qkv_grad, logit_sums, qkv_sums, sums_one = run_backward(
        qkv, attend, d_mixed, d_resid, tokens, scatter, first_gain[None], first_bias[None], qkv_weight
    )
    returned = from_behind((out_tail, grad_tail), "space", 1)
    block_out = lax.dynamic_update_slice(block_out, returned[0], (0, 0, 0))
    image_grad = lax.dynamic_update_slice(image_grad, returned[1], (0, 0, 0))
    terms = jnp.transpose(logit_sums.reshape(PAD, HEADS, LANES), (1, 0, 2)).reshape(HEADS, PAD * LANES)
    table_grad = jnp.dot(terms, onehot, precision=lax.Precision.HIGHEST)
    table_rows = jnp.pad(table_grad, ((0, 0), (0, D - ENTRIES)))
    pieces = (
        [up_grad[:, c : c + D] for c in range(0, MLP, D)]
        + [down_grad_t[:, c : c + D] for c in range(0, MLP, D)]
        + [qkv_grad[:, c : c + D] for c in range(0, 3 * D, D)]
        + [proj_grad]
        + [table_rows, sums_one[:2], sums_two[:4], up_sums[:1].reshape(4, D), qkv_sums[:1].reshape(3, D)]
    )
    packed = jnp.concatenate(pieces, 0)
    unit = 16 << HALVINGS
    packed = jnp.pad(packed, ((0, -packed.shape[0] % unit), (0, 0)))
    if lax.axis_size("dp") * lax.axis_size("space") == 128:
        total = sum_everywhere(packed).astype(F32)
    else:
        total = lax.psum(packed, AXES)
    wide = [total[i * D : (i + 1) * D] for i in range(12)]
    small = total[12 * D :]
    return (
        block_out,
        image_grad,
        small[8],
        small[9],
        jnp.concatenate(wide[8:11], 1),
        small[18],
        small[20],
        small[:HEADS, :ENTRIES].T,
        wide[11],
        small[12],
        small[10],
        small[11],
        jnp.concatenate(wide[0:4], 1),
        small[14:18].reshape(MLP),
        jnp.concatenate([w.T for w in wide[4:8]], 0),
        small[13],
    )


def solution(mesh):
    tokens = P(AXES, None, None)
    return jax.shard_map(
        body,
        mesh=mesh,
        in_specs=(tokens, tokens, P(AXES, None)) + (P(),) * 14,
        out_specs=(tokens, tokens) + (P(),) * 14,
        check_vma=False,
    )
```

```python
import math

import jax
import jax.numpy as jnp
import numpy as np
from jax import lax
from jax.experimental import pallas as pl
from jax.experimental.pallas import tpu as pltpu
from jax.sharding import PartitionSpec as P

WIN = 7
SHIFT = 3
HEADS = 8
TOKENS = WIN * WIN
PAD = 56
LANES = 64
ENTRIES = (2 * WIN - 1) * (2 * WIN - 1)
COLS = 42
WINDOWS = COLS // WIN
STRIP = WINDOWS * PAD
ROW = 48
D = 256
MLP = 1024
BF16 = jnp.bfloat16
F32 = jnp.float32
epsilon = 1e-05
neg = -1000000000.0
AXES = ("dp", "space")
SCALE = 1.0 / math.sqrt(D // HEADS)
SMALL_ONE = 2 * MLP + D
SMALL_TWO = 3 * D
ROWS_ONE = SMALL_ONE + 32
ROWS_TWO = SMALL_TWO + 32


def from_behind(block, axis, distance):
    devices = range(lax.axis_size(axis))
    route = [((i - distance) % len(devices), i) for i in devices]
    return lax.ppermute(block, axis, route)


def place(i, j):
    return 8 * i + j


def gather_matrix():
    out = np.zeros((STRIP, WIN * ROW), np.float32)
    for w in range(WINDOWS):
        for i in range(WIN):
            for j in range(WIN):
                out[w * PAD + place(i, j), i * ROW + (w * WIN + j + SHIFT) % COLS] = 1.0
    return out


def label_matrices():
    spread = np.zeros((COLS, WINDOWS * 2 * LANES), np.float32)
    rows = np.zeros((WIN, WINDOWS * 2 * LANES), np.float32)
    for w in range(WINDOWS):
        for copy in range(2):
            for i in range(WIN):
                for j in range(WIN):
                    col = (w * 2 + copy) * LANES + place(i, j)
                    spread[(w * WIN + j + SHIFT) % COLS, col] = 1.0
                    rows[i, col] = 1.0
    return spread, rows


def entry_matrix():
    out = np.zeros((WIN * 128, D), np.float32)
    for kj in range(WIN):
        for di in range(1 - WIN, WIN):
            for qj in range(WIN):
                entry = (di + WIN - 1) * (2 * WIN - 1) + qj - kj + WIN - 1
                out[kj * 128 + (8 * di + qj) % 128, entry] = 1.0
    return out


def head_mask():
    return (np.arange(4 * LANES)[:, None] // LANES == np.arange(128)[None] // 32).astype(np.float32)


def dot(a, b):
    return jnp.dot(a, b, preferred_element_type=F32)


def dot_nt(a, b):
    return lax.dot_general(a, b, (((1,), (1,)), ((), ())), preferred_element_type=F32)


def dot_tn(a, b):
    return lax.dot_general(a, b, (((0,), (0,)), ((), ())), preferred_element_type=F32)


def normalize(values):
    center = values - jnp.mean(values, -1, keepdims=True)
    variance = jnp.mean(center * center, -1, keepdims=True)
    recip_dev = lax.rsqrt(variance + epsilon)
    return center * recip_dev, recip_dev


def norm_backward(upstream, normal_part, recip_dev, gain):
    scaled = upstream * gain
    inner_mean = jnp.mean(scaled, -1, keepdims=True)
    cross_mean = jnp.mean(scaled * normal_part, -1, keepdims=True)
    return recip_dev * (scaled - inner_mean - normal_part * cross_mean)


def col_sum(values):
    return jnp.sum(values, 0, keepdims=True)


def raster_rows(ref, halo, s):
    last = s == pl.num_programs(0) - 1
    blank = jnp.zeros((ROW - COLS, D), BF16)
    rows = []
    for i in range(WIN):
        g = s * WIN + i + SHIFT
        if i < WIN - SHIFT:
            value = ref[g]
        else:
            value = jnp.where(last, halo[i - (WIN - SHIFT)], ref[jnp.minimum(g, COLS - 1)])
        rows += [value, blank]
    return jnp.concatenate(rows, 0)


def put_rows(raster, out, tail, s):
    last = s == pl.num_programs(0) - 1
    for i in range(WIN):
        value = raster[i * ROW : i * ROW + COLS]
        g = s * WIN + i + SHIFT
        if i < WIN - SHIFT:
            out[g] = value
        else:

            @pl.when(last)
            def _():
                tail[i - (WIN - SHIFT)] = value

            @pl.when(jnp.logical_not(last))
            def _():
                out[g] = value


def pad_rows(values):
    return jnp.concatenate([values, jnp.zeros((LANES - PAD,) + values.shape[1:], values.dtype)], 0)


def head_blocks(values, mask):
    low = pad_rows(values).astype(BF16)
    return [jnp.concatenate([low[:, g : g + 128]] * 4, 0) * mask[...] for g in (0, 128)]


def turn_pair(values):
    turned = values.T
    return jnp.concatenate([turned[:LANES], turned[LANES:]], 1)


def three_parts(values):
    high = values.astype(BF16)
    rest = values - high.astype(F32)
    middle = rest.astype(BF16)
    return high, middle, (rest - middle.astype(F32)).astype(BF16)


def lane_ids(shape):
    return lax.broadcasted_iota(jnp.int32, shape, 1)


def build_bias(table, entries, by_head, bias_t):
    parts = three_parts(table)
    for kj in range(WIN):
        one = entries[kj * 128 : (kj + 1) * 128]
        by_head[:, kj, :] = dot_nt(parts[0], one) + dot_nt(parts[1], one) + dot_nt(parts[2], one)
    by_head[:, WIN, :] = jnp.full((HEADS, 128), neg, F32)
    lane = lane_ids((8, 128))
    for pair in range(HEADS // 2):
        for ki in range(WIN):
            first = pltpu.roll(by_head[2 * pair], 8 * ki, 1)
            second = pltpu.roll(by_head[2 * pair + 1], (8 * ki + LANES) % 128, 1)
            bias_t[8 * ki : 8 * ki + 8, 128 * pair : 128 * pair + 128] = jnp.where(
                lane < LANES, first, second
            )


def table_gradient(logit_sums, entries, by_head):
    lane = lane_ids((8, 128))
    for pair in range(HEADS // 2):
        for half in range(2):
            total = jnp.zeros((8, 128), F32)
            for ki in range(WIN):
                block = logit_sums[8 * ki : 8 * ki + 8, 128 * pair : 128 * pair + 128]
                own = jnp.where((lane < LANES) == (half == 0), block, 0.0)
                total = total + pltpu.roll(own, (128 - 8 * ki - LANES * half) % 128, 1)
            by_head[2 * pair + half] = total
    out = jnp.zeros((HEADS, D), F32)
    for kj in range(WIN):
        one = entries[kj * 128 : (kj + 1) * 128]
        for part in three_parts(by_head[:, kj, :]):
            out = out + dot(part, one)
    return out


def forward_kernel(
    image, image_halo, cot, cot_halo, regions, regions_halo, spread, spread_rows, gather, scatter,
    mask, entries, table, gain_one, bias_one, w_qkv, b_query, b_value, w_proj, b_proj,
    gain_two, bias_two, w_up, b_up, w_down, b_down,
    block_out, tail, qkv_out, attend_out, d_mixed_out, d_resid_out, tokens_out, grads,
    lane_labels, by_head, bias_t, second_all, d_inner_all, active_all, cot_all, mixed_all, d_branch_all,
):
    s = pl.program_id(0)
    steps = pl.num_programs(0)
    small = SMALL_ONE

    @pl.when(s == 0)
    def _():
        own = dot(regions[...].astype(F32).astype(BF16), spread[...])
        halo = dot(regions_halo[...], spread[...])
        for n in range(COLS // WIN):
            top = n * WIN + SHIFT
            part = own[top : min(top + WIN, COLS)]
            if top + WIN > COLS:
                part = jnp.concatenate([part, halo], 0)
            row = jnp.sum(part * spread_rows[...], 0, keepdims=True)
            lane_labels[n] = jnp.concatenate(
                [row[:, 128 * w : 128 * w + 128] for w in range(WINDOWS)] + [jnp.zeros((2, 128), F32)], 0
            )
        build_bias(table[...], entries, by_head, bias_t)
        grads[small : small + 32] = jnp.zeros((32, D), F32)

    rows = pl.ds(pl.multiple_of(s * STRIP, 16), STRIP)
    tokens = dot(gather[...], raster_rows(image, image_halo, s))
    cot_f32 = dot(gather[...], raster_rows(cot, cot_halo, s))
    cot_low = cot_f32.astype(BF16)
    cot_all[rows] = cot_low
    tokens_out[...] = tokens.astype(BF16)
    normal_one, _ = normalize(tokens)
    first_low = (normal_one * gain_one[...] + bias_one[...]).astype(BF16)
    query = dot(first_low, w_qkv[:, :D]) + b_query[...]
    key = dot(first_low, w_qkv[:, D : 2 * D])
    value = dot(first_low, w_qkv[:, 2 * D :]) + b_value[...]
    qkv_out[:, :D] = query.astype(BF16)
    qkv_out[:, D : 2 * D] = key.astype(BF16)
    qkv_out[:, 2 * D :] = value.astype(BF16)

    key_labels = lane_labels[s].T
    spans = [slice(w * PAD, (w + 1) * PAD) for w in range(WINDOWS)]
    logits = []
    for span in spans:
        blocks = head_blocks(query[span], mask)
        key_low = key[span].astype(BF16)
        logits.append([dot_nt(key_low[:, 128 * g : 128 * g + 128], blocks[g]) for g in range(2)])
    turned = []
    for w in range(WINDOWS):
        same = key_labels[:PAD, w : w + 1] == lane_labels[s, w : w + 1, :]
        turned.append([])
        for pair in range(HEADS // 2):
            cols = slice(128 * pair, 128 * pair + 128)
            part = logits[w][pair // 2][:, 128 * (pair % 2) : 128 * (pair % 2) + 128]
            part = jnp.where(same, part * SCALE + bias_t[:, cols], neg)
            powers = jnp.exp(part - jnp.max(part, 0, keepdims=True))
            attend = powers * (1.0 / jnp.sum(powers, 0, keepdims=True))
            attend_low = pad_rows(attend).astype(BF16)
            attend_out[w, :, cols] = attend_low
            turned[w].append(turn_pair(attend_low))
    mixed_parts = []
    for w, span in enumerate(spans):
        blocks = head_blocks(value[span], mask)
        mixed_parts.append(
            jnp.concatenate(
                [
                    dot(jnp.concatenate(turned[w][2 * g : 2 * g + 2], 1), blocks[g])[:PAD]
                    for g in range(2)
                ],
                1,
            )
        )
    mixed_low = jnp.concatenate(mixed_parts, 0).astype(BF16)
    mixed_all[rows] = mixed_low

    resid = tokens + dot(mixed_low, w_proj[...]) + b_proj[...]
    normal_two, recip_two = normalize(resid)
    second_low = (normal_two * gain_two[...] + bias_two[...]).astype(BF16)
    second_all[rows] = second_low

    result = resid + b_down[...]
    d_second = jnp.zeros((STRIP, D), F32)
    for n in range(MLP // D):
        cols = slice(n * D, (n + 1) * D)
        inner = dot(second_low, w_up[:, cols]) + b_up[:, cols]
        cumulative = 0.5 * lax.erf(inner * 0.7071067811865476) + 0.5
        active_low = (inner * cumulative).astype(BF16)
        active_all[rows, cols] = active_low
        result = result + dot(active_low, w_down[cols])
        gauss = jnp.exp2(inner * inner * (-0.5 * 1.4426950408889634))
        slope = cumulative + inner * gauss * 0.3989422804014327
        d_inner = (dot_nt(cot_low, w_down[cols]) * slope).astype(BF16)
        d_inner_all[rows, cols] = d_inner
        grads[small + 4 + n : small + 5 + n] += col_sum(d_inner.astype(F32))
        d_second = d_second + dot_nt(d_inner, w_up[:, cols])
    put_rows(dot(scatter[...], result.astype(BF16)).astype(BF16), block_out, tail, s)

    d_resid = cot_f32 + norm_backward(d_second, normal_two, recip_two, gain_two[...])
    d_branch = d_resid.astype(BF16)
    d_branch_all[rows] = d_branch
    d_resid_out[...] = d_resid
    d_mixed_out[...] = dot_nt(d_branch, w_proj[...]).astype(BF16)
    grads[small : small + 1] += col_sum(d_second * normal_two)
    grads[small + 1 : small + 2] += col_sum(d_second)
    grads[small + 2 : small + 3] += col_sum(d_branch.astype(F32))
    grads[small + 3 : small + 4] += col_sum(cot_f32)

    @pl.when(s == steps - 1)
    def _():
        for n in range(MLP // D):
            cols = slice(n * D, (n + 1) * D)
            grads[n * D : (n + 1) * D] = dot_tn(second_all[...], d_inner_all[:, cols])
            grads[MLP + n * D : MLP + (n + 1) * D] = dot_tn(cot_all[...], active_all[:, cols])
        grads[2 * MLP : 2 * MLP + D] = dot_tn(mixed_all[...], d_branch_all[...])


def backward_kernel(
    qkv_in, attend_in, d_mixed_in, d_resid_in, tokens_in, scatter, mask, entries,
    gain_one, bias_one, w_qkv,
    image_grad, tail, grads,
    by_head, logit_sums, first_all, d_qkv_all,
):
    s = pl.program_id(0)
    steps = pl.num_programs(0)
    small = SMALL_TWO

    @pl.when(s == 0)
    def _():
        logit_sums[...] = jnp.zeros_like(logit_sums)
        grads[small : small + 32] = jnp.zeros((32, D), F32)

    rows = pl.ds(pl.multiple_of(s * STRIP, 16), STRIP)
    query = qkv_in[:, :D].astype(F32)
    key = qkv_in[:, D : 2 * D].astype(F32)
    value = qkv_in[:, 2 * D :].astype(F32)
    d_mixed = d_mixed_in[...].astype(F32)
    spans = [slice(w * PAD, (w + 1) * PAD) for w in range(WINDOWS)]
    mixed_blocks = []
    d_attends = []
    for span in spans:
        blocks = head_blocks(d_mixed[span], mask)
        mixed_blocks.append(blocks)
        value_low = value[span].astype(BF16)
        d_attends.append([dot_nt(value_low[:, 128 * g : 128 * g + 128], blocks[g]) for g in range(2)])
    d_logits = []
    for w in range(WINDOWS):
        d_logits.append([])
        for pair in range(HEADS // 2):
            cols = slice(128 * pair, 128 * pair + 128)
            part = d_attends[w][pair // 2][:, 128 * (pair % 2) : 128 * (pair % 2) + 128]
            attend = attend_in[w, :, cols].astype(F32)[:PAD]
            cross = jnp.sum(part * attend, 0, keepdims=True)
            low = pad_rows(attend * (part - cross)).astype(BF16)
            logit_sums[:, cols] += low.astype(F32)[:PAD]
            d_logits[w].append(low)
    parts = []
    for w, span in enumerate(spans):
        query_blocks = head_blocks(query[span], mask)
        key_blocks = head_blocks(key[span], mask)
        d_query, d_key, d_value = [], [], []
        for g in range(2):
            pairs = d_logits[w][2 * g : 2 * g + 2]
            d_value.append(dot(attend_in[w, :, 256 * g : 256 * g + 256], mixed_blocks[w][g])[:PAD])
            d_key.append(dot(jnp.concatenate(pairs, 1), query_blocks[g])[:PAD] * SCALE)
            turned = jnp.concatenate([turn_pair(p) for p in pairs], 1)
            d_query.append(dot(turned, key_blocks[g])[:PAD] * SCALE)
        parts.append(jnp.concatenate(d_query + d_key + d_value, 1))
    d_qkv = jnp.concatenate(parts, 0).astype(BF16)
    d_qkv_all[rows] = d_qkv
    totals = col_sum(d_qkv.astype(F32))
    grads[small + 8 : small + 9] += totals[:, :D]
    grads[small + 9 : small + 10] += totals[:, 2 * D :]

    normal_one, recip_one = normalize(tokens_in[...].astype(F32))
    first_all[rows] = (normal_one * gain_one[...] + bias_one[...]).astype(BF16)
    d_first = dot_nt(d_qkv, w_qkv[...])
    grads[small + 10 : small + 11] += col_sum(d_first * normal_one)
    grads[small + 11 : small + 12] += col_sum(d_first)
    grad = d_resid_in[...] + norm_backward(d_first, normal_one, recip_one, gain_one[...])
    put_rows(dot(scatter[...], grad.astype(BF16)).astype(BF16), image_grad, tail, s)

    @pl.when(s == steps - 1)
    def _():
        for n in range(3):
            cols = slice(n * D, (n + 1) * D)
            grads[n * D : (n + 1) * D] = dot_tn(first_all[...], d_qkv_all[:, cols])
        grads[small : small + 8] = table_gradient(logit_sums, entries, by_head)


def whole(shape):
    return pl.BlockSpec(shape, lambda s: (0,) * len(shape))


def strips(shape):
    return pl.BlockSpec(shape, lambda s: (s,) + (0,) * (len(shape) - 1))


def struct(shape, dtype):
    return jax.ShapeDtypeStruct(shape, dtype)


params = pltpu.CompilerParams(
    vmem_limit_bytes=56 * 1024 * 1024, dimension_semantics=("arbitrary",)
)


def run_forward(*args):
    n = COLS // WIN
    total = n * STRIP
    return pl.pallas_call(
        forward_kernel,
        grid=(n,),
        in_specs=[whole(a.shape) for a in args],
        out_specs=[
            whole((COLS, COLS, D)),
            whole((SHIFT, COLS, D)),
            strips((STRIP, 3 * D)),
            strips((WINDOWS, LANES, HEADS * LANES)),
            strips((STRIP, D)),
            strips((STRIP, D)),
            strips((STRIP, D)),
            whole((ROWS_ONE, D)),
        ],
        out_shape=[
            struct((COLS, COLS, D), BF16),
            struct((SHIFT, COLS, D), BF16),
            struct((total, 3 * D), BF16),
            struct((n * WINDOWS, LANES, HEADS * LANES), BF16),
            struct((total, D), BF16),
            struct((total, D), F32),
            struct((total, D), BF16),
            struct((ROWS_ONE, D), F32),
        ],
        scratch_shapes=[
            pltpu.VMEM((n, 8, 128), F32),
            pltpu.VMEM((HEADS, 8, 128), F32),
            pltpu.VMEM((PAD, HEADS * LANES), F32),
            pltpu.VMEM((total, D), BF16),
            pltpu.VMEM((total, MLP), BF16),
            pltpu.VMEM((total, MLP), BF16),
            pltpu.VMEM((total, D), BF16),
            pltpu.VMEM((total, D), BF16),
            pltpu.VMEM((total, D), BF16),
        ],
        compiler_params=params,
        cost_estimate=pl.CostEstimate(
            flops=2 * total * 5 * D * MLP * 2, bytes_accessed=20_000_000, transcendentals=0
        ),
        name="forward_and_mlp_backward",
    )(*args)


def run_backward(*args):
    n = COLS // WIN
    total = n * STRIP
    in_specs = [
        strips((STRIP, 3 * D)),
        strips((WINDOWS, LANES, HEADS * LANES)),
        strips((STRIP, D)),
        strips((STRIP, D)),
        strips((STRIP, D)),
    ] + [whole(a.shape) for a in args[5:]]
    return pl.pallas_call(
        backward_kernel,
        grid=(n,),
        in_specs=in_specs,
        out_specs=[
            whole((COLS, COLS, D)),
            whole((SHIFT, COLS, D)),
            whole((ROWS_TWO, D)),
        ],
        out_shape=[
            struct((COLS, COLS, D), BF16),
            struct((SHIFT, COLS, D), BF16),
            struct((ROWS_TWO, D), F32),
        ],
        scratch_shapes=[
            pltpu.VMEM((HEADS, 8, 128), F32),
            pltpu.VMEM((PAD, HEADS * LANES), F32),
            pltpu.VMEM((total, D), BF16),
            pltpu.VMEM((total, 3 * D), BF16),
        ],
        compiler_params=params,
        cost_estimate=pl.CostEstimate(
            flops=2 * total * 9 * D * D * 4, bytes_accessed=12_000_000, transcendentals=0
        ),
        name="attention_backward",
    )(*args)


def unpack_kernel(
    first_half, second_half,
    gain_one, bias_one, w_qkv, b_query, b_value, table, w_proj, b_proj,
    gain_two, bias_two, w_up, b_up, w_down, b_down,
):
    def one(start, count):
        half = ROWS_ONE // 2
        if start + count <= half:
            return first_half[start : start + count].astype(F32)
        if start >= half:
            return second_half[start - half : start - half + count].astype(F32)
        return jnp.concatenate([one(start, half - start), one(half, start + count - half)], 0)

    def two(start, count):
        half, base = ROWS_TWO // 2, ROWS_ONE // 2
        if start + count <= half:
            return first_half[base + start : base + start + count].astype(F32)
        if start >= half:
            return second_half[base + start - half : base + start - half + count].astype(F32)
        return jnp.concatenate([two(start, half - start), two(half, start + count - half)], 0)

    for n in range(MLP // D):
        w_up[:, n * D : (n + 1) * D] = one(n * D, D)
        w_down[n * D : (n + 1) * D] = one(MLP + n * D, D).T
    w_proj[...] = one(2 * MLP, D)
    for n in range(3):
        w_qkv[:, n * D : (n + 1) * D] = two(n * D, D)
    small = one(SMALL_ONE, 16)
    gain_two[...] = small[0:1]
    bias_two[...] = small[1:2]
    b_proj[...] = small[2:3]
    b_down[...] = small[3:4]
    for n in range(MLP // D):
        b_up[:, n * D : (n + 1) * D] = small[4 + n : 5 + n]
    small = two(SMALL_TWO, 16)
    table[...] = small[:HEADS, :ENTRIES]
    b_query[...] = small[8:9]
    b_value[...] = small[9:10]
    gain_one[...] = small[10:11]
    bias_one[...] = small[11:12]


def run_unpack(first_half, second_half):
    shapes = [
        (1, D), (1, D), (D, 3 * D), (1, D), (1, D), (HEADS, ENTRIES), (D, D), (1, D),
        (1, D), (1, D), (D, MLP), (1, MLP), (MLP, D), (1, D),
    ]
    out = pl.pallas_call(
        unpack_kernel,
        out_shape=[struct(shape, F32) for shape in shapes],
        compiler_params=pltpu.CompilerParams(vmem_limit_bytes=40 * 1024 * 1024),
        name="unpack_gradients",
    )(first_half, second_half)
    out = [v[0] if v.shape[0] == 1 else v for v in out]
    out[5] = out[5].T
    return tuple(out)


def coords(index):
    dp, space = divmod(index, 32)
    return {"c": dp % 2, "y": dp // 2 + 2 * ((space // 4) % 2), "x": space % 4, "z": space // 8}


def index_of(c, y, x, z):
    return ((y % 2) * 2 + c) * 32 + z * 8 + (y // 2) * 4 + x


STEPS = (
    ("c", "c", 0),
    ("y", "x", 0),
    ("x", "z", 0),
    ("z", "y", 0),
    ("y", "x", 1),
    ("x", "z", 1),
    ("z", "y", 1),
)
HALVINGS = 3


def partners(step):
    out = []
    for i in range(128):
        at = coords(i)
        axis = step[at["c"]]
        to = dict(at)
        to[axis] = at[axis] ^ (1 << step[2])
        out.append((i, index_of(**to)))
    return out


def own_bit(step, at):
    bits = [(at[step[core]] >> step[2]) & 1 for core in range(2)]
    return jnp.where(at["c"] == 0, bits[0], bits[1])


def take_half(rows, which):
    half = rows.shape[0] // 2
    return lax.dynamic_slice_in_dim(rows, which * half, half, 0)


def core_exchange(rows, at):
    if lax.axis_size("dp") == 1:
        return take_half(rows, 0)
    keep = at["c"]
    got = lax.ppermute(take_half(rows, 1 - keep).astype(BF16), AXES, partners(STEPS[0]))
    return take_half(rows, keep) + got.astype(F32)


def sum_everywhere(rows, at):
    kept = []
    for step in STEPS[1:HALVINGS]:
        keep = own_bit(step, at)
        got = lax.ppermute(take_half(rows, 1 - keep).astype(BF16), AXES, partners(step))
        rows = take_half(rows, keep) + got.astype(F32)
        kept.append(keep)
    low = rows.astype(BF16)
    for step in STEPS[HALVINGS:]:
        got = lax.ppermute(low, AXES, partners(step))
        low = (low.astype(F32) + got.astype(F32)).astype(BF16)
    for step, keep in zip(reversed(STEPS[1:HALVINGS]), reversed(kept)):
        got = lax.ppermute(low, AXES, partners(step))
        first = jnp.where(keep == 0, low, got)
        second = jnp.where(keep == 0, got, low)
        low = jnp.concatenate([first, second], 0)
    return low


def body(
    image_in, cotangent, regions, first_gain, first_bias, qkv_weight, query_bias, value_bias,
    position_table, proj_weight, proj_bias, second_gain, second_bias, up_weight, up_bias,
    down_weight, down_bias,
):
    many = lax.axis_size("dp") * lax.axis_size("space") == 128
    me = lax.axis_index(AXES)
    at = coords(me)
    arrived = from_behind(
        (image_in[:SHIFT], cotangent[:SHIFT], regions[:SHIFT].astype(BF16)), "space", -1
    )
    gather = gather_matrix()
    spread, spread_rows = label_matrices()
    entries = jnp.asarray(entry_matrix(), BF16)
    mask = jnp.asarray(head_mask(), BF16)
    scatter = jnp.asarray(gather.T, BF16)
    table = jnp.pad(position_table.T, ((0, 0), (0, D - ENTRIES)))
    block_out, out_tail, qkv, attend, d_mixed, d_resid, tokens, grads_one = run_forward(
        image_in, arrived[0], cotangent, arrived[1], regions, arrived[2],
        jnp.asarray(spread, BF16), jnp.asarray(spread_rows), jnp.asarray(gather, BF16), scatter,
        mask, entries, table, first_gain[None], first_bias[None], qkv_weight, query_bias[None],
        value_bias[None], proj_weight, proj_bias[None], second_gain[None], second_bias[None],
        up_weight, up_bias[None], down_weight, down_bias[None],
    )
    image_grad, grad_tail, grads_two = run_backward(
        qkv, attend, d_mixed, d_resid, tokens, scatter, mask, entries,
        first_gain[None], first_bias[None], qkv_weight,
    )
    own = jnp.concatenate([core_exchange(grads_one, at), core_exchange(grads_two, at)], 0)
    returned = from_behind((out_tail, grad_tail), "space", 1)
    if many:
        own = sum_everywhere(own, at)
        other = lax.ppermute(own, AXES, partners(STEPS[0]))
        first_half = jnp.where(at["c"] == 0, own, other)
        second_half = jnp.where(at["c"] == 0, other, own)
    else:
        first_half = own.astype(BF16)
        second_half = jnp.concatenate([take_half(grads_one, 1), take_half(grads_two, 1)], 0).astype(BF16)
    block_out = lax.dynamic_update_slice(block_out, returned[0], (0, 0, 0))
    image_grad = lax.dynamic_update_slice(image_grad, returned[1], (0, 0, 0))
    return (block_out, image_grad) + run_unpack(first_half, second_half)


def solution(mesh):
    tokens = P(AXES, None, None)
    return jax.shard_map(
        body,
        mesh=mesh,
        in_specs=(tokens, tokens, P(AXES, None)) + (P(),) * 14,
        out_specs=(tokens, tokens) + (P(),) * 14,
        check_vma=False,
    )
```

```python
import functools
import math

import jax
import jax.numpy as jnp
import numpy as np
from jax import lax
from jax.experimental import pallas as pl
from jax.experimental.pallas import tpu as pltpu
from jax.sharding import PartitionSpec as P

WIN = 7
SHIFT = 3
HEADS = 8
TOKENS = WIN * WIN
PAD = 56
LANES = 64
ENTRIES = (2 * WIN - 1) * (2 * WIN - 1)
COLS = 42
WINDOWS = COLS // WIN
STRIP = WINDOWS * PAD
STRIPS = COLS // WIN
FIELD_STEPS = STRIPS // 2
TOTAL = STRIPS * STRIP
ROW = 48
D = 256
MLP = 1024
BF16 = jnp.bfloat16
F32 = jnp.float32
epsilon = 1e-05
neg = -1000000000.0
AXES = ("dp", "space")
SCALE = 1.0 / math.sqrt(D // HEADS)
LOG2E = 1.4426950408889634
UP = 0
DOWN = (MLP, MLP + 2 * D + 32)
SMALL_ONE = MLP + 2 * D
HALF = SMALL_ONE + 32
PROJ = HALF + 2 * D
QKV = PROJ + D
SMALL_TWO = QKV + 3 * D
assert SMALL_TWO + 32 == 2 * HALF


def from_behind(block, axis, distance):
    devices = range(lax.axis_size(axis))
    route = [((i - distance) % len(devices), i) for i in devices]
    return lax.ppermute(block, axis, route)


def place(i, j):
    return 8 * i + j


def gather_matrix():
    out = np.zeros((STRIP, WIN * ROW), np.float32)
    for w in range(WINDOWS):
        for i in range(WIN):
            for j in range(WIN):
                out[w * PAD + place(i, j), i * ROW + (w * WIN + j + SHIFT) % COLS] = 1.0
    return out


def label_matrices():
    spread = np.zeros((COLS, WINDOWS * 2 * LANES), np.float32)
    rows = np.zeros((WIN, WINDOWS * 2 * LANES), np.float32)
    for w in range(WINDOWS):
        for copy in range(2):
            for i in range(WIN):
                for j in range(WIN):
                    col = (w * 2 + copy) * LANES + place(i, j)
                    spread[(w * WIN + j + SHIFT) % COLS, col] = 1.0
                    rows[i, col] = 1.0
    return spread, rows


def entry_matrix():
    out = np.zeros((WIN * 128, D), np.float32)
    for kj in range(WIN):
        for di in range(1 - WIN, WIN):
            for qj in range(WIN):
                entry = (di + WIN - 1) * (2 * WIN - 1) + qj - kj + WIN - 1
                out[kj * 128 + (8 * di + qj) % 128, entry] = 1.0
    return out


def head_mask():
    return (np.arange(4 * LANES)[:, None] // LANES == np.arange(128)[None] // 32).astype(np.float32)


def dot(a, b):
    return jnp.dot(a, b, preferred_element_type=F32)


def dot_nt(a, b):
    return lax.dot_general(a, b, (((1,), (1,)), ((), ())), preferred_element_type=F32)


def dot_tn(a, b):
    return lax.dot_general(a, b, (((0,), (0,)), ((), ())), preferred_element_type=F32)


def normalize(values):
    center = values - jnp.mean(values, -1, keepdims=True)
    variance = jnp.mean(center * center, -1, keepdims=True)
    recip_dev = lax.rsqrt(variance + epsilon)
    return center * recip_dev, recip_dev


def norm_backward(upstream, normal_part, recip_dev, gain):
    scaled = upstream * gain
    inner_mean = jnp.mean(scaled, -1, keepdims=True)
    cross_mean = jnp.mean(scaled * normal_part, -1, keepdims=True)
    return recip_dev * (scaled - inner_mean - normal_part * cross_mean)


def col_sum(values):
    return jnp.sum(values, 0, keepdims=True)


def raster_rows(ref, halo, first, s):
    last = s == STRIPS - 1
    blank = jnp.zeros((ROW - COLS, D), BF16)
    rows = []
    for i in range(WIN):
        g = s * WIN + i + SHIFT
        if i < WIN - SHIFT:
            value = ref[g]
        else:
            value = jnp.where(
                last, halo[first + i - (WIN - SHIFT)], ref[jnp.minimum(g, COLS - 1)]
            )
        rows += [value, blank]
    return jnp.concatenate(rows, 0)


def put_rows(raster, out, tail, stage, sems, first):
    t = pl.program_id(0)
    slot = lax.rem(t, 2)
    strip = first + t

    def whole_strip(n):
        return pltpu.make_async_copy(
            stage.at[lax.rem(n, 2)], out.at[pl.ds((first + n) * WIN + SHIFT, WIN)], sems.at[lax.rem(n, 2)]
        )

    @pl.when(t >= 2)
    def _():
        whole_strip(t - 2).wait()

    for i in range(WIN):
        stage[slot, i] = raster[i * ROW : i * ROW + COLS]

    @pl.when(strip < STRIPS - 1)
    def _():
        whole_strip(t).start()

    final = pl.num_programs(0) - 1

    @pl.when(t == final)
    def _():
        if first + FIELD_STEPS < STRIPS:
            whole_strip(t - 1).wait()
            whole_strip(t).wait()
        else:
            own = pltpu.make_async_copy(
                stage.at[slot, 0 : WIN - SHIFT], out.at[COLS - (WIN - SHIFT) : COLS], sems.at[slot]
            )
            below = pltpu.make_async_copy(stage.at[slot, WIN - SHIFT : WIN], tail, sems.at[2])
            own.start()
            below.start()
            whole_strip(t - 1).wait()
            own.wait()
            below.wait()


def pad_rows(values):
    return jnp.concatenate([values, jnp.zeros((LANES - PAD,) + values.shape[1:], values.dtype)], 0)


def head_blocks(low, mask):
    return [jnp.concatenate([low[:, g : g + 128]] * 4, 0) * mask[...] for g in (0, 128)]


def turn_pair(values):
    turned = values.T
    return jnp.concatenate([turned[:LANES], turned[LANES:]], 1)


def three_parts(values):
    high = values.astype(BF16)
    rest = values - high.astype(F32)
    middle = rest.astype(BF16)
    return high, middle, (rest - middle.astype(F32)).astype(BF16)


def lane_ids(shape):
    return lax.broadcasted_iota(jnp.int32, shape, 1)


def build_bias(table, entries, by_head, bias_t):
    parts = three_parts(table * LOG2E)
    for kj in range(WIN):
        one = entries[kj * 128 : (kj + 1) * 128, :ENTRIES]
        by_head[:, kj, :] = dot_nt(parts[0], one) + dot_nt(parts[1], one) + dot_nt(parts[2], one)
    by_head[:, WIN, :] = jnp.full((HEADS, 128), neg, F32)
    lane = lane_ids((8, 128))
    for pair in range(HEADS // 2):
        for ki in range(WIN):
            first = pltpu.roll(by_head[2 * pair], 8 * ki, 1)
            second = pltpu.roll(by_head[2 * pair + 1], (8 * ki + LANES) % 128, 1)
            bias_t[8 * ki : 8 * ki + 8, 128 * pair : 128 * pair + 128] = jnp.where(
                lane < LANES, first, second
            )


def table_gradient(logit_sums, entries, by_head):
    lane = lane_ids((8, 128))
    for pair in range(HEADS // 2):
        for half in range(2):
            total = jnp.zeros((8, 128), F32)
            for ki in range(WIN):
                block = logit_sums[8 * ki : 8 * ki + 8, 128 * pair : 128 * pair + 128]
                own = jnp.where((lane < LANES) == (half == 0), block, 0.0)
                total = total + pltpu.roll(own, (128 - 8 * ki - LANES * half) % 128, 1)
            by_head[2 * pair + half] = total
    out = jnp.zeros((HEADS, D), F32)
    for kj in range(WIN):
        one = entries[kj * 128 : (kj + 1) * 128]
        for part in three_parts(by_head[:, kj, :]):
            out = out + dot(part, one)
    return out


def spans():
    return [slice(w * PAD, (w + 1) * PAD) for w in range(WINDOWS)]


def forward_stage(s, r):
    rows = pl.ds(pl.multiple_of(s * STRIP, 16), STRIP)
    slot = lax.rem(s, 2)
    tokens = dot(r.gather[...], raster_rows(r.image, r.halo, 0, s))
    r.tokens_out[...] = tokens.astype(BF16)
    yield
    r.cot_all[rows] = dot(r.gather[...], raster_rows(r.cot, r.halo, SHIFT, s)).astype(BF16)
    yield
    normal_one, _ = normalize(tokens)
    first_low = (normal_one * r.gain_one[...] + r.bias_one[...]).astype(BF16)
    r.first_all[rows, :D] = first_low
    yield
    query = dot(first_low, r.w_qkv[:, :D]) + r.b_query[...]
    key = dot(first_low, r.w_qkv[:, D : 2 * D])
    value = dot(first_low, r.w_qkv[:, 2 * D :]) + r.b_value[...]
    yield
    key_labels = r.lane_labels[s].T
    logits = []
    for w, span in enumerate(spans()):
        query_low = pad_rows(query[span]).astype(BF16)
        key_low = pad_rows(key[span]).astype(BF16)
        value_low = pad_rows(value[span]).astype(BF16)
        r.qkv_win[slot, w, :, :D] = query_low
        r.qkv_win[slot, w, :, D : 2 * D] = key_low
        r.qkv_win[slot, w, :, 2 * D :] = value_low
        blocks = head_blocks(query_low, r.mask)
        logits.append(
            [dot_nt(key_low[:, 128 * g : 128 * g + 128], blocks[g])[:PAD] for g in range(2)]
        )
        yield
    turned = []
    for w in range(WINDOWS):
        same = key_labels[:PAD, w : w + 1] == r.lane_labels[s, w : w + 1, :]
        turned.append([])
        for pair in range(HEADS // 2):
            cols = slice(128 * pair, 128 * pair + 128)
            part = logits[w][pair // 2][:, 128 * (pair % 2) : 128 * (pair % 2) + 128]
            part = jnp.where(same, part * (SCALE * LOG2E) + r.bias_t[:, cols], neg)
            powers = jnp.exp2(part - jnp.max(part, 0, keepdims=True))
            attend = powers * (1.0 / jnp.sum(powers, 0, keepdims=True))
            attend_low = pad_rows(attend).astype(BF16)
            r.attend_win[slot, w, :, cols] = attend_low
            turned[w].append(turn_pair(attend_low))
        yield
    mixed_parts = []
    for w in range(WINDOWS):
        blocks = head_blocks(r.qkv_win[slot, w, :, 2 * D :], r.mask)
        mixed_parts.append(
            jnp.concatenate(
                [
                    dot(jnp.concatenate(turned[w][2 * g : 2 * g + 2], 1), blocks[g])[:PAD]
                    for g in range(2)
                ],
                1,
            )
        )
        yield
    mixed_low = jnp.concatenate(mixed_parts, 0).astype(BF16)
    r.mixed_all[rows] = mixed_low
    resid = tokens + dot(mixed_low, r.w_proj[...]) + r.b_proj[...]
    r.resid_win[slot] = resid
    yield


def backward_stage(s, r):
    rows = pl.ds(pl.multiple_of(s * STRIP, 16), STRIP)
    slot = lax.rem(s, 2)
    sums = r.sums
    resid = r.resid_win[slot]
    r.resid_out[...] = resid
    normal_two, recip_two = normalize(resid)
    second_low = (normal_two * r.gain_two[...] + r.bias_two[...]).astype(BF16)
    r.second_all[rows, :D] = second_low
    yield
    cot_low = r.cot_all[rows]
    d_second = jnp.zeros((STRIP, D), F32)
    for n in range(MLP // D):
        cols = slice(n * D, (n + 1) * D)
        inner = dot(second_low, r.w_up[:, cols]) + r.b_up[:, cols]
        cumulative = 0.5 * lax.erf(inner * 0.7071067811865476) + 0.5
        active_low = (inner * cumulative).astype(BF16)
        r.active_all[rows, cols] = active_low
        r.active_out[:, cols] = active_low
        yield
        gauss = jnp.exp2(inner * inner * (-0.5 * LOG2E))
        slope = cumulative + inner * gauss * 0.3989422804014327
        d_inner = (dot_nt(cot_low, r.w_down[cols]) * slope).astype(BF16)
        r.d_inner_all[rows, cols] = d_inner
        yield
        d_second = d_second + dot_nt(d_inner, r.w_up[:, cols])
        yield
    cot_f32 = cot_low.astype(F32)
    d_resid = cot_f32 + norm_backward(d_second, normal_two, recip_two, r.gain_two[...])
    d_branch = d_resid.astype(BF16)
    r.d_branch_all[rows] = d_branch
    r.d_resid_out[...] = d_resid
    yield
    d_mixed = dot_nt(d_branch, r.w_proj[...])
    yield
    sums[0:1] += col_sum(d_second * normal_two)
    sums[1:2] += col_sum(d_second)
    sums[2:3] += col_sum(d_resid)
    sums[3:4] += col_sum(cot_f32)
    yield
    mixed_blocks = []
    d_attends = []
    for w, span in enumerate(spans()):
        blocks = head_blocks(pad_rows(d_mixed[span]).astype(BF16), r.mask)
        mixed_blocks.append(blocks)
        value_low = r.qkv_win[slot, w, :, 2 * D :]
        d_attends.append(
            [dot_nt(value_low[:, 128 * g : 128 * g + 128], blocks[g])[:PAD] for g in range(2)]
        )
        yield
    d_logits = []
    turned = []
    for w in range(WINDOWS):
        d_logits.append([])
        turned.append([])
        for pair in range(HEADS // 2):
            cols = slice(128 * pair, 128 * pair + 128)
            part = d_attends[w][pair // 2][:, 128 * (pair % 2) : 128 * (pair % 2) + 128]
            attend = r.attend_win[slot, w, :, cols].astype(F32)[:PAD]
            cross = jnp.sum(part * attend, 0, keepdims=True)
            part = attend * (part - cross)
            r.logit_sums[:, cols] += part
            low = pad_rows(part).astype(BF16)
            d_logits[w].append(low)
            turned[w].append(turn_pair(low))
        yield
    parts = []
    for w in range(WINDOWS):
        query_blocks = head_blocks(r.qkv_win[slot, w, :, :D], r.mask)
        key_blocks = head_blocks(r.qkv_win[slot, w, :, D : 2 * D], r.mask)
        d_query, d_key, d_value = [], [], []
        for g in range(2):
            two = slice(2 * g, 2 * g + 2)
            attend_low = r.attend_win[slot, w, :, 256 * g : 256 * g + 256]
            d_value.append(dot(attend_low, mixed_blocks[w][g])[:PAD])
            d_key.append(dot(jnp.concatenate(d_logits[w][two], 1), query_blocks[g])[:PAD] * SCALE)
            d_query.append(dot(jnp.concatenate(turned[w][two], 1), key_blocks[g])[:PAD] * SCALE)
        parts.append(jnp.concatenate(d_query + d_key + d_value, 1))
        yield
    d_qkv = jnp.concatenate(parts, 0).astype(BF16)
    r.d_qkv_all[rows] = d_qkv
    r.d_qkv_out[...] = d_qkv
    yield


def run(*stages):
    order = []
    for n, stage in enumerate(stages):
        count = PIECES[stage.__name__]
        order += [((piece + 0.5) / count * (0.5 if n else 1.0), n) for piece in range(count)]
    for _, n in sorted(order):
        next(stages[n])
    for stage in stages:
        assert next(stage, None) is None


PIECES = {"forward_stage": 5 + 3 * WINDOWS, "backward_stage": 1 + 3 * (MLP // D) + 3 + 3 * WINDOWS + 1}


def down_rows(n):
    return DOWN[n // 2] + (n % 2) * D


def finish(r):
    core = lax.rem(lax.axis_index("dp"), 2)
    grads = r.grads

    def put(start, rows):
        grads[start : start + rows.shape[0]] = rows
        r.grads_low[start : start + rows.shape[0]] = rows.astype(BF16)

    def sends(n, start, count):
        half, at = divmod(start, HALF)
        span = pl.ds(at, count)
        keep = pltpu.make_async_copy(grads.at[pl.ds(start, count)], r.keep.at[span], r.sems.at[n])
        send = pltpu.make_async_copy(r.grads_low.at[pl.ds(start, count)], r.send.at[span], r.sems.at[n])
        return half, keep, send

    def begin(half, keep, send):
        @pl.when(core == half)
        def _():
            keep.start()

        @pl.when(core != half)
        def _():
            send.start()

    def end(half, keep, send):
        @pl.when(core == half)
        def _():
            keep.wait()

        @pl.when(core != half)
        def _():
            send.wait()

    small = SMALL_TWO
    put(small, table_gradient(r.logit_sums, r.entries, r.by_head))
    product = dot_tn(r.first_all[:, : D + 8], r.d_qkv_all[...])
    sums = product[D : D + 8]
    for n in range(3):
        put(QKV + n * D, product[:D, n * D : (n + 1) * D])
    bias_grad = jnp.zeros((8, D), F32)
    for part in three_parts(sums):
        bias_grad = bias_grad + dot_nt(part, r.w_qkv[...])
    cross = jnp.zeros((8, D), F32)
    for part in three_parts(product[:D] * r.w_qkv[...].astype(F32)):
        cross = cross + dot_nt(jnp.ones((8, 3 * D), BF16), part)
    gain_grad = (cross[0:1] - r.bias_one[...] * bias_grad[0:1]) / r.gain_one[...]
    put(
        small + 8,
        jnp.concatenate(
            [sums[0:1, :D], sums[0:1, 2 * D :], gain_grad, bias_grad[0:1], jnp.zeros((20, D), F32)], 0
        ),
    )
    put(PROJ, dot_tn(r.mixed_all[...], r.d_branch_all[...]))
    product = dot_tn(r.second_all[:, : D + 8], r.d_inner_all[...])
    for n in range(MLP // D):
        put(UP + n * D, product[:D, n * D : (n + 1) * D])
    ups = [product[D : D + 1, n * D : (n + 1) * D] for n in range(MLP // D)]
    put(SMALL_ONE, jnp.concatenate([r.sums[0:4]] + ups + [jnp.zeros((24, D), F32)], 0))
    copies = [sends(0, UP, MLP), sends(1, SMALL_ONE, 32), sends(2, PROJ, 2 * HALF - PROJ)]
    for copy in copies:
        begin(*copy)
    product = dot_tn(r.cot_all[...], r.active_all[...])
    for n in range(MLP // D):
        put(down_rows(n), product[:, n * D : (n + 1) * D])
    later = [sends(3, DOWN[0], 2 * D), sends(4, DOWN[1], 2 * D)]
    for copy in later:
        begin(*copy)
    for copy in copies + later:
        end(*copy)


class Refs:
    def __init__(self, names, refs):
        self.__dict__.update(zip(names, refs))


NAMES = [
    "image", "cot", "halo", "regions", "regions_halo", "spread", "spread_rows", "gather", "mask", "entries", "table",
    "gain_one", "bias_one", "w_qkv", "b_query", "b_value", "w_proj", "b_proj", "gain_two", "bias_two", "w_up", "b_up",
    "w_down", "keep", "send", "tokens_out", "resid_out", "active_out", "d_resid_out", "d_qkv_out",
    "lane_labels", "by_head", "bias_t", "logit_sums", "qkv_win", "attend_win", "resid_win", "sums",
    "first_all", "cot_all", "mixed_all", "second_all", "active_all", "d_inner_all", "d_branch_all", "d_qkv_all",
    "grads", "grads_low", "sems",
]


def grads_kernel(*refs):
    r = Refs(NAMES, refs)
    s = pl.program_id(0)

    @pl.when(s == 0)
    def _():
        own = dot(r.regions[...].astype(F32).astype(BF16), r.spread[...])
        below = dot(r.regions_halo[...], r.spread[...])
        for n in range(STRIPS):
            top = n * WIN + SHIFT
            part = own[top : min(top + WIN, COLS)]
            if top + WIN > COLS:
                part = jnp.concatenate([part, below], 0)
            row = jnp.sum(part * r.spread_rows[...], 0, keepdims=True)
            r.lane_labels[n] = jnp.concatenate(
                [row[:, 128 * w : 128 * w + 128] for w in range(WINDOWS)] + [jnp.zeros((2, 128), F32)], 0
            )
        build_bias(r.table[...], r.entries, r.by_head, r.bias_t)
        r.logit_sums[...] = jnp.zeros_like(r.logit_sums)
        one = (lane_ids((TOTAL, 128)) == 0).astype(F32).astype(BF16)
        r.first_all[:, D:] = one
        r.second_all[:, D:] = one
        r.sums[...] = jnp.zeros_like(r.sums)
        run(forward_stage(s, r))

    @pl.when((s > 0) & (s < STRIPS))
    def _():
        run(backward_stage(s - 1, r), forward_stage(s, r))

    @pl.when(s == STRIPS)
    def _():
        run(backward_stage(s - 1, r))
        finish(r)


def output_kernel(first, active, resid, w_down, b_down, scatter, *rest):
    result = resid[...] + b_down[...] + dot(active[...], w_down[...])
    put_rows(dot(scatter[...], result.astype(BF16)).astype(BF16), *rest[-4:], first)


def image_kernel(first, d_qkv, d_resid, tokens, w_qkv, gain, scatter, *rest):
    normal, recip_dev = normalize(tokens[...].astype(F32))
    d_first = dot_nt(d_qkv[...], w_qkv[...])
    grad = d_resid[...] + norm_backward(d_first, normal, recip_dev, gain[...])
    put_rows(dot(scatter[...], grad.astype(BF16)).astype(BF16), *rest[-4:], first)


def whole(shape):
    return pl.BlockSpec(shape, lambda s: (0,) * len(shape))


def strips(shape):
    return pl.BlockSpec(shape, lambda s: (s,) + (0,) * (len(shape) - 1))


def struct(shape, dtype):
    return jax.ShapeDtypeStruct(shape, dtype)


def params(mebibytes):
    return pltpu.CompilerParams(
        vmem_limit_bytes=mebibytes * 1024 * 1024, dimension_semantics=("arbitrary",)
    )


def run_grads(*args):
    early = lambda s: (jnp.minimum(s, STRIPS - 1), 0)
    late = lambda s: (jnp.maximum(s - 1, 0), 0)
    return pl.pallas_call(
        grads_kernel,
        grid=(STRIPS + 1,),
        in_specs=[whole(a.shape) for a in args],
        out_specs=[
            pl.BlockSpec(memory_space=pl.ANY),
            pl.BlockSpec(memory_space=pl.ANY),
            pl.BlockSpec((STRIP, D), early),
            pl.BlockSpec((STRIP, D), late),
            pl.BlockSpec((STRIP, MLP), late),
            pl.BlockSpec((STRIP, D), late),
            pl.BlockSpec((STRIP, 3 * D), late),
        ],
        out_shape=[
            struct((HALF, D), F32),
            struct((HALF, D), BF16),
            struct((TOTAL, D), BF16),
            struct((TOTAL, D), F32),
            struct((TOTAL, MLP), BF16),
            struct((TOTAL, D), F32),
            struct((TOTAL, 3 * D), BF16),
        ],
        scratch_shapes=[
            pltpu.VMEM((STRIPS, 8, 128), F32),
            pltpu.VMEM((HEADS, 8, 128), F32),
            pltpu.VMEM((PAD, HEADS * LANES), F32),
            pltpu.VMEM((PAD, HEADS * LANES), F32),
            pltpu.VMEM((2, WINDOWS, LANES, 3 * D), BF16),
            pltpu.VMEM((2, WINDOWS, LANES, HEADS * LANES), BF16),
            pltpu.VMEM((2, STRIP, D), F32),
            pltpu.VMEM((8, D), F32),
            pltpu.VMEM((TOTAL, D + 128), BF16),
            pltpu.VMEM((TOTAL, D), BF16),
            pltpu.VMEM((TOTAL, D), BF16),
            pltpu.VMEM((TOTAL, D + 128), BF16),
            pltpu.VMEM((TOTAL, MLP), BF16),
            pltpu.VMEM((TOTAL, MLP), BF16),
            pltpu.VMEM((TOTAL, D), BF16),
            pltpu.VMEM((TOTAL, 3 * D), BF16),
            pltpu.VMEM((2 * HALF, D), F32),
            pltpu.VMEM((2 * HALF, D), BF16),
            pltpu.SemaphoreType.DMA((5,)),
        ],
        compiler_params=params(60),
        cost_estimate=pl.CostEstimate(
            flops=2 * TOTAL * 10 * D * MLP, bytes_accessed=20_000_000, transcendentals=0
        ),
        name="all_gradients",
    )(*args)


def run_field(kernel, name, first, blocks, others, field=None):
    args = list(blocks) + list(others) + ([] if field is None else [field])
    return pl.pallas_call(
        functools.partial(kernel, first),
        grid=(FIELD_STEPS,),
        in_specs=[pl.BlockSpec((STRIP, a.shape[1]), lambda t: (first + t, 0)) for a in blocks]
        + [whole(a.shape) for a in others]
        + ([] if field is None else [there]),
        out_specs=[there, there],
        out_shape=[struct((COLS, COLS, D), BF16), struct((SHIFT, COLS, D), BF16)],
        scratch_shapes=[pltpu.VMEM((2, WIN, COLS, D), BF16), pltpu.SemaphoreType.DMA((3,))],
        input_output_aliases={} if field is None else {len(args) - 1: 0},
        compiler_params=params(60),
        cost_estimate=pl.CostEstimate(
            flops=2 * TOTAL * 4 * D * D, bytes_accessed=9_000_000, transcendentals=0
        ),
        name=name,
    )(*args)


def unpack_half(half, rows, w_up, w_down, w_proj, w_qkv, stage, sems):
    def down(first):
        for n in range(2):
            stage[n * D : (n + 1) * D, :D] = rows[first + n * D : first + (n + 1) * D].astype(F32).T
        at = pl.ds(half * 2 * D, 2 * D)
        return pltpu.make_async_copy(stage.at[pl.ds(0, 2 * D), pl.ds(0, D)], w_down.at[at], sems.at[0])

    def wide(out, first, count, at, sem):
        for n in range(count):
            part = rows[first + n * D : first + (n + 1) * D].astype(F32)
            stage[at : at + D, n * D : (n + 1) * D] = part
        return pltpu.make_async_copy(stage.at[pl.ds(at, D), pl.ds(0, count * D)], out, sems.at[sem])

    copies = []
    if half == 0:
        copies.append(wide(w_up, UP, MLP // D, 2 * D, 1))
        copies[-1].start()
        copies.append(down(DOWN[0]))
        copies[-1].start()
    else:
        copies.append(wide(w_qkv, QKV - HALF, 3, 2 * D, 1))
        copies[-1].start()
        copies.append(wide(w_proj, PROJ - HALF, 1, 3 * D, 2))
        copies[-1].start()
        copies.append(down(DOWN[1] - HALF))
        copies[-1].start()
    for copy in copies:
        copy.wait()


def unpack_first_kernel(own, *refs):
    core = lax.rem(lax.axis_index("dp"), 2)
    for half in range(2):

        @pl.when(core == half)
        def _():
            unpack_half(half, own, *refs)


def unpack_second_kernel(
    other, own, in_up, in_down, in_proj, in_qkv, w_up, w_down, w_proj, w_qkv,
    gain_one, bias_one, b_query, b_value, table, b_proj, gain_two, bias_two, b_up, b_down, stage, sems,
):
    core = lax.rem(lax.axis_index("dp"), 2)
    for half in range(2):

        @pl.when(core != half)
        def _():
            unpack_half(half, other, w_up, w_down, w_proj, w_qkv, stage, sems)

    small = slice(SMALL_ONE, HALF)
    mine, others = own[small].astype(F32), other[small].astype(F32)
    first = jnp.where(core == 0, mine, others)
    second = jnp.where(core == 0, others, mine)
    for n, out in enumerate((gain_two, bias_two, b_proj, b_down)):
        out[...] = first[n : n + 1]
    for n in range(MLP // D):
        b_up[:, n * D : (n + 1) * D] = first[4 + n : 5 + n]
    table[...] = second[:HEADS, :ENTRIES]
    for n, out in enumerate((b_query, b_value, gain_one, bias_one)):
        out[...] = second[HEADS + n : HEADS + n + 1]


LARGE = ((D, MLP), (MLP, D), (D, D), (D, 3 * D))
UNPACK_SCRATCH = [pltpu.VMEM((4 * D, MLP), F32), pltpu.SemaphoreType.DMA((3,))]
there = pl.BlockSpec(memory_space=pl.ANY)


def unpack_first(own):
    return pl.pallas_call(
        unpack_first_kernel,
        grid=(1,),
        in_specs=[whole(own.shape)],
        out_specs=[there] * 4,
        out_shape=[struct(shape, F32) for shape in LARGE],
        scratch_shapes=UNPACK_SCRATCH,
        compiler_params=params(24),
        cost_estimate=pl.CostEstimate(flops=0, bytes_accessed=2_400_000, transcendentals=0),
        name="unpack_own_half",
    )(own)


def unpack_second(other, own, large):
    one, four = (1, D), (1, MLP)
    shapes = [one, one, one, one, (HEADS, ENTRIES), one, one, one, four, one]
    out = pl.pallas_call(
        unpack_second_kernel,
        grid=(1,),
        in_specs=[whole(other.shape), whole(own.shape)] + [there] * 4,
        out_specs=[there] * 4 + [whole(shape) for shape in shapes],
        out_shape=[struct(shape, F32) for shape in LARGE] + [struct(shape, F32) for shape in shapes],
        scratch_shapes=UNPACK_SCRATCH,
        input_output_aliases={2: 0, 3: 1, 4: 2, 5: 3},
        compiler_params=params(24),
        name="unpack_other_half",
    )(other, own, *large)
    w_up, w_down, w_proj, w_qkv = out[:4]
    gain_one, bias_one, b_query, b_value, table, b_proj, gain_two, bias_two, b_up, b_down = out[4:]
    return (
        gain_one[0], bias_one[0], w_qkv, b_query[0], b_value[0], table.T, w_proj, b_proj[0],
        gain_two[0], bias_two[0], w_up, b_up[0], w_down, b_down[0],
    )


def coords(index):
    dp, space = divmod(index, 32)
    return {"c": dp % 2, "y": dp // 2 + 2 * ((space // 4) % 2), "x": space % 4, "z": space // 8}


def index_of(c, y, x, z):
    return ((y % 2) * 2 + c) * 32 + z * 8 + (y // 2) * 4 + x


STEPS = (
    ("c", "c", 0),
    ("y", "x", 0),
    ("x", "z", 0),
    ("z", "y", 0),
    ("y", "x", 1),
    ("x", "z", 1),
    ("z", "y", 1),
)
HALVINGS = 3


def partners(step):
    out = []
    for i in range(128):
        at = coords(i)
        axis = step[at["c"]]
        to = dict(at)
        to[axis] = 3 - at[axis] if step[2] else at[axis] ^ 1
        out.append((i, index_of(**to)))
    return out


def own_bit(step, at):
    bits = [((at[step[core]] + 1) // 2) % 2 for core in range(2)]
    return jnp.where(at["c"] == 0, bits[0], bits[1])


def take(rows, start, count):
    return lax.dynamic_slice_in_dim(rows, start, count, 0)


def sum_everywhere(mine, got_core, at, pieces):
    made = {}
    left = list(pieces)

    def exchange(send, step, rows):
        nonlocal made
        got = lax.ppermute(send, AXES, partners(step))
        if left:
            made, rows = lax.optimization_barrier((made, rows))
            made = left.pop(0)(made)
            got, made, rows = lax.optimization_barrier((got, made, rows))
        return got, rows

    kept = []
    rows = None
    for step in STEPS[1:HALVINGS]:
        keep = own_bit(step, at)
        kept.append(keep)
        if rows is None:
            half = mine.shape[0] // 2

            def part(which):
                return take(mine, which * half, half) + take(got_core, which * half, half).astype(F32)

            send, rows = part(1 - keep), part(keep)
        else:
            half = rows.shape[0] // 2
            send, rows = take(rows, (1 - keep) * half, half), take(rows, keep * half, half)
        got, rows = exchange(send.astype(BF16), step, rows)
        rows = rows + got.astype(F32)
    low = rows.astype(BF16)
    for step in STEPS[HALVINGS:]:
        got, low = exchange(low, step, low)
        low = (low.astype(F32) + got.astype(F32)).astype(BF16)
    for step, keep in zip(reversed(STEPS[1:HALVINGS]), reversed(kept)):
        got, low = exchange(low, step, low)
        first = jnp.where(keep == 0, low, got)
        second = jnp.where(keep == 0, got, low)
        low = jnp.concatenate([first, second], 0)
    return low, made


def body(
    image_in, cotangent, regions, first_gain, first_bias, qkv_weight, query_bias, value_bias,
    position_table, proj_weight, proj_bias, second_gain, second_bias, up_weight, up_bias,
    down_weight, down_bias,
):
    many = lax.axis_size("dp") * lax.axis_size("space") == 128
    me = lax.axis_index(AXES)
    at = coords(me)
    halo = jnp.concatenate([image_in[:SHIFT], cotangent[:SHIFT]], 0)
    halo, regions_halo = from_behind((halo, regions[:SHIFT].astype(BF16)), "space", -1)
    gather = gather_matrix()
    spread, spread_rows = label_matrices()
    entries = jnp.asarray(entry_matrix(), BF16)
    mask = jnp.asarray(head_mask(), BF16)
    scatter = jnp.asarray(gather.T, BF16)
    mine, send, tokens, resid, active, d_resid, d_qkv = run_grads(
        image_in, cotangent, halo, regions, regions_halo,
        jnp.asarray(spread, BF16), jnp.asarray(spread_rows), jnp.asarray(gather, BF16),
        mask, entries, position_table.T, first_gain[None], first_bias[None], qkv_weight, query_bias[None],
        value_bias[None], proj_weight, proj_bias[None], second_gain[None], second_bias[None],
        up_weight, up_bias[None], down_weight,
    )
    if many:
        got = lax.ppermute(send, AXES, partners(STEPS[0]))

    def block_output(part, field):
        others = (down_weight, down_bias[None], scatter)
        return run_field(output_kernel, "block_output", part * FIELD_STEPS, (active, resid), others, field)

    def image_gradient(part, field):
        others = (qkv_weight, first_gain[None], scatter)
        blocks = (d_qkv, d_resid, tokens)
        return run_field(image_kernel, "image_gradient", part * FIELD_STEPS, blocks, others, field)

    def halo_rows(made):
        return made | {"halo": from_behind((made["out"][1], made["image"][1]), "space", 1)}

    def fields(made):
        return {
            "block_out": lax.dynamic_update_slice(made["out"][0], made["halo"][0], (0, 0, 0)),
            "image_grad": lax.dynamic_update_slice(made["image"][0], made["halo"][1], (0, 0, 0)),
        }

    pieces = [
        lambda made: {"out": block_output(0, None)},
        lambda made: {"out": block_output(1, made["out"][0])},
        lambda made: made | {"image": image_gradient(0, None)},
        lambda made: made | {"image": image_gradient(1, made["image"][0])},
        lambda made: made,
        lambda made: made,
        halo_rows,
        fields,
    ]
    if many:
        own, made = sum_everywhere(mine, got, at, pieces)
        other = lax.ppermute(own, AXES, partners(STEPS[0]))
        large = unpack_first(own)
        other, large = lax.optimization_barrier((other, large))
    else:
        made = {}
        for piece in pieces:
            made = piece(made)
        own, other = mine.astype(BF16), send
        large = unpack_first(own)
    return (made["block_out"], made["image_grad"]) + unpack_second(other, own, large)


def solution(mesh):
    tokens = P(AXES, None, None)
    return jax.shard_map(
        body,
        mesh=mesh,
        in_specs=(tokens, tokens, P(AXES, None)) + (P(),) * 14,
        out_specs=(tokens, tokens) + (P(),) * 14,
        check_vma=False,
    )
```

```python
import functools
import math

import jax
import jax.numpy as jnp
import numpy as np
from jax import lax
from jax.experimental import pallas as pl
from jax.experimental.pallas import tpu as pltpu
from jax.sharding import PartitionSpec as P

WIN = 7
SHIFT = 3
HEADS = 8
TOKENS = WIN * WIN
PAD = 56
LANES = 64
ENTRIES = (2 * WIN - 1) * (2 * WIN - 1)
COLS = 42
WINDOWS = COLS // WIN
STRIP = WINDOWS * PAD
STRIPS = COLS // WIN
FIELD_STEPS = STRIPS // 2
TOTAL = STRIPS * STRIP
ROW = 48
D = 256
MLP = 1024
BF16 = jnp.bfloat16
F32 = jnp.float32
epsilon = 1e-05
neg = -1000000000.0
AXES = ("dp", "space")
SCALE = 1.0 / math.sqrt(D // HEADS)
LOG2E = 1.4426950408889634
UP = 0
DOWN = (MLP, MLP + 2 * D + 32)
SMALL_ONE = MLP + 2 * D
HALF = SMALL_ONE + 32
PROJ = HALF + 2 * D
QKV = PROJ + D
SMALL_TWO = QKV + 3 * D
assert SMALL_TWO + 32 == 2 * HALF


def from_behind(block, axis, distance):
    devices = range(lax.axis_size(axis))
    route = [((i - distance) % len(devices), i) for i in devices]
    return lax.ppermute(block, axis, route)


def place(i, j):
    return 8 * i + j


def gather_matrix():
    out = np.zeros((STRIP, WIN * ROW), np.float32)
    for w in range(WINDOWS):
        for i in range(WIN):
            for j in range(WIN):
                out[w * PAD + place(i, j), i * ROW + (w * WIN + j + SHIFT) % COLS] = 1.0
    return out


def label_matrices():
    spread = np.zeros((COLS, WINDOWS * 2 * LANES), np.float32)
    rows = np.zeros((WIN, WINDOWS * 2 * LANES), np.float32)
    for w in range(WINDOWS):
        for copy in range(2):
            for i in range(WIN):
                for j in range(WIN):
                    col = (w * 2 + copy) * LANES + place(i, j)
                    spread[(w * WIN + j + SHIFT) % COLS, col] = 1.0
                    rows[i, col] = 1.0
    return spread, rows


def entry_matrix():
    out = np.zeros((WIN * 128, D), np.float32)
    for kj in range(WIN):
        for di in range(1 - WIN, WIN):
            for qj in range(WIN):
                entry = (di + WIN - 1) * (2 * WIN - 1) + qj - kj + WIN - 1
                out[kj * 128 + (8 * di + qj) % 128, entry] = 1.0
    return out


def head_mask():
    return (np.arange(4 * LANES)[:, None] // LANES == np.arange(128)[None] // 32).astype(np.float32)


def dot(a, b):
    return jnp.dot(a, b, preferred_element_type=F32)


def dot_nt(a, b):
    return lax.dot_general(a, b, (((1,), (1,)), ((), ())), preferred_element_type=F32)


def dot_tn(a, b):
    return lax.dot_general(a, b, (((0,), (0,)), ((), ())), preferred_element_type=F32)


def normalize(values):
    center = values - jnp.mean(values, -1, keepdims=True)
    variance = jnp.mean(center * center, -1, keepdims=True)
    recip_dev = lax.rsqrt(variance + epsilon)
    return center * recip_dev, recip_dev


def norm_backward(upstream, normal_part, recip_dev, gain):
    scaled = upstream * gain
    inner_mean = jnp.mean(scaled, -1, keepdims=True)
    cross_mean = jnp.mean(scaled * normal_part, -1, keepdims=True)
    return recip_dev * (scaled - inner_mean - normal_part * cross_mean)


def col_sum(values):
    return jnp.sum(values, 0, keepdims=True)


def raster_rows(ref, halo, first, s):
    last = s == STRIPS - 1
    blank = jnp.zeros((ROW - COLS, D), BF16)
    rows = []
    for i in range(WIN):
        g = s * WIN + i + SHIFT
        if i < WIN - SHIFT:
            value = ref[g]
        else:
            value = jnp.where(
                last, halo[first + i - (WIN - SHIFT)], ref[jnp.minimum(g, COLS - 1)]
            )
        rows += [value, blank]
    return jnp.concatenate(rows, 0)


def put_rows(raster, first, which, out, tails, stage, sems):
    t = pl.program_id(0)
    slot = lax.rem(t, 2)

    def whole_strip(n):
        return pltpu.make_async_copy(
            stage.at[lax.rem(n, 2)], out.at[pl.ds((first + n) * WIN + SHIFT, WIN)], sems.at[lax.rem(n, 2)]
        )

    @pl.when(t >= 2)
    def _():
        whole_strip(t - 2).wait()

    for i in range(WIN):
        stage[slot, i] = raster[i * ROW : i * ROW + COLS]

    @pl.when(first + t < STRIPS - 1)
    def _():
        whole_strip(t).start()

    @pl.when(t == FIELD_STEPS - 1)
    def _():
        if tails is None:
            whole_strip(t - 1).wait()
            whole_strip(t).wait()
        else:
            own = pltpu.make_async_copy(
                stage.at[slot, 0 : WIN - SHIFT], out.at[COLS - (WIN - SHIFT) : COLS], sems.at[slot]
            )
            below = pltpu.make_async_copy(stage.at[slot, WIN - SHIFT : WIN], tails.at[which], sems.at[2])
            own.start()
            below.start()
            whole_strip(t - 1).wait()
            own.wait()
            below.wait()


def pad_rows(values):
    return jnp.concatenate([values, jnp.zeros((LANES - PAD,) + values.shape[1:], values.dtype)], 0)


def head_blocks(low, mask):
    return [jnp.concatenate([low[:, g : g + 128]] * 4, 0) * mask[...] for g in (0, 128)]


def turn_pair(values):
    turned = values.T
    return jnp.concatenate([turned[:LANES], turned[LANES:]], 1)


def three_parts(values):
    high = values.astype(BF16)
    rest = values - high.astype(F32)
    middle = rest.astype(BF16)
    return high, middle, (rest - middle.astype(F32)).astype(BF16)


def lane_ids(shape):
    return lax.broadcasted_iota(jnp.int32, shape, 1)


def build_bias(table, entries, by_head, bias_t):
    parts = three_parts(table * LOG2E)
    for kj in range(WIN):
        one = entries[kj * 128 : (kj + 1) * 128, :ENTRIES]
        by_head[:, kj, :] = dot_nt(parts[0], one) + dot_nt(parts[1], one) + dot_nt(parts[2], one)
    by_head[:, WIN, :] = jnp.full((HEADS, 128), neg, F32)
    lane = lane_ids((8, 128))
    for pair in range(HEADS // 2):
        for ki in range(WIN):
            first = pltpu.roll(by_head[2 * pair], 8 * ki, 1)
            second = pltpu.roll(by_head[2 * pair + 1], (8 * ki + LANES) % 128, 1)
            bias_t[8 * ki : 8 * ki + 8, 128 * pair : 128 * pair + 128] = jnp.where(
                lane < LANES, first, second
            )


def table_gradient(logit_sums, entries, by_head):
    lane = lane_ids((8, 128))
    for pair in range(HEADS // 2):
        for half in range(2):
            total = jnp.zeros((8, 128), F32)
            for ki in range(WIN):
                block = logit_sums[8 * ki : 8 * ki + 8, 128 * pair : 128 * pair + 128]
                own = jnp.where((lane < LANES) == (half == 0), block, 0.0)
                total = total + pltpu.roll(own, (128 - 8 * ki - LANES * half) % 128, 1)
            by_head[2 * pair + half] = total
    out = jnp.zeros((HEADS, D), F32)
    for kj in range(WIN):
        one = entries[kj * 128 : (kj + 1) * 128]
        for part in three_parts(by_head[:, kj, :]):
            out = out + dot(part, one)
    return out


def spans():
    return [slice(w * PAD, (w + 1) * PAD) for w in range(WINDOWS)]


def forward_stage(s, r):
    rows = pl.ds(pl.multiple_of(s * STRIP, 16), STRIP)
    slot = lax.rem(s, 2)
    tokens = dot(r.gather[...], raster_rows(r.image, r.halo, 0, s))
    r.tokens_out[...] = tokens.astype(BF16)
    yield
    r.cot_all[rows] = dot(r.gather[...], raster_rows(r.cot, r.halo, SHIFT, s)).astype(BF16)
    yield
    normal_one, _ = normalize(tokens)
    first_low = (normal_one * r.gain_one[...] + r.bias_one[...]).astype(BF16)
    r.first_all[rows, :D] = first_low
    yield
    query = dot(first_low, r.w_qkv[:, :D]) + r.b_query[...]
    key = dot(first_low, r.w_qkv[:, D : 2 * D])
    value = dot(first_low, r.w_qkv[:, 2 * D :]) + r.b_value[...]
    yield
    key_labels = r.lane_labels[s].T
    logits = []
    for w, span in enumerate(spans()):
        query_low = pad_rows(query[span]).astype(BF16)
        key_low = pad_rows(key[span]).astype(BF16)
        value_low = pad_rows(value[span]).astype(BF16)
        r.qkv_win[slot, w, :, :D] = query_low
        r.qkv_win[slot, w, :, D : 2 * D] = key_low
        r.qkv_win[slot, w, :, 2 * D :] = value_low
        blocks = head_blocks(query_low, r.mask)
        logits.append(
            [dot_nt(key_low[:, 128 * g : 128 * g + 128], blocks[g])[:PAD] for g in range(2)]
        )
        yield
    turned = []
    for w in range(WINDOWS):
        same = key_labels[:PAD, w : w + 1] == r.lane_labels[s, w : w + 1, :]
        turned.append([])
        for pair in range(HEADS // 2):
            cols = slice(128 * pair, 128 * pair + 128)
            part = logits[w][pair // 2][:, 128 * (pair % 2) : 128 * (pair % 2) + 128]
            part = jnp.where(same, part * (SCALE * LOG2E) + r.bias_t[:, cols], neg)
            powers = jnp.exp2(part - jnp.max(part, 0, keepdims=True))
            attend = powers * (1.0 / jnp.sum(powers, 0, keepdims=True))
            attend_low = pad_rows(attend).astype(BF16)
            r.attend_win[slot, w, :, cols] = attend_low
            turned[w].append(turn_pair(attend_low))
        yield
    mixed_parts = []
    for w in range(WINDOWS):
        blocks = head_blocks(r.qkv_win[slot, w, :, 2 * D :], r.mask)
        mixed_parts.append(
            jnp.concatenate(
                [
                    dot(jnp.concatenate(turned[w][2 * g : 2 * g + 2], 1), blocks[g])[:PAD]
                    for g in range(2)
                ],
                1,
            )
        )
        yield
    mixed_low = jnp.concatenate(mixed_parts, 0).astype(BF16)
    r.mixed_all[rows] = mixed_low
    resid = tokens + dot(mixed_low, r.w_proj[...]) + r.b_proj[...]
    r.resid_win[slot] = resid
    yield


def backward_stage(s, r):
    rows = pl.ds(pl.multiple_of(s * STRIP, 16), STRIP)
    slot = lax.rem(s, 2)
    sums = r.sums
    resid = r.resid_win[slot]
    r.resid_out[...] = resid
    normal_two, recip_two = normalize(resid)
    second_low = (normal_two * r.gain_two[...] + r.bias_two[...]).astype(BF16)
    r.second_all[rows, :D] = second_low
    yield
    cot_low = r.cot_all[rows]
    d_second = jnp.zeros((STRIP, D), F32)
    for n in range(MLP // D):
        cols = slice(n * D, (n + 1) * D)
        inner = dot(second_low, r.w_up[:, cols]) + r.b_up[:, cols]
        cumulative = 0.5 * lax.erf(inner * 0.7071067811865476) + 0.5
        active_low = (inner * cumulative).astype(BF16)
        r.active_all[rows, cols] = active_low
        r.active_out[:, cols] = active_low
        yield
        gauss = jnp.exp2(inner * inner * (-0.5 * LOG2E))
        slope = cumulative + inner * gauss * 0.3989422804014327
        d_inner = (dot_nt(cot_low, r.w_down[cols]) * slope).astype(BF16)
        r.d_inner_all[rows, cols] = d_inner
        yield
        d_second = d_second + dot_nt(d_inner, r.w_up[:, cols])
        yield
    cot_f32 = cot_low.astype(F32)
    d_resid = cot_f32 + norm_backward(d_second, normal_two, recip_two, r.gain_two[...])
    d_branch = d_resid.astype(BF16)
    r.d_branch_all[rows] = d_branch
    r.d_resid_out[...] = d_resid
    yield
    d_mixed = dot_nt(d_branch, r.w_proj[...])
    yield
    sums[0:1] += col_sum(d_second * normal_two)
    sums[1:2] += col_sum(d_second)
    sums[2:3] += col_sum(d_resid)
    sums[3:4] += col_sum(cot_f32)
    yield
    mixed_blocks = []
    d_attends = []
    for w, span in enumerate(spans()):
        blocks = head_blocks(pad_rows(d_mixed[span]).astype(BF16), r.mask)
        mixed_blocks.append(blocks)
        value_low = r.qkv_win[slot, w, :, 2 * D :]
        d_attends.append(
            [dot_nt(value_low[:, 128 * g : 128 * g + 128], blocks[g])[:PAD] for g in range(2)]
        )
        yield
    d_logits = []
    turned = []
    for w in range(WINDOWS):
        d_logits.append([])
        turned.append([])
        for pair in range(HEADS // 2):
            cols = slice(128 * pair, 128 * pair + 128)
            part = d_attends[w][pair // 2][:, 128 * (pair % 2) : 128 * (pair % 2) + 128]
            attend = r.attend_win[slot, w, :, cols].astype(F32)[:PAD]
            cross = jnp.sum(part * attend, 0, keepdims=True)
            part = attend * (part - cross)
            r.logit_sums[:, cols] += part
            low = pad_rows(part).astype(BF16)
            d_logits[w].append(low)
            turned[w].append(turn_pair(low))
        yield
    parts = []
    for w in range(WINDOWS):
        query_blocks = head_blocks(r.qkv_win[slot, w, :, :D], r.mask)
        key_blocks = head_blocks(r.qkv_win[slot, w, :, D : 2 * D], r.mask)
        d_query, d_key, d_value = [], [], []
        for g in range(2):
            two = slice(2 * g, 2 * g + 2)
            attend_low = r.attend_win[slot, w, :, 256 * g : 256 * g + 256]
            d_value.append(dot(attend_low, mixed_blocks[w][g])[:PAD])
            d_key.append(dot(jnp.concatenate(d_logits[w][two], 1), query_blocks[g])[:PAD] * SCALE)
            d_query.append(dot(jnp.concatenate(turned[w][two], 1), key_blocks[g])[:PAD] * SCALE)
        parts.append(jnp.concatenate(d_query + d_key + d_value, 1))
        yield
    d_qkv = jnp.concatenate(parts, 0).astype(BF16)
    r.d_qkv_all[rows] = d_qkv
    r.d_qkv_out[...] = d_qkv
    yield


def run(*stages):
    order = []
    for n, stage in enumerate(stages):
        count = PIECES[stage.__name__]
        order += [((piece + 0.5) / count * (0.5 if n else 1.0), n) for piece in range(count)]
    for _, n in sorted(order):
        next(stages[n])
    for stage in stages:
        assert next(stage, None) is None


PIECES = {"forward_stage": 5 + 3 * WINDOWS, "backward_stage": 1 + 3 * (MLP // D) + 3 + 3 * WINDOWS + 1}


def down_rows(n):
    return DOWN[n // 2] + (n % 2) * D


def finish(r):
    core = lax.rem(lax.axis_index("dp"), 2)
    grads = r.grads

    def put(start, rows):
        grads[start : start + rows.shape[0]] = rows
        r.grads_low[start : start + rows.shape[0]] = rows.astype(BF16)

    def sends(n, start, count):
        half, at = divmod(start, HALF)
        span = pl.ds(at, count)
        keep = pltpu.make_async_copy(grads.at[pl.ds(start, count)], r.keep.at[span], r.sems.at[n])
        send = pltpu.make_async_copy(r.grads_low.at[pl.ds(start, count)], r.send.at[span], r.sems.at[n])
        return half, keep, send

    def begin(half, keep, send):
        @pl.when(core == half)
        def _():
            keep.start()

        @pl.when(core != half)
        def _():
            send.start()

    def end(half, keep, send):
        @pl.when(core == half)
        def _():
            keep.wait()

        @pl.when(core != half)
        def _():
            send.wait()

    small = SMALL_TWO
    put(small, table_gradient(r.logit_sums, r.entries, r.by_head))
    product = dot_tn(r.first_all[:, : D + 8], r.d_qkv_all[...])
    sums = product[D : D + 8]
    for n in range(3):
        put(QKV + n * D, product[:D, n * D : (n + 1) * D])
    bias_grad = jnp.zeros((8, D), F32)
    for part in three_parts(sums):
        bias_grad = bias_grad + dot_nt(part, r.w_qkv[...])
    cross = jnp.zeros((8, D), F32)
    for part in three_parts(product[:D] * r.w_qkv[...].astype(F32)):
        cross = cross + dot_nt(jnp.ones((8, 3 * D), BF16), part)
    gain_grad = (cross[0:1] - r.bias_one[...] * bias_grad[0:1]) / r.gain_one[...]
    put(
        small + 8,
        jnp.concatenate(
            [sums[0:1, :D], sums[0:1, 2 * D :], gain_grad, bias_grad[0:1], jnp.zeros((20, D), F32)], 0
        ),
    )
    put(PROJ, dot_tn(r.mixed_all[...], r.d_branch_all[...]))
    product = dot_tn(r.second_all[:, : D + 8], r.d_inner_all[...])
    for n in range(MLP // D):
        put(UP + n * D, product[:D, n * D : (n + 1) * D])
    ups = [product[D : D + 1, n * D : (n + 1) * D] for n in range(MLP // D)]
    put(SMALL_ONE, jnp.concatenate([r.sums[0:4]] + ups + [jnp.zeros((24, D), F32)], 0))
    copies = [sends(0, UP, MLP), sends(1, SMALL_ONE, 32), sends(2, PROJ, 2 * HALF - PROJ)]
    for copy in copies:
        begin(*copy)
    product = dot_tn(r.cot_all[...], r.active_all[...])
    for n in range(MLP // D):
        put(down_rows(n), product[:, n * D : (n + 1) * D])
    later = [sends(3, DOWN[0], 2 * D), sends(4, DOWN[1], 2 * D)]
    for copy in later:
        begin(*copy)
    for copy in copies + later:
        end(*copy)


class Refs:
    def __init__(self, names, refs):
        self.__dict__.update(zip(names, refs))


NAMES = [
    "image", "cot", "halo", "regions", "regions_halo", "spread", "spread_rows", "gather", "mask", "entries", "table",
    "gain_one", "bias_one", "w_qkv", "b_query", "b_value", "w_proj", "b_proj", "gain_two", "bias_two", "w_up", "b_up",
    "w_down", "keep", "send", "tokens_out", "resid_out", "active_out", "d_resid_out", "d_qkv_out",
    "lane_labels", "by_head", "bias_t", "logit_sums", "qkv_win", "attend_win", "resid_win", "sums",
    "first_all", "cot_all", "mixed_all", "second_all", "active_all", "d_inner_all", "d_branch_all", "d_qkv_all",
    "grads", "grads_low", "sems",
]


def grads_kernel(*refs):
    r = Refs(NAMES, refs)
    s = pl.program_id(0)

    @pl.when(s == 0)
    def _():
        own = dot(r.regions[...].astype(F32).astype(BF16), r.spread[...])
        below = dot(r.regions_halo[...], r.spread[...])
        for n in range(STRIPS):
            top = n * WIN + SHIFT
            part = own[top : min(top + WIN, COLS)]
            if top + WIN > COLS:
                part = jnp.concatenate([part, below], 0)
            row = jnp.sum(part * r.spread_rows[...], 0, keepdims=True)
            r.lane_labels[n] = jnp.concatenate(
                [row[:, 128 * w : 128 * w + 128] for w in range(WINDOWS)] + [jnp.zeros((2, 128), F32)], 0
            )
        build_bias(r.table[...], r.entries, r.by_head, r.bias_t)
        r.logit_sums[...] = jnp.zeros_like(r.logit_sums)
        one = (lane_ids((TOTAL, 128)) == 0).astype(F32).astype(BF16)
        r.first_all[:, D:] = one
        r.second_all[:, D:] = one
        r.sums[...] = jnp.zeros_like(r.sums)
        run(forward_stage(s, r))

    @pl.when((s > 0) & (s < STRIPS))
    def _():
        run(backward_stage(s - 1, r), forward_stage(s, r))

    @pl.when(s == STRIPS)
    def _():
        run(backward_stage(s - 1, r))
        finish(r)


def output_strip(active, resid, w_down, b_down, scatter):
    result = resid[...] + b_down[...] + dot(active[...], w_down[...])
    return dot(scatter[...], result.astype(BF16)).astype(BF16)


def image_strip(d_qkv, d_resid, tokens, w_qkv, gain, scatter):
    normal, recip_dev = normalize(tokens[...].astype(F32))
    d_first = dot_nt(d_qkv[...], w_qkv[...])
    grad = d_resid[...] + norm_backward(d_first, normal, recip_dev, gain[...])
    return dot(scatter[...], grad.astype(BF16)).astype(BF16)


there = pl.BlockSpec(memory_space=pl.ANY)


def whole(shape):
    return pl.BlockSpec(shape, lambda s: (0,) * len(shape))


def strips(shape):
    return pl.BlockSpec(shape, lambda s: (s,) + (0,) * (len(shape) - 1))


def struct(shape, dtype):
    return jax.ShapeDtypeStruct(shape, dtype)


def params(mebibytes):
    return pltpu.CompilerParams(
        vmem_limit_bytes=mebibytes * 1024 * 1024, dimension_semantics=("arbitrary",)
    )


def run_grads(*args):
    early = lambda s: (jnp.minimum(s, STRIPS - 1), 0)
    late = lambda s: (jnp.maximum(s - 1, 0), 0)
    return pl.pallas_call(
        grads_kernel,
        grid=(STRIPS + 1,),
        in_specs=[whole(a.shape) for a in args],
        out_specs=[
            pl.BlockSpec(memory_space=pl.ANY),
            pl.BlockSpec(memory_space=pl.ANY),
            pl.BlockSpec((STRIP, D), early),
            pl.BlockSpec((STRIP, D), late),
            pl.BlockSpec((STRIP, MLP), late),
            pl.BlockSpec((STRIP, D), late),
            pl.BlockSpec((STRIP, 3 * D), late),
        ],
        out_shape=[
            struct((HALF, D), F32),
            struct((HALF, D), BF16),
            struct((TOTAL, D), BF16),
            struct((TOTAL, D), F32),
            struct((TOTAL, MLP), BF16),
            struct((TOTAL, D), F32),
            struct((TOTAL, 3 * D), BF16),
        ],
        scratch_shapes=[
            pltpu.VMEM((STRIPS, 8, 128), F32),
            pltpu.VMEM((HEADS, 8, 128), F32),
            pltpu.VMEM((PAD, HEADS * LANES), F32),
            pltpu.VMEM((PAD, HEADS * LANES), F32),
            pltpu.VMEM((2, WINDOWS, LANES, 3 * D), BF16),
            pltpu.VMEM((2, WINDOWS, LANES, HEADS * LANES), BF16),
            pltpu.VMEM((2, STRIP, D), F32),
            pltpu.VMEM((8, D), F32),
            pltpu.VMEM((TOTAL, D + 128), BF16),
            pltpu.VMEM((TOTAL, D), BF16),
            pltpu.VMEM((TOTAL, D), BF16),
            pltpu.VMEM((TOTAL, D + 128), BF16),
            pltpu.VMEM((TOTAL, MLP), BF16),
            pltpu.VMEM((TOTAL, MLP), BF16),
            pltpu.VMEM((TOTAL, D), BF16),
            pltpu.VMEM((TOTAL, 3 * D), BF16),
            pltpu.VMEM((2 * HALF, D), F32),
            pltpu.VMEM((2 * HALF, D), BF16),
            pltpu.SemaphoreType.DMA((5,)),
        ],
        compiler_params=params(60),
        cost_estimate=pl.CostEstimate(
            flops=2 * TOTAL * 10 * D * MLP, bytes_accessed=20_000_000, transcendentals=0
        ),
        name="all_gradients",
    )(*args)


def run_field(strip, name, which, blocks, others, field=None, tails=None):
    lower = field is None
    first = FIELD_STEPS if lower else 0
    given = [a for a in (field, tails) if a is not None]
    inputs = len(blocks) + len(others)
    shapes = [struct((COLS, COLS, D), BF16)] + [struct((2, SHIFT, COLS, D), BF16)] * lower

    def kernel(*refs):
        out = refs[inputs + len(given)]
        below = refs[inputs + len(given) + 1] if lower else None
        put_rows(strip(*refs[:inputs]), first, which, out, below, *refs[-2:])

    return pl.pallas_call(
        kernel,
        grid=(FIELD_STEPS,),
        in_specs=[pl.BlockSpec((STRIP, a.shape[1]), lambda t: (first + t, 0)) for a in blocks]
        + [whole(a.shape) for a in others]
        + [there] * len(given),
        out_specs=[there] * len(shapes),
        out_shape=shapes,
        scratch_shapes=[pltpu.VMEM((2, WIN, COLS, D), BF16), pltpu.SemaphoreType.DMA((3,))],
        input_output_aliases={inputs: 1 if lower else 0} if given else {},
        compiler_params=params(60),
        cost_estimate=pl.CostEstimate(
            flops=2 * TOTAL * 4 * D * D, bytes_accessed=9_000_000, transcendentals=0
        ),
        name=name,
    )(*blocks, *others, *given)


def unpack_half(half, rows, w_up, w_down, w_proj, w_qkv, stage, sems):
    def down(first):
        for n in range(2):
            stage[n * D : (n + 1) * D, :D] = rows[first + n * D : first + (n + 1) * D].astype(F32).T
        at = pl.ds(half * 2 * D, 2 * D)
        return pltpu.make_async_copy(stage.at[pl.ds(0, 2 * D), pl.ds(0, D)], w_down.at[at], sems.at[0])

    def wide(out, first, count, at, sem):
        for n in range(count):
            part = rows[first + n * D : first + (n + 1) * D].astype(F32)
            stage[at : at + D, n * D : (n + 1) * D] = part
        return pltpu.make_async_copy(stage.at[pl.ds(at, D), pl.ds(0, count * D)], out, sems.at[sem])

    copies = []
    if half == 0:
        copies.append(wide(w_up, UP, MLP // D, 2 * D, 1))
        copies[-1].start()
        copies.append(down(DOWN[0]))
        copies[-1].start()
    else:
        copies.append(wide(w_qkv, QKV - HALF, 3, 2 * D, 1))
        copies[-1].start()
        copies.append(wide(w_proj, PROJ - HALF, 1, 3 * D, 2))
        copies[-1].start()
        copies.append(down(DOWN[1] - HALF))
        copies[-1].start()
    for copy in copies:
        copy.wait()


def unpack_first_kernel(own, *refs):
    core = lax.rem(lax.axis_index("dp"), 2)
    for half in range(2):

        @pl.when(core == half)
        def _():
            unpack_half(half, own, *refs)


def unpack_second_kernel(
    other, own, in_up, in_down, in_proj, in_qkv, w_up, w_down, w_proj, w_qkv,
    gain_one, bias_one, b_query, b_value, table, b_proj, gain_two, bias_two, b_up, b_down, stage, sems,
):
    core = lax.rem(lax.axis_index("dp"), 2)
    for half in range(2):

        @pl.when(core != half)
        def _():
            unpack_half(half, other, w_up, w_down, w_proj, w_qkv, stage, sems)

    small = slice(SMALL_ONE, HALF)
    mine, others = own[small].astype(F32), other[small].astype(F32)
    first = jnp.where(core == 0, mine, others)
    second = jnp.where(core == 0, others, mine)
    for n, out in enumerate((gain_two, bias_two, b_proj, b_down)):
        out[...] = first[n : n + 1]
    for n in range(MLP // D):
        b_up[:, n * D : (n + 1) * D] = first[4 + n : 5 + n]
    table[...] = second[:HEADS, :ENTRIES]
    for n, out in enumerate((b_query, b_value, gain_one, bias_one)):
        out[...] = second[HEADS + n : HEADS + n + 1]


LARGE = ((D, MLP), (MLP, D), (D, D), (D, 3 * D))
UNPACK_SCRATCH = [pltpu.VMEM((4 * D, MLP), F32), pltpu.SemaphoreType.DMA((3,))]
def unpack_first(own):
    return pl.pallas_call(
        unpack_first_kernel,
        grid=(1,),
        in_specs=[whole(own.shape)],
        out_specs=[there] * 4,
        out_shape=[struct(shape, F32) for shape in LARGE],
        scratch_shapes=UNPACK_SCRATCH,
        compiler_params=params(24),
        cost_estimate=pl.CostEstimate(flops=0, bytes_accessed=2_400_000, transcendentals=0),
        name="unpack_own_half",
    )(own)


def unpack_second(other, own, large):
    one, four = (1, D), (1, MLP)
    shapes = [one, one, one, one, (HEADS, ENTRIES), one, one, one, four, one]
    out = pl.pallas_call(
        unpack_second_kernel,
        grid=(1,),
        in_specs=[whole(other.shape), whole(own.shape)] + [there] * 4,
        out_specs=[there] * 4 + [whole(shape) for shape in shapes],
        out_shape=[struct(shape, F32) for shape in LARGE] + [struct(shape, F32) for shape in shapes],
        scratch_shapes=UNPACK_SCRATCH,
        input_output_aliases={2: 0, 3: 1, 4: 2, 5: 3},
        compiler_params=params(24),
        name="unpack_other_half",
    )(other, own, *large)
    w_up, w_down, w_proj, w_qkv = out[:4]
    gain_one, bias_one, b_query, b_value, table, b_proj, gain_two, bias_two, b_up, b_down = out[4:]
    return (
        gain_one[0], bias_one[0], w_qkv, b_query[0], b_value[0], table.T, w_proj, b_proj[0],
        gain_two[0], bias_two[0], w_up, b_up[0], w_down, b_down[0],
    )


def coords(index):
    dp, space = divmod(index, 32)
    return {"c": dp % 2, "y": dp // 2 + 2 * ((space // 4) % 2), "x": space % 4, "z": space // 8}


def index_of(c, y, x, z):
    return ((y % 2) * 2 + c) * 32 + z * 8 + (y // 2) * 4 + x


DISTANCES = (2, 1, 3)
STAGES = (("y", "x"), ("x", "z"), ("z", "y"))


def other_core():
    return [(i, index_of(**(coords(i) | {"c": 1 - i // 32 % 2}))) for i in range(128)]


def around(stage, distance):
    out = []
    for i in range(128):
        at = coords(i)
        axis = stage[at["c"]]
        out.append((i, index_of(**(at | {axis: (at[axis] + distance) % 4}))))
    return out


def take(rows, start, count):
    return lax.dynamic_slice_in_dim(rows, start, count, 0)


def sum_everywhere(mine, got_core, at, pieces):
    made = {}
    left = list(pieces)

    def exchange(stage, sends, own):
        nonlocal made
        got = [lax.ppermute(sends[d], AXES, around(stage, d)) for d in DISTANCES]
        made, own = lax.optimization_barrier((made, own))
        made = left.pop(0)(made)
        got, made, own = lax.optimization_barrier((got, made, own))
        return dict(zip(DISTANCES, got)), own

    def place(stage):
        return jnp.where(at["c"] == 0, at[stage[0]], at[stage[1]])

    stage = STAGES[0]
    here = place(stage)
    count = mine.shape[0] // 4

    def part(which):
        start = which * count
        return take(mine, start, count) + take(got_core, start, count).astype(F32)

    sends = {d: part((here + d) % 4).astype(BF16) for d in DISTANCES}
    got, rows = exchange(stage, sends, part(here))
    for d in DISTANCES:
        rows = rows + got[d].astype(F32)
    low = rows.astype(BF16)
    for stage in STAGES[1:]:
        got, low = exchange(stage, {d: low for d in DISTANCES}, low)
        pairs = low.astype(F32) + got[2].astype(F32), got[1].astype(F32) + got[3].astype(F32)
        low = (pairs[0] + pairs[1]).astype(BF16)
    got, low = exchange(STAGES[0], {d: low for d in DISTANCES}, low)
    whole_half = jnp.zeros((4 * count, D), BF16)
    for d, rows in [(0, low), *got.items()]:
        whole_half = lax.dynamic_update_slice(whole_half, rows, ((here - d) % 4 * count, 0))
    return whole_half, made


def body(
    image_in, cotangent, regions, first_gain, first_bias, qkv_weight, query_bias, value_bias,
    position_table, proj_weight, proj_bias, second_gain, second_bias, up_weight, up_bias,
    down_weight, down_bias,
):
    many = lax.axis_size("dp") * lax.axis_size("space") == 128
    me = lax.axis_index(AXES)
    at = coords(me)
    halo = jnp.concatenate([image_in[:SHIFT], cotangent[:SHIFT]], 0)
    halo, regions_halo = from_behind((halo, regions[:SHIFT].astype(BF16)), "space", -1)
    gather = gather_matrix()
    spread, spread_rows = label_matrices()
    entries = jnp.asarray(entry_matrix(), BF16)
    mask = jnp.asarray(head_mask(), BF16)
    scatter = jnp.asarray(gather.T, BF16)
    mine, send, tokens, resid, active, d_resid, d_qkv = run_grads(
        image_in, cotangent, halo, regions, regions_halo,
        jnp.asarray(spread, BF16), jnp.asarray(spread_rows), jnp.asarray(gather, BF16),
        mask, entries, position_table.T, first_gain[None], first_bias[None], qkv_weight, query_bias[None],
        value_bias[None], proj_weight, proj_bias[None], second_gain[None], second_bias[None],
        up_weight, up_bias[None], down_weight,
    )
    if many:
        got = lax.ppermute(send, AXES, other_core())

    def block_output(*given):
        others = (down_weight, down_bias[None], scatter)
        return run_field(output_strip, "block_output", 0, (active, resid), others, *given)

    def image_gradient(*given):
        others = (qkv_weight, first_gain[None], scatter)
        return run_field(image_strip, "image_gradient", 1, (d_qkv, d_resid, tokens), others, *given)

    def lower_out(made):
        field, tails = block_output()
        return {"out": field, "tails": tails}

    def lower_image(made):
        field, tails = image_gradient(None, made["tails"])
        return made | {"image": field, "tails": tails}

    def upper_out(made):
        return made | {"out": block_output(made["out"])[0]}

    def upper_image(made):
        halo = from_behind(made["tails"], "space", 1)
        return {"out": made["out"], "image": image_gradient(made["image"])[0], "halo": halo}

    pieces = [lower_out, lower_image, upper_out, upper_image]
    if many:
        own, made = sum_everywhere(mine, got, at, pieces)
        other = lax.ppermute(own, AXES, other_core())
        large = unpack_first(own)
        other, large = lax.optimization_barrier((other, large))
    else:
        made = {}
        for piece in pieces:
            made = piece(made)
        own, other = mine.astype(BF16), send
        large = unpack_first(own)
    block_out = lax.dynamic_update_slice(made["out"], made["halo"][0], (0, 0, 0))
    image_grad = lax.dynamic_update_slice(made["image"], made["halo"][1], (0, 0, 0))
    return (block_out, image_grad) + unpack_second(other, own, large)


def solution(mesh):
    tokens = P(AXES, None, None)
    return jax.shard_map(
        body,
        mesh=mesh,
        in_specs=(tokens, tokens, P(AXES, None)) + (P(),) * 14,
        out_specs=(tokens, tokens) + (P(),) * 14,
        check_vma=False,
    )
```

```python
import functools
import math

import jax
import jax.numpy as jnp
import numpy as np
from jax import lax
from jax.experimental import pallas as pl
from jax.experimental.pallas import tpu as pltpu
from jax.sharding import PartitionSpec as P

WIN = 7
SHIFT = 3
HEADS = 8
TOKENS = WIN * WIN
PAD = 56
LANES = 64
ENTRIES = (2 * WIN - 1) * (2 * WIN - 1)
COLS = 42
WINDOWS = COLS // WIN
STRIP = WINDOWS * PAD
STRIPS = COLS // WIN
FIELD_STEPS = STRIPS // 2
TOTAL = STRIPS * STRIP
ROW = 48
D = 256
MLP = 1024
BF16 = jnp.bfloat16
F32 = jnp.float32
epsilon = 1e-05
neg = -1000000000.0
AXES = ("dp", "space")
SCALE = 1.0 / math.sqrt(D // HEADS)
LOG2E = 1.4426950408889634
UP = 0
DOWN = (MLP, MLP + 2 * D + 32)
SMALL_ONE = MLP + 2 * D
HALF = SMALL_ONE + 32
PROJ = HALF + 2 * D
QKV = PROJ + D
SMALL_TWO = QKV + 3 * D
assert SMALL_TWO + 32 == 2 * HALF


def from_behind(block, axis, distance):
    devices = range(lax.axis_size(axis))
    route = [((i - distance) % len(devices), i) for i in devices]
    return lax.ppermute(block, axis, route)


def place(i, j):
    return 8 * i + j


def gather_matrix():
    out = np.zeros((STRIP, WIN * ROW), np.float32)
    for w in range(WINDOWS):
        for i in range(WIN):
            for j in range(WIN):
                out[w * PAD + place(i, j), i * ROW + (w * WIN + j + SHIFT) % COLS] = 1.0
    return out


def label_matrices():
    spread = np.zeros((COLS, WINDOWS * 2 * LANES), np.float32)
    rows = np.zeros((WIN, WINDOWS * 2 * LANES), np.float32)
    for w in range(WINDOWS):
        for copy in range(2):
            for i in range(WIN):
                for j in range(WIN):
                    col = (w * 2 + copy) * LANES + place(i, j)
                    spread[(w * WIN + j + SHIFT) % COLS, col] = 1.0
                    rows[i, col] = 1.0
    return spread, rows


def entry_matrix():
    out = np.zeros((WIN * 128, D), np.float32)
    for kj in range(WIN):
        for di in range(1 - WIN, WIN):
            for qj in range(WIN):
                entry = (di + WIN - 1) * (2 * WIN - 1) + qj - kj + WIN - 1
                out[kj * 128 + (8 * di + qj) % 128, entry] = 1.0
    return out


def head_mask():
    return (np.arange(4 * LANES)[:, None] // LANES == np.arange(128)[None] // 32).astype(np.float32)


def dot(a, b):
    return jnp.dot(a, b, preferred_element_type=F32)


def dot_nt(a, b):
    return lax.dot_general(a, b, (((1,), (1,)), ((), ())), preferred_element_type=F32)


def dot_tn(a, b):
    return lax.dot_general(a, b, (((0,), (0,)), ((), ())), preferred_element_type=F32)


def normalize(values):
    center = values - jnp.mean(values, -1, keepdims=True)
    variance = jnp.mean(center * center, -1, keepdims=True)
    recip_dev = lax.rsqrt(variance + epsilon)
    return center * recip_dev, recip_dev


def norm_backward(upstream, normal_part, recip_dev, gain):
    scaled = upstream * gain
    inner_mean = jnp.mean(scaled, -1, keepdims=True)
    cross_mean = jnp.mean(scaled * normal_part, -1, keepdims=True)
    return recip_dev * (scaled - inner_mean - normal_part * cross_mean)


def col_sum(values):
    return jnp.sum(values, 0, keepdims=True)


def raster_rows(ref, halo, first, s):
    last = s == STRIPS - 1
    blank = jnp.zeros((ROW - COLS, D), BF16)
    rows = []
    for i in range(WIN):
        g = s * WIN + i + SHIFT
        if i < WIN - SHIFT:
            value = ref[g]
        else:
            value = jnp.where(
                last, halo[first + i - (WIN - SHIFT)], ref[jnp.minimum(g, COLS - 1)]
            )
        rows += [value, blank]
    return jnp.concatenate(rows, 0)


def put_rows(raster, first, which, out, tails, stage, sems):
    t = pl.program_id(0)
    slot = lax.rem(t, 2)

    def whole_strip(n):
        return pltpu.make_async_copy(
            stage.at[lax.rem(n, 2)], out.at[pl.ds((first + n) * WIN + SHIFT, WIN)], sems.at[lax.rem(n, 2)]
        )

    @pl.when(t >= 2)
    def _():
        whole_strip(t - 2).wait()

    for i in range(WIN):
        stage[slot, i] = raster[i * ROW : i * ROW + COLS]

    @pl.when(first + t < STRIPS - 1)
    def _():
        whole_strip(t).start()

    @pl.when(t == FIELD_STEPS - 1)
    def _():
        if tails is None:
            whole_strip(t - 1).wait()
            whole_strip(t).wait()
        else:
            own = pltpu.make_async_copy(
                stage.at[slot, 0 : WIN - SHIFT], out.at[COLS - (WIN - SHIFT) : COLS], sems.at[slot]
            )
            below = pltpu.make_async_copy(stage.at[slot, WIN - SHIFT : WIN], tails.at[which], sems.at[2])
            own.start()
            below.start()
            whole_strip(t - 1).wait()
            own.wait()
            below.wait()


def pad_rows(values):
    return jnp.concatenate([values, jnp.zeros((LANES - PAD,) + values.shape[1:], values.dtype)], 0)


def head_blocks(low, mask):
    return [jnp.concatenate([low[:, g : g + 128]] * 4, 0) * mask[...] for g in (0, 128)]


def turn_pair(values):
    turned = values.T
    return jnp.concatenate([turned[:LANES], turned[LANES:]], 1)


def three_parts(values):
    high = values.astype(BF16)
    rest = values - high.astype(F32)
    middle = rest.astype(BF16)
    return high, middle, (rest - middle.astype(F32)).astype(BF16)


def lane_ids(shape):
    return lax.broadcasted_iota(jnp.int32, shape, 1)


def build_bias(table, entries, by_head, bias_t):
    parts = three_parts(table * LOG2E)
    for kj in range(WIN):
        one = entries[kj * 128 : (kj + 1) * 128, :ENTRIES]
        by_head[:, kj, :] = dot_nt(parts[0], one) + dot_nt(parts[1], one) + dot_nt(parts[2], one)
    by_head[:, WIN, :] = jnp.full((HEADS, 128), neg, F32)
    lane = lane_ids((8, 128))
    for pair in range(HEADS // 2):
        for ki in range(WIN):
            first = pltpu.roll(by_head[2 * pair], 8 * ki, 1)
            second = pltpu.roll(by_head[2 * pair + 1], (8 * ki + LANES) % 128, 1)
            bias_t[8 * ki : 8 * ki + 8, 128 * pair : 128 * pair + 128] = jnp.where(
                lane < LANES, first, second
            )


def table_gradient(logit_sums, entries, by_head):
    lane = lane_ids((8, 128))
    for pair in range(HEADS // 2):
        for half in range(2):
            total = jnp.zeros((8, 128), F32)
            for ki in range(WIN):
                block = logit_sums[8 * ki : 8 * ki + 8, 128 * pair : 128 * pair + 128]
                own = jnp.where((lane < LANES) == (half == 0), block, 0.0)
                total = total + pltpu.roll(own, (128 - 8 * ki - LANES * half) % 128, 1)
            by_head[2 * pair + half] = total
    out = jnp.zeros((HEADS, D), F32)
    for kj in range(WIN):
        one = entries[kj * 128 : (kj + 1) * 128]
        for part in three_parts(by_head[:, kj, :]):
            out = out + dot(part, one)
    return out


def spans():
    return [slice(w * PAD, (w + 1) * PAD) for w in range(WINDOWS)]


def forward_stage(s, r):
    rows = pl.ds(pl.multiple_of(s * STRIP, 16), STRIP)
    slot = lax.rem(s, 2)
    tokens = dot(r.gather[...], raster_rows(r.image, r.halo, 0, s))
    r.tokens_out[...] = tokens.astype(BF16)
    yield
    r.cot_all[rows] = dot(r.gather[...], raster_rows(r.cot, r.halo, SHIFT, s)).astype(BF16)
    yield
    normal_one, _ = normalize(tokens)
    first_low = (normal_one * r.gain_one[...] + r.bias_one[...]).astype(BF16)
    r.first_all[rows, :D] = first_low
    yield
    query = dot(first_low, r.w_qkv[:, :D]) + r.b_query[...]
    key = dot(first_low, r.w_qkv[:, D : 2 * D])
    value = dot(first_low, r.w_qkv[:, 2 * D :]) + r.b_value[...]
    yield
    key_labels = r.lane_labels[s].T
    logits = []
    for w, span in enumerate(spans()):
        query_low = pad_rows(query[span]).astype(BF16)
        key_low = pad_rows(key[span]).astype(BF16)
        value_low = pad_rows(value[span]).astype(BF16)
        r.qkv_win[slot, w, :, :D] = query_low
        r.qkv_win[slot, w, :, D : 2 * D] = key_low
        r.qkv_win[slot, w, :, 2 * D :] = value_low
        blocks = head_blocks(query_low, r.mask)
        logits.append(
            [dot_nt(key_low[:, 128 * g : 128 * g + 128], blocks[g])[:PAD] for g in range(2)]
        )
        yield
    turned = []
    for w in range(WINDOWS):
        same = key_labels[:PAD, w : w + 1] == r.lane_labels[s, w : w + 1, :]
        turned.append([])
        for pair in range(HEADS // 2):
            cols = slice(128 * pair, 128 * pair + 128)
            part = logits[w][pair // 2][:, 128 * (pair % 2) : 128 * (pair % 2) + 128]
            part = jnp.where(same, part * (SCALE * LOG2E) + r.bias_t[:, cols], neg)
            powers = jnp.exp2(part - jnp.max(part, 0, keepdims=True))
            attend = powers * (1.0 / jnp.sum(powers, 0, keepdims=True))
            attend_low = pad_rows(attend).astype(BF16)
            r.attend_win[slot, w, :, cols] = attend_low
            turned[w].append(turn_pair(attend_low))
        yield
    mixed_parts = []
    for w in range(WINDOWS):
        blocks = head_blocks(r.qkv_win[slot, w, :, 2 * D :], r.mask)
        mixed_parts.append(
            jnp.concatenate(
                [
                    dot(jnp.concatenate(turned[w][2 * g : 2 * g + 2], 1), blocks[g])[:PAD]
                    for g in range(2)
                ],
                1,
            )
        )
        yield
    mixed_low = jnp.concatenate(mixed_parts, 0).astype(BF16)
    r.mixed_all[rows] = mixed_low
    resid = tokens + dot(mixed_low, r.w_proj[...]) + r.b_proj[...]
    r.resid_win[slot] = resid
    yield


def backward_stage(s, r):
    rows = pl.ds(pl.multiple_of(s * STRIP, 16), STRIP)
    slot = lax.rem(s, 2)
    sums = r.sums
    resid = r.resid_win[slot]
    r.resid_out[...] = resid
    normal_two, recip_two = normalize(resid)
    second_low = (normal_two * r.gain_two[...] + r.bias_two[...]).astype(BF16)
    r.second_all[rows, :D] = second_low
    yield
    cot_low = r.cot_all[rows]
    d_second = jnp.zeros((STRIP, D), F32)
    for n in range(MLP // D):
        cols = slice(n * D, (n + 1) * D)
        inner = dot(second_low, r.w_up[:, cols]) + r.b_up[:, cols]
        cumulative = 0.5 * lax.erf(inner * 0.7071067811865476) + 0.5
        active_low = (inner * cumulative).astype(BF16)
        r.active_all[rows, cols] = active_low
        r.active_out[:, cols] = active_low
        yield
        gauss = jnp.exp2(inner * inner * (-0.5 * LOG2E))
        slope = cumulative + inner * gauss * 0.3989422804014327
        d_inner = (dot_nt(cot_low, r.w_down[cols]) * slope).astype(BF16)
        r.d_inner_all[rows, cols] = d_inner
        yield
        d_second = d_second + dot_nt(d_inner, r.w_up[:, cols])
        yield
    cot_f32 = cot_low.astype(F32)
    d_resid = cot_f32 + norm_backward(d_second, normal_two, recip_two, r.gain_two[...])
    d_branch = d_resid.astype(BF16)
    r.d_branch_all[rows] = d_branch
    r.d_resid_out[...] = d_resid
    yield
    d_mixed = dot_nt(d_branch, r.w_proj[...])
    yield
    sums[0:1] += col_sum(d_second * normal_two)
    sums[1:2] += col_sum(d_second)
    sums[2:3] += col_sum(d_resid)
    sums[3:4] += col_sum(cot_f32)
    yield
    mixed_blocks = []
    d_attends = []
    for w, span in enumerate(spans()):
        blocks = head_blocks(pad_rows(d_mixed[span]).astype(BF16), r.mask)
        mixed_blocks.append(blocks)
        value_low = r.qkv_win[slot, w, :, 2 * D :]
        d_attends.append(
            [dot_nt(value_low[:, 128 * g : 128 * g + 128], blocks[g])[:PAD] for g in range(2)]
        )
        yield
    d_logits = []
    turned = []
    for w in range(WINDOWS):
        d_logits.append([])
        turned.append([])
        for pair in range(HEADS // 2):
            cols = slice(128 * pair, 128 * pair + 128)
            part = d_attends[w][pair // 2][:, 128 * (pair % 2) : 128 * (pair % 2) + 128]
            attend = r.attend_win[slot, w, :, cols].astype(F32)[:PAD]
            cross = jnp.sum(part * attend, 0, keepdims=True)
            part = attend * (part - cross)
            r.logit_sums[:, cols] += part
            low = pad_rows(part).astype(BF16)
            d_logits[w].append(low)
            turned[w].append(turn_pair(low))
        yield
    parts = []
    for w in range(WINDOWS):
        query_blocks = head_blocks(r.qkv_win[slot, w, :, :D], r.mask)
        key_blocks = head_blocks(r.qkv_win[slot, w, :, D : 2 * D], r.mask)
        d_query, d_key, d_value = [], [], []
        for g in range(2):
            two = slice(2 * g, 2 * g + 2)
            attend_low = r.attend_win[slot, w, :, 256 * g : 256 * g + 256]
            d_value.append(dot(attend_low, mixed_blocks[w][g])[:PAD])
            d_key.append(dot(jnp.concatenate(d_logits[w][two], 1), query_blocks[g])[:PAD] * SCALE)
            d_query.append(dot(jnp.concatenate(turned[w][two], 1), key_blocks[g])[:PAD] * SCALE)
        parts.append(jnp.concatenate(d_query + d_key + d_value, 1))
        yield
    d_qkv = jnp.concatenate(parts, 0).astype(BF16)
    r.d_qkv_all[rows] = d_qkv
    r.d_qkv_out[...] = d_qkv
    yield


def run(*stages):
    order = []
    for n, stage in enumerate(stages):
        count = PIECES[stage.__name__]
        order += [((piece + 0.5) / count * (0.5 if n else 1.0), n) for piece in range(count)]
    for _, n in sorted(order):
        next(stages[n])
    for stage in stages:
        assert next(stage, None) is None


PIECES = {"forward_stage": 5 + 3 * WINDOWS, "backward_stage": 1 + 3 * (MLP // D) + 3 + 3 * WINDOWS + 1}


def down_rows(n):
    return DOWN[n // 2] + (n % 2) * D


def finish(r):
    core = lax.rem(lax.axis_index("dp"), 2)
    grads = r.grads

    def put(start, rows):
        grads[start : start + rows.shape[0]] = rows
        r.grads_low[start : start + rows.shape[0]] = rows.astype(BF16)

    def sends(n, start, count):
        half, at = divmod(start, HALF)
        span = pl.ds(at, count)
        keep = pltpu.make_async_copy(grads.at[pl.ds(start, count)], r.keep.at[span], r.sems.at[n])
        send = pltpu.make_async_copy(r.grads_low.at[pl.ds(start, count)], r.send.at[span], r.sems.at[n])
        return half, keep, send

    def begin(half, keep, send):
        @pl.when(core == half)
        def _():
            keep.start()

        @pl.when(core != half)
        def _():
            send.start()

    def end(half, keep, send):
        @pl.when(core == half)
        def _():
            keep.wait()

        @pl.when(core != half)
        def _():
            send.wait()

    small = SMALL_TWO
    put(small, table_gradient(r.logit_sums, r.entries, r.by_head))
    product = dot_tn(r.first_all[:, : D + 8], r.d_qkv_all[...])
    sums = product[D : D + 8]
    for n in range(3):
        put(QKV + n * D, product[:D, n * D : (n + 1) * D])
    bias_grad = jnp.zeros((8, D), F32)
    for part in three_parts(sums):
        bias_grad = bias_grad + dot_nt(part, r.w_qkv[...])
    cross = jnp.zeros((8, D), F32)
    for part in three_parts(product[:D] * r.w_qkv[...].astype(F32)):
        cross = cross + dot_nt(jnp.ones((8, 3 * D), BF16), part)
    gain_grad = (cross[0:1] - r.bias_one[...] * bias_grad[0:1]) / r.gain_one[...]
    put(
        small + 8,
        jnp.concatenate(
            [sums[0:1, :D], sums[0:1, 2 * D :], gain_grad, bias_grad[0:1], jnp.zeros((20, D), F32)], 0
        ),
    )
    put(PROJ, dot_tn(r.mixed_all[...], r.d_branch_all[...]))
    product = dot_tn(r.second_all[:, : D + 8], r.d_inner_all[...])
    for n in range(MLP // D):
        put(UP + n * D, product[:D, n * D : (n + 1) * D])
    ups = [product[D : D + 1, n * D : (n + 1) * D] for n in range(MLP // D)]
    put(SMALL_ONE, jnp.concatenate([r.sums[0:4]] + ups + [jnp.zeros((24, D), F32)], 0))
    copies = [sends(0, UP, MLP), sends(1, SMALL_ONE, 32), sends(2, PROJ, 2 * HALF - PROJ)]
    for copy in copies:
        begin(*copy)
    product = dot_tn(r.cot_all[...], r.active_all[...])
    for n in range(MLP // D):
        put(down_rows(n), product[:, n * D : (n + 1) * D])
    later = [sends(3, DOWN[0], 2 * D), sends(4, DOWN[1], 2 * D)]
    for copy in later:
        begin(*copy)
    for copy in copies + later:
        end(*copy)


class Refs:
    def __init__(self, names, refs):
        self.__dict__.update(zip(names, refs))


NAMES = [
    "image", "cot", "halo", "regions", "regions_halo", "spread", "spread_rows", "gather", "mask", "entries", "table",
    "gain_one", "bias_one", "w_qkv", "b_query", "b_value", "w_proj", "b_proj", "gain_two", "bias_two", "w_up", "b_up",
    "w_down", "keep", "send", "tokens_out", "resid_out", "active_out", "d_resid_out", "d_qkv_out",
    "lane_labels", "by_head", "bias_t", "logit_sums", "qkv_win", "attend_win", "resid_win", "sums",
    "first_all", "cot_all", "mixed_all", "second_all", "active_all", "d_inner_all", "d_branch_all", "d_qkv_all",
    "grads", "grads_low", "sems",
]


def put_labels(r, n, part):
    row = jnp.sum(part * r.spread_rows[...], 0, keepdims=True)
    windows = [row[:, 128 * w : 128 * w + 128] for w in range(WINDOWS)]
    r.lane_labels[n] = jnp.concatenate(windows + [jnp.zeros((2, 128), F32)], 0)


def grads_kernel(*refs):
    r = Refs(NAMES, refs)
    s = pl.program_id(0)

    @pl.when(s == 0)
    def _():
        own = dot(r.regions[...].astype(F32).astype(BF16), r.spread[...])
        for n in range(STRIPS - 1):
            put_labels(r, n, own[n * WIN + SHIFT : (n + 1) * WIN + SHIFT])
        below = dot(r.regions_halo[...], r.spread[...])
        put_labels(r, STRIPS - 1, jnp.concatenate([own[COLS - (WIN - SHIFT) :], below], 0))
        build_bias(r.table[...], r.entries, r.by_head, r.bias_t)
        r.logit_sums[...] = jnp.zeros_like(r.logit_sums)
        one = (lane_ids((TOTAL, 128)) == 0).astype(F32).astype(BF16)
        r.first_all[:, D:] = one
        r.second_all[:, D:] = one
        r.sums[...] = jnp.zeros_like(r.sums)
        run(forward_stage(s, r))

    @pl.when((s > 0) & (s < STRIPS))
    def _():
        run(backward_stage(s - 1, r), forward_stage(s, r))

    @pl.when(s == STRIPS)
    def _():
        run(backward_stage(s - 1, r))
        finish(r)


def output_strip(active, resid, w_down, b_down, scatter):
    result = resid[...] + b_down[...] + dot(active[...], w_down[...])
    return dot(scatter[...], result.astype(BF16)).astype(BF16)


def image_strip(d_qkv, d_resid, tokens, w_qkv, gain, scatter):
    normal, recip_dev = normalize(tokens[...].astype(F32))
    d_first = dot_nt(d_qkv[...], w_qkv[...])
    grad = d_resid[...] + norm_backward(d_first, normal, recip_dev, gain[...])
    return dot(scatter[...], grad.astype(BF16)).astype(BF16)


there = pl.BlockSpec(memory_space=pl.ANY)


def whole(shape):
    return pl.BlockSpec(shape, lambda s: (0,) * len(shape))


def strips(shape):
    return pl.BlockSpec(shape, lambda s: (s,) + (0,) * (len(shape) - 1))


def struct(shape, dtype):
    return jax.ShapeDtypeStruct(shape, dtype)


def params(mebibytes):
    return pltpu.CompilerParams(
        vmem_limit_bytes=mebibytes * 1024 * 1024, dimension_semantics=("arbitrary",)
    )


def pack_kernel(image, cot, regions, rows, labels):
    rows[0:SHIFT] = image[...]
    rows[SHIFT:] = cot[...]
    labels[...] = regions[0:SHIFT].astype(F32).astype(BF16)


def pack_first_rows(image, cot, regions):
    return pl.pallas_call(
        pack_kernel,
        grid=(1,),
        in_specs=[whole((SHIFT, COLS, D)), whole((SHIFT, COLS, D)), whole(regions.shape)],
        out_specs=[whole((2 * SHIFT, COLS, D)), whole((SHIFT, COLS))],
        out_shape=[pltpu.VMEM((2 * SHIFT, COLS, D), BF16), pltpu.VMEM((SHIFT, COLS), BF16)],
        compiler_params=params(62),
        name="pack_first_rows",
    )(image, cot, regions)


def run_grads(*args):
    early = lambda s: (jnp.minimum(s, STRIPS - 1), 0)
    late = lambda s: (jnp.maximum(s - 1, 0), 0)
    return pl.pallas_call(
        grads_kernel,
        grid=(STRIPS + 1,),
        in_specs=[whole(a.shape) for a in args],
        out_specs=[
            pl.BlockSpec(memory_space=pl.ANY),
            pl.BlockSpec(memory_space=pl.ANY),
            pl.BlockSpec((STRIP, D), early),
            pl.BlockSpec((STRIP, D), late),
            pl.BlockSpec((STRIP, MLP), late),
            pl.BlockSpec((STRIP, D), late),
            pl.BlockSpec((STRIP, 3 * D), late),
        ],
        out_shape=[
            pltpu.VMEM((HALF, D), F32),
            pltpu.VMEM((HALF, D), BF16),
            struct((TOTAL, D), BF16),
            struct((TOTAL, D), F32),
            struct((TOTAL, MLP), BF16),
            struct((TOTAL, D), F32),
            struct((TOTAL, 3 * D), BF16),
        ],
        scratch_shapes=[
            pltpu.VMEM((STRIPS, 8, 128), F32),
            pltpu.VMEM((HEADS, 8, 128), F32),
            pltpu.VMEM((PAD, HEADS * LANES), F32),
            pltpu.VMEM((PAD, HEADS * LANES), F32),
            pltpu.VMEM((2, WINDOWS, LANES, 3 * D), BF16),
            pltpu.VMEM((2, WINDOWS, LANES, HEADS * LANES), BF16),
            pltpu.VMEM((2, STRIP, D), F32),
            pltpu.VMEM((8, D), F32),
            pltpu.VMEM((TOTAL, D + 128), BF16),
            pltpu.VMEM((TOTAL, D), BF16),
            pltpu.VMEM((TOTAL, D), BF16),
            pltpu.VMEM((TOTAL, D + 128), BF16),
            pltpu.VMEM((TOTAL, MLP), BF16),
            pltpu.VMEM((TOTAL, MLP), BF16),
            pltpu.VMEM((TOTAL, D), BF16),
            pltpu.VMEM((TOTAL, 3 * D), BF16),
            pltpu.VMEM((2 * HALF, D), F32),
            pltpu.VMEM((2 * HALF, D), BF16),
            pltpu.SemaphoreType.DMA((5,)),
        ],
        compiler_params=params(58),
        cost_estimate=pl.CostEstimate(
            flops=2 * TOTAL * 10 * D * MLP, bytes_accessed=20_000_000, transcendentals=0
        ),
        name="all_gradients",
    )(*args)


def run_field(strip, name, which, blocks, others, field=None, tails=None):
    lower = field is None
    first = FIELD_STEPS if lower else 0
    given = [a for a in (field, tails) if a is not None]
    inputs = len(blocks) + len(others)
    shapes = [struct((COLS, COLS, D), BF16)] + [struct((2, SHIFT, COLS, D), BF16)] * lower

    def kernel(*refs):
        out = refs[inputs + len(given)]
        below = refs[inputs + len(given) + 1] if lower else None
        put_rows(strip(*refs[:inputs]), first, which, out, below, *refs[-2:])

    return pl.pallas_call(
        kernel,
        grid=(FIELD_STEPS,),
        in_specs=[pl.BlockSpec((STRIP, a.shape[1]), lambda t: (first + t, 0)) for a in blocks]
        + [whole(a.shape) for a in others]
        + [there] * len(given),
        out_specs=[there] * len(shapes),
        out_shape=shapes,
        scratch_shapes=[pltpu.VMEM((2, WIN, COLS, D), BF16), pltpu.SemaphoreType.DMA((3,))],
        input_output_aliases={inputs: 1 if lower else 0} if given else {},
        compiler_params=params(60),
        cost_estimate=pl.CostEstimate(
            flops=2 * TOTAL * 4 * D * D, bytes_accessed=9_000_000, transcendentals=0
        ),
        name=name,
    )(*blocks, *others, *given)


def unpack_half(half, rows, w_up, w_down, w_proj, w_qkv, stage, sems):
    def down(first):
        for n in range(2):
            stage[n * D : (n + 1) * D, :D] = rows[first + n * D : first + (n + 1) * D].astype(F32).T
        at = pl.ds(half * 2 * D, 2 * D)
        return pltpu.make_async_copy(stage.at[pl.ds(0, 2 * D), pl.ds(0, D)], w_down.at[at], sems.at[0])

    def wide(out, first, count, at, sem):
        for n in range(count):
            part = rows[first + n * D : first + (n + 1) * D].astype(F32)
            stage[at : at + D, n * D : (n + 1) * D] = part
        return pltpu.make_async_copy(stage.at[pl.ds(at, D), pl.ds(0, count * D)], out, sems.at[sem])

    copies = []
    if half == 0:
        copies.append(wide(w_up, UP, MLP // D, 2 * D, 1))
        copies[-1].start()
        copies.append(down(DOWN[0]))
        copies[-1].start()
    else:
        copies.append(wide(w_qkv, QKV - HALF, 3, 2 * D, 1))
        copies[-1].start()
        copies.append(wide(w_proj, PROJ - HALF, 1, 3 * D, 2))
        copies[-1].start()
        copies.append(down(DOWN[1] - HALF))
        copies[-1].start()
    for copy in copies:
        copy.wait()


def unpack_first_kernel(own, *refs):
    core = lax.rem(lax.axis_index("dp"), 2)
    for half in range(2):

        @pl.when(core == half)
        def _():
            unpack_half(half, own, *refs)


def unpack_second_kernel(
    other, own, in_up, in_down, in_proj, in_qkv, w_up, w_down, w_proj, w_qkv,
    gain_one, bias_one, b_query, b_value, table, b_proj, gain_two, bias_two, b_up, b_down, stage, sems,
):
    core = lax.rem(lax.axis_index("dp"), 2)
    for half in range(2):

        @pl.when(core != half)
        def _():
            unpack_half(half, other, w_up, w_down, w_proj, w_qkv, stage, sems)

    small = slice(SMALL_ONE, HALF)
    mine, others = own[small].astype(F32), other[small].astype(F32)
    first = jnp.where(core == 0, mine, others)
    second = jnp.where(core == 0, others, mine)
    for n, out in enumerate((gain_two, bias_two, b_proj, b_down)):
        out[...] = first[n : n + 1]
    for n in range(MLP // D):
        b_up[:, n * D : (n + 1) * D] = first[4 + n : 5 + n]
    table[...] = second[:HEADS, :ENTRIES]
    for n, out in enumerate((b_query, b_value, gain_one, bias_one)):
        out[...] = second[HEADS + n : HEADS + n + 1]


LARGE = ((D, MLP), (MLP, D), (D, D), (D, 3 * D))
UNPACK_SCRATCH = [pltpu.VMEM((4 * D, MLP), F32), pltpu.SemaphoreType.DMA((3,))]
def unpack_first(own):
    return pl.pallas_call(
        unpack_first_kernel,
        grid=(1,),
        in_specs=[whole(own.shape)],
        out_specs=[there] * 4,
        out_shape=[struct(shape, F32) for shape in LARGE],
        scratch_shapes=UNPACK_SCRATCH,
        compiler_params=params(24),
        cost_estimate=pl.CostEstimate(flops=0, bytes_accessed=2_400_000, transcendentals=0),
        name="unpack_own_half",
    )(own)


def unpack_second(other, own, large):
    one, four = (1, D), (1, MLP)
    shapes = [one, one, one, one, (HEADS, ENTRIES), one, one, one, four, one]
    out = pl.pallas_call(
        unpack_second_kernel,
        grid=(1,),
        in_specs=[whole(other.shape), whole(own.shape)] + [there] * 4,
        out_specs=[there] * 4 + [whole(shape) for shape in shapes],
        out_shape=[struct(shape, F32) for shape in LARGE] + [struct(shape, F32) for shape in shapes],
        scratch_shapes=UNPACK_SCRATCH,
        input_output_aliases={2: 0, 3: 1, 4: 2, 5: 3},
        compiler_params=params(24),
        name="unpack_other_half",
    )(other, own, *large)
    w_up, w_down, w_proj, w_qkv = out[:4]
    gain_one, bias_one, b_query, b_value, table, b_proj, gain_two, bias_two, b_up, b_down = out[4:]
    return (
        gain_one[0], bias_one[0], w_qkv, b_query[0], b_value[0], table.T, w_proj, b_proj[0],
        gain_two[0], bias_two[0], w_up, b_up[0], w_down, b_down[0],
    )


def coords(index):
    dp, space = divmod(index, 32)
    return {"c": dp % 2, "y": dp // 2 + 2 * ((space // 4) % 2), "x": space % 4, "z": space // 8}


def index_of(c, y, x, z):
    return ((y % 2) * 2 + c) * 32 + z * 8 + (y // 2) * 4 + x


DISTANCES = (2, 1, 3)
STAGES = (("y", "x"), ("x", "z"), ("z", "y"))


def other_core():
    return [(i, index_of(**(coords(i) | {"c": 1 - i // 32 % 2}))) for i in range(128)]


def around(stage, distance):
    out = []
    for i in range(128):
        at = coords(i)
        axis = stage[at["c"]]
        out.append((i, index_of(**(at | {axis: (at[axis] + distance) % 4}))))
    return out


def take(rows, start, count):
    return lax.dynamic_slice_in_dim(rows, start, count, 0)


def sum_everywhere(mine, got_core, at, pieces):
    made = {}
    left = list(pieces)

    def exchange(stage, sends, own):
        nonlocal made
        ahead, beside = left.pop(0)
        early = ahead(made)
        got = [lax.ppermute(sends[d], AXES, around(stage, d)) for d in DISTANCES]
        made, own = lax.optimization_barrier((made, own))
        made = beside(made)
        got, made, early, own = lax.optimization_barrier((got, made, early, own))
        made = made | early
        return dict(zip(DISTANCES, got)), own

    def place(stage):
        return jnp.where(at["c"] == 0, at[stage[0]], at[stage[1]])

    stage = STAGES[0]
    here = place(stage)
    count = mine.shape[0] // 4

    def part(which):
        start = which * count
        return take(mine, start, count) + take(got_core, start, count).astype(F32)

    sends = {d: part((here + d) % 4).astype(BF16) for d in DISTANCES}
    got, rows = exchange(stage, sends, part(here))
    for d in DISTANCES:
        rows = rows + got[d].astype(F32)
    low = rows.astype(BF16)
    for stage in STAGES[1:]:
        got, low = exchange(stage, {d: low for d in DISTANCES}, low)
        pairs = low.astype(F32) + got[2].astype(F32), got[1].astype(F32) + got[3].astype(F32)
        low = (pairs[0] + pairs[1]).astype(BF16)
    got, low = exchange(STAGES[0], {d: low for d in DISTANCES}, low)
    whole_half = jnp.zeros((4 * count, D), BF16)
    for d, rows in [(0, low), *got.items()]:
        whole_half = lax.dynamic_update_slice(whole_half, rows, ((here - d) % 4 * count, 0))
    return whole_half, made


def body(
    image_in, cotangent, regions, first_gain, first_bias, qkv_weight, query_bias, value_bias,
    position_table, proj_weight, proj_bias, second_gain, second_bias, up_weight, up_bias,
    down_weight, down_bias,
):
    many = lax.axis_size("dp") * lax.axis_size("space") == 128
    me = lax.axis_index(AXES)
    at = coords(me)
    first_rows = pack_first_rows(image_in, cotangent, regions)
    halo, regions_halo = from_behind(first_rows, "space", -1)
    gather = gather_matrix()
    spread, spread_rows = label_matrices()
    entries = jnp.asarray(entry_matrix(), BF16)
    mask = jnp.asarray(head_mask(), BF16)
    scatter = jnp.asarray(gather.T, BF16)
    mine, send, tokens, resid, active, d_resid, d_qkv = run_grads(
        image_in, cotangent, halo, regions, regions_halo,
        jnp.asarray(spread, BF16), jnp.asarray(spread_rows), jnp.asarray(gather, BF16),
        mask, entries, position_table.T, first_gain[None], first_bias[None], qkv_weight, query_bias[None],
        value_bias[None], proj_weight, proj_bias[None], second_gain[None], second_bias[None],
        up_weight, up_bias[None], down_weight,
    )
    if many:
        got = lax.ppermute(send, AXES, other_core())

    def block_output(*given):
        others = (down_weight, down_bias[None], scatter)
        return run_field(output_strip, "block_output", 0, (active, resid), others, *given)

    def image_gradient(*given):
        others = (qkv_weight, first_gain[None], scatter)
        return run_field(image_strip, "image_gradient", 1, (d_qkv, d_resid, tokens), others, *given)

    def lower_out(made):
        field, tails = block_output()
        return {"out": field, "tails": tails}

    def lower_image(made):
        field, tails = image_gradient(None, made["tails"])
        return made | {"image": field, "tails": tails}

    def upper_out(made):
        return made | {"out": block_output(made["out"])[0]}

    def return_rows(made):
        return {"returned": from_behind(made["tails"], "space", 1)}

    def upper_image(made):
        return made | {"image": image_gradient(made["image"])[0]}

    def nothing(made):
        return {}

    pieces = [(nothing, lower_out), (nothing, lower_image), (nothing, upper_out), (return_rows, upper_image)]
    if many:
        own, made = sum_everywhere(mine, got, at, pieces)
        other = lax.ppermute(own, AXES, other_core())
        large = unpack_first(own)
        other, large = lax.optimization_barrier((other, large))
    else:
        made = {}
        for ahead, beside in pieces:
            made = beside(made) | ahead(made)
        own, other = mine.astype(BF16), send
        large = unpack_first(own)
    block_out = lax.dynamic_update_slice(made["out"], made["returned"][0], (0, 0, 0))
    image_grad = lax.dynamic_update_slice(made["image"], made["returned"][1], (0, 0, 0))
    return (block_out, image_grad) + unpack_second(other, own, large)


def solution(mesh):
    tokens = P(AXES, None, None)
    return jax.shard_map(
        body,
        mesh=mesh,
        in_specs=(tokens, tokens, P(AXES, None)) + (P(),) * 14,
        out_specs=(tokens, tokens) + (P(),) * 14,
        check_vma=False,
    )
```

```python
import functools
import math

import jax
import jax.numpy as jnp
import numpy as np
from jax import lax
from jax.experimental import pallas as pl
from jax.experimental.pallas import tpu as pltpu
from jax.sharding import PartitionSpec as P

WIN = 7
SHIFT = 3
HEADS = 8
TOKENS = WIN * WIN
PAD = 56
LANES = 64
ENTRIES = (2 * WIN - 1) * (2 * WIN - 1)
COLS = 42
WINDOWS = COLS // WIN
STRIP = WINDOWS * PAD
STRIPS = COLS // WIN
SENT = 5
FIELD_STEPS = STRIPS // 2
TOTAL = STRIPS * STRIP
ROW = 48
D = 256
MLP = 1024
BF16 = jnp.bfloat16
F32 = jnp.float32
epsilon = 1e-05
neg = -1000000000.0
AXES = ("dp", "space")
SCALE = 1.0 / math.sqrt(D // HEADS)
LOG2E = 1.4426950408889634
UP = 0
DOWN = (MLP, MLP + 2 * D + 32)
SMALL_ONE = MLP + 2 * D
HALF = SMALL_ONE + 32
PROJ = HALF + 2 * D
QKV = PROJ + D
SMALL_TWO = QKV + 3 * D
assert SMALL_TWO + 32 == 2 * HALF


def from_behind(block, axis, distance):
    devices = range(lax.axis_size(axis))
    route = [((i - distance) % len(devices), i) for i in devices]
    return lax.ppermute(block, axis, route)


def place(i, j):
    return 8 * i + j


def gather_matrix():
    out = np.zeros((STRIP, WIN * ROW), np.float32)
    for w in range(WINDOWS):
        for i in range(WIN):
            for j in range(WIN):
                out[w * PAD + place(i, j), i * ROW + (w * WIN + j + SHIFT) % COLS] = 1.0
    return out


def label_matrices():
    spread = np.zeros((COLS, WINDOWS * 2 * LANES), np.float32)
    rows = np.zeros((WIN, WINDOWS * 2 * LANES), np.float32)
    for w in range(WINDOWS):
        for copy in range(2):
            for i in range(WIN):
                for j in range(WIN):
                    col = (w * 2 + copy) * LANES + place(i, j)
                    spread[(w * WIN + j + SHIFT) % COLS, col] = 1.0
                    rows[i, col] = 1.0
    return spread, rows


def entry_matrix():
    out = np.zeros((WIN * 128, D), np.float32)
    for kj in range(WIN):
        for di in range(1 - WIN, WIN):
            for qj in range(WIN):
                entry = (di + WIN - 1) * (2 * WIN - 1) + qj - kj + WIN - 1
                out[kj * 128 + (8 * di + qj) % 128, entry] = 1.0
    return out


def head_mask():
    return (np.arange(4 * LANES)[:, None] // LANES == np.arange(128)[None] // 32).astype(np.float32)


def dot(a, b):
    return jnp.dot(a, b, preferred_element_type=F32)


def dot_nt(a, b):
    return lax.dot_general(a, b, (((1,), (1,)), ((), ())), preferred_element_type=F32)


def dot_tn(a, b):
    return lax.dot_general(a, b, (((0,), (0,)), ((), ())), preferred_element_type=F32)


def normalize(values):
    center = values - jnp.mean(values, -1, keepdims=True)
    variance = jnp.mean(center * center, -1, keepdims=True)
    recip_dev = lax.rsqrt(variance + epsilon)
    return center * recip_dev, recip_dev


def norm_backward(upstream, normal_part, recip_dev, gain):
    scaled = upstream * gain
    inner_mean = jnp.mean(scaled, -1, keepdims=True)
    cross_mean = jnp.mean(scaled * normal_part, -1, keepdims=True)
    return recip_dev * (scaled - inner_mean - normal_part * cross_mean)


def col_sum(values):
    return jnp.sum(values, 0, keepdims=True)


def raster_rows(ref, halo, first, s):
    last = s == STRIPS - 1
    blank = jnp.zeros((ROW - COLS, D), BF16)
    rows = []
    for i in range(WIN):
        g = s * WIN + i + SHIFT
        if i < WIN - SHIFT:
            value = ref[g]
        else:
            value = jnp.where(
                last, halo[first + i - (WIN - SHIFT)], ref[jnp.minimum(g, COLS - 1)]
            )
        rows += [value, blank]
    return jnp.concatenate(rows, 0)


def put_rows(raster, first, which, out, tails, stage, sems):
    t = pl.program_id(0)
    slot = lax.rem(t, 2)

    def whole_strip(n):
        return pltpu.make_async_copy(
            stage.at[lax.rem(n, 2)], out.at[pl.ds((first + n) * WIN + SHIFT, WIN)], sems.at[lax.rem(n, 2)]
        )

    @pl.when(t >= 2)
    def _():
        whole_strip(t - 2).wait()

    for i in range(WIN):
        stage[slot, i] = raster[i * ROW : i * ROW + COLS]

    @pl.when(first + t < STRIPS - 1)
    def _():
        whole_strip(t).start()

    @pl.when(t == FIELD_STEPS - 1)
    def _():
        if tails is None:
            whole_strip(t - 1).wait()
            whole_strip(t).wait()
        else:
            own = pltpu.make_async_copy(
                stage.at[slot, 0 : WIN - SHIFT], out.at[COLS - (WIN - SHIFT) : COLS], sems.at[slot]
            )
            below = pltpu.make_async_copy(stage.at[slot, WIN - SENT : WIN], tails.at[which], sems.at[2])
            own.start()
            below.start()
            whole_strip(t - 1).wait()
            own.wait()
            below.wait()


def pad_rows(values):
    return jnp.concatenate([values, jnp.zeros((LANES - PAD,) + values.shape[1:], values.dtype)], 0)


def head_blocks(low, mask):
    return [jnp.concatenate([low[:, g : g + 128]] * 4, 0) * mask[...] for g in (0, 128)]


def turn_pair(values):
    turned = values.T
    return jnp.concatenate([turned[:LANES], turned[LANES:]], 1)


def three_parts(values):
    high = values.astype(BF16)
    rest = values - high.astype(F32)
    middle = rest.astype(BF16)
    return high, middle, (rest - middle.astype(F32)).astype(BF16)


def lane_ids(shape):
    return lax.broadcasted_iota(jnp.int32, shape, 1)


def build_bias(table, entries, by_head, bias_t):
    parts = three_parts(table * LOG2E)
    for kj in range(WIN):
        one = entries[kj * 128 : (kj + 1) * 128, :ENTRIES]
        by_head[:, kj, :] = dot_nt(parts[0], one) + dot_nt(parts[1], one) + dot_nt(parts[2], one)
    by_head[:, WIN, :] = jnp.full((HEADS, 128), neg, F32)
    lane = lane_ids((8, 128))
    for pair in range(HEADS // 2):
        for ki in range(WIN):
            first = pltpu.roll(by_head[2 * pair], 8 * ki, 1)
            second = pltpu.roll(by_head[2 * pair + 1], (8 * ki + LANES) % 128, 1)
            bias_t[8 * ki : 8 * ki + 8, 128 * pair : 128 * pair + 128] = jnp.where(
                lane < LANES, first, second
            )


def table_gradient(logit_sums, entries, by_head):
    lane = lane_ids((8, 128))
    for pair in range(HEADS // 2):
        for half in range(2):
            total = jnp.zeros((8, 128), F32)
            for ki in range(WIN):
                block = logit_sums[8 * ki : 8 * ki + 8, 128 * pair : 128 * pair + 128]
                own = jnp.where((lane < LANES) == (half == 0), block, 0.0)
                total = total + pltpu.roll(own, (128 - 8 * ki - LANES * half) % 128, 1)
            by_head[2 * pair + half] = total
    out = jnp.zeros((HEADS, D), F32)
    for kj in range(WIN):
        one = entries[kj * 128 : (kj + 1) * 128]
        for part in three_parts(by_head[:, kj, :]):
            out = out + dot(part, one)
    return out


def spans():
    return [slice(w * PAD, (w + 1) * PAD) for w in range(WINDOWS)]


def forward_stage(s, r):
    rows = pl.ds(pl.multiple_of(s * STRIP, 16), STRIP)
    slot = lax.rem(s, 2)
    tokens = dot(r.gather[...], raster_rows(r.image, r.halo, 0, s))
    r.tokens_out[...] = tokens.astype(BF16)
    yield
    r.cot_all[rows] = dot(r.gather[...], raster_rows(r.cot, r.halo, SHIFT, s)).astype(BF16)
    yield
    normal_one, _ = normalize(tokens)
    first_low = (normal_one * r.gain_one[...] + r.bias_one[...]).astype(BF16)
    r.first_all[rows, :D] = first_low
    yield
    query = dot(first_low, r.w_qkv[:, :D]) + r.b_query[...]
    key = dot(first_low, r.w_qkv[:, D : 2 * D])
    value = dot(first_low, r.w_qkv[:, 2 * D :]) + r.b_value[...]
    yield
    key_labels = r.lane_labels[s].T
    logits = []
    for w, span in enumerate(spans()):
        query_low = pad_rows(query[span]).astype(BF16)
        key_low = pad_rows(key[span]).astype(BF16)
        value_low = pad_rows(value[span]).astype(BF16)
        r.qkv_win[slot, w, :, :D] = query_low
        r.qkv_win[slot, w, :, D : 2 * D] = key_low
        r.qkv_win[slot, w, :, 2 * D :] = value_low
        blocks = head_blocks(query_low, r.mask)
        logits.append(
            [dot_nt(key_low[:, 128 * g : 128 * g + 128], blocks[g])[:PAD] for g in range(2)]
        )
        yield
    turned = []
    for w in range(WINDOWS):
        same = key_labels[:PAD, w : w + 1] == r.lane_labels[s, w : w + 1, :]
        turned.append([])
        for pair in range(HEADS // 2):
            cols = slice(128 * pair, 128 * pair + 128)
            part = logits[w][pair // 2][:, 128 * (pair % 2) : 128 * (pair % 2) + 128]
            part = jnp.where(same, part * (SCALE * LOG2E) + r.bias_t[:, cols], neg)
            powers = jnp.exp2(part - jnp.max(part, 0, keepdims=True))
            attend = powers * (1.0 / jnp.sum(powers, 0, keepdims=True))
            attend_low = pad_rows(attend).astype(BF16)
            r.attend_win[slot, w, :, cols] = attend_low
            turned[w].append(turn_pair(attend_low))
        yield
    mixed_parts = []
    for w in range(WINDOWS):
        blocks = head_blocks(r.qkv_win[slot, w, :, 2 * D :], r.mask)
        mixed_parts.append(
            jnp.concatenate(
                [
                    dot(jnp.concatenate(turned[w][2 * g : 2 * g + 2], 1), blocks[g])[:PAD]
                    for g in range(2)
                ],
                1,
            )
        )
        yield
    mixed_low = jnp.concatenate(mixed_parts, 0).astype(BF16)
    r.mixed_all[rows] = mixed_low
    resid = tokens + dot(mixed_low, r.w_proj[...]) + r.b_proj[...]
    r.resid_win[slot] = resid
    yield


def backward_stage(s, r):
    rows = pl.ds(pl.multiple_of(s * STRIP, 16), STRIP)
    slot = lax.rem(s, 2)
    sums = r.sums
    resid = r.resid_win[slot]
    r.resid_out[...] = resid
    normal_two, recip_two = normalize(resid)
    second_low = (normal_two * r.gain_two[...] + r.bias_two[...]).astype(BF16)
    r.second_all[rows, :D] = second_low
    yield
    cot_low = r.cot_all[rows]
    d_second = jnp.zeros((STRIP, D), F32)
    for n in range(MLP // D):
        cols = slice(n * D, (n + 1) * D)
        inner = dot(second_low, r.w_up[:, cols]) + r.b_up[:, cols]
        cumulative = 0.5 * lax.erf(inner * 0.7071067811865476) + 0.5
        active_low = (inner * cumulative).astype(BF16)
        r.active_all[rows, cols] = active_low
        r.active_out[:, cols] = active_low
        yield
        gauss = jnp.exp2(inner * inner * (-0.5 * LOG2E))
        slope = cumulative + inner * gauss * 0.3989422804014327
        d_inner = (dot_nt(cot_low, r.w_down[cols]) * slope).astype(BF16)
        r.d_inner_all[rows, cols] = d_inner
        yield
        d_second = d_second + dot_nt(d_inner, r.w_up[:, cols])
        yield
    cot_f32 = cot_low.astype(F32)
    d_resid = cot_f32 + norm_backward(d_second, normal_two, recip_two, r.gain_two[...])
    d_branch = d_resid.astype(BF16)
    r.d_branch_all[rows] = d_branch
    r.d_resid_out[...] = d_resid
    yield
    d_mixed = dot_nt(d_branch, r.w_proj[...])
    yield
    sums[0:1] += col_sum(d_second * normal_two)
    sums[1:2] += col_sum(d_second)
    sums[2:3] += col_sum(d_resid)
    sums[3:4] += col_sum(cot_f32)
    yield
    mixed_blocks = []
    d_attends = []
    for w, span in enumerate(spans()):
        blocks = head_blocks(pad_rows(d_mixed[span]).astype(BF16), r.mask)
        mixed_blocks.append(blocks)
        value_low = r.qkv_win[slot, w, :, 2 * D :]
        d_attends.append(
            [dot_nt(value_low[:, 128 * g : 128 * g + 128], blocks[g])[:PAD] for g in range(2)]
        )
        yield
    d_logits = []
    turned = []
    for w in range(WINDOWS):
        d_logits.append([])
        turned.append([])
        for pair in range(HEADS // 2):
            cols = slice(128 * pair, 128 * pair + 128)
            part = d_attends[w][pair // 2][:, 128 * (pair % 2) : 128 * (pair % 2) + 128]
            attend = r.attend_win[slot, w, :, cols].astype(F32)[:PAD]
            cross = jnp.sum(part * attend, 0, keepdims=True)
            part = attend * (part - cross)
            r.logit_sums[:, cols] += part
            low = pad_rows(part).astype(BF16)
            d_logits[w].append(low)
            turned[w].append(turn_pair(low))
        yield
    parts = []
    for w in range(WINDOWS):
        query_blocks = head_blocks(r.qkv_win[slot, w, :, :D], r.mask)
        key_blocks = head_blocks(r.qkv_win[slot, w, :, D : 2 * D], r.mask)
        d_query, d_key, d_value = [], [], []
        for g in range(2):
            two = slice(2 * g, 2 * g + 2)
            attend_low = r.attend_win[slot, w, :, 256 * g : 256 * g + 256]
            d_value.append(dot(attend_low, mixed_blocks[w][g])[:PAD])
            d_key.append(dot(jnp.concatenate(d_logits[w][two], 1), query_blocks[g])[:PAD] * SCALE)
            d_query.append(dot(jnp.concatenate(turned[w][two], 1), key_blocks[g])[:PAD] * SCALE)
        parts.append(jnp.concatenate(d_query + d_key + d_value, 1))
        yield
    d_qkv = jnp.concatenate(parts, 0).astype(BF16)
    r.d_qkv_all[rows] = d_qkv
    r.d_qkv_out[...] = d_qkv
    yield


def run(*stages):
    order = []
    for n, stage in enumerate(stages):
        count = PIECES[stage.__name__]
        order += [((piece + 0.5) / count * (0.5 if n else 1.0), n) for piece in range(count)]
    for _, n in sorted(order):
        next(stages[n])
    for stage in stages:
        assert next(stage, None) is None


PIECES = {"forward_stage": 5 + 3 * WINDOWS, "backward_stage": 1 + 3 * (MLP // D) + 3 + 3 * WINDOWS + 1}


def down_rows(n):
    return DOWN[n // 2] + (n % 2) * D


def finish(r):
    core = lax.rem(lax.axis_index("dp"), 2)
    grads = r.grads

    def put(start, rows):
        grads[start : start + rows.shape[0]] = rows
        r.grads_low[start : start + rows.shape[0]] = rows.astype(BF16)

    def sends(n, start, count):
        half, at = divmod(start, HALF)
        span = pl.ds(at, count)
        keep = pltpu.make_async_copy(grads.at[pl.ds(start, count)], r.keep.at[span], r.sems.at[n])
        send = pltpu.make_async_copy(r.grads_low.at[pl.ds(start, count)], r.send.at[span], r.sems.at[n])
        return half, keep, send

    def begin(half, keep, send):
        @pl.when(core == half)
        def _():
            keep.start()

        @pl.when(core != half)
        def _():
            send.start()

    def end(half, keep, send):
        @pl.when(core == half)
        def _():
            keep.wait()

        @pl.when(core != half)
        def _():
            send.wait()

    small = SMALL_TWO
    put(small, table_gradient(r.logit_sums, r.entries, r.by_head))
    product = dot_tn(r.first_all[:, : D + 8], r.d_qkv_all[...])
    sums = product[D : D + 8]
    for n in range(3):
        put(QKV + n * D, product[:D, n * D : (n + 1) * D])
    bias_grad = jnp.zeros((8, D), F32)
    for part in three_parts(sums):
        bias_grad = bias_grad + dot_nt(part, r.w_qkv[...])
    cross = jnp.zeros((8, D), F32)
    for part in three_parts(product[:D] * r.w_qkv[...].astype(F32)):
        cross = cross + dot_nt(jnp.ones((8, 3 * D), BF16), part)
    gain_grad = (cross[0:1] - r.bias_one[...] * bias_grad[0:1]) / r.gain_one[...]
    put(
        small + 8,
        jnp.concatenate(
            [sums[0:1, :D], sums[0:1, 2 * D :], gain_grad, bias_grad[0:1], jnp.zeros((20, D), F32)], 0
        ),
    )
    put(PROJ, dot_tn(r.mixed_all[...], r.d_branch_all[...]))
    product = dot_tn(r.second_all[:, : D + 8], r.d_inner_all[...])
    for n in range(MLP // D):
        put(UP + n * D, product[:D, n * D : (n + 1) * D])
    ups = [product[D : D + 1, n * D : (n + 1) * D] for n in range(MLP // D)]
    put(SMALL_ONE, jnp.concatenate([r.sums[0:4]] + ups + [jnp.zeros((24, D), F32)], 0))
    copies = [sends(0, UP, MLP), sends(1, SMALL_ONE, 32), sends(2, PROJ, 2 * HALF - PROJ)]
    for copy in copies:
        begin(*copy)
    product = dot_tn(r.cot_all[...], r.active_all[...])
    for n in range(MLP // D):
        put(down_rows(n), product[:, n * D : (n + 1) * D])
    later = [sends(3, DOWN[0], 2 * D), sends(4, DOWN[1], 2 * D)]
    for copy in later:
        begin(*copy)
    for copy in copies + later:
        end(*copy)


class Refs:
    def __init__(self, names, refs):
        self.__dict__.update(zip(names, refs))


NAMES = [
    "image", "cot", "halo", "regions", "regions_halo", "spread", "spread_rows", "gather", "mask", "entries", "table",
    "gain_one", "bias_one", "w_qkv", "b_query", "b_value", "w_proj", "b_proj", "gain_two", "bias_two", "w_up", "b_up",
    "w_down", "keep", "send", "tokens_out", "resid_out", "active_out", "d_resid_out", "d_qkv_out",
    "lane_labels", "by_head", "bias_t", "logit_sums", "qkv_win", "attend_win", "resid_win", "sums",
    "first_all", "cot_all", "mixed_all", "second_all", "active_all", "d_inner_all", "d_branch_all", "d_qkv_all",
    "grads", "grads_low", "sems",
]


def put_labels(r, n, part):
    row = jnp.sum(part * r.spread_rows[...], 0, keepdims=True)
    windows = [row[:, 128 * w : 128 * w + 128] for w in range(WINDOWS)]
    r.lane_labels[n] = jnp.concatenate(windows + [jnp.zeros((2, 128), F32)], 0)


def grads_kernel(*refs):
    r = Refs(NAMES, refs)
    s = pl.program_id(0)

    @pl.when(s == 0)
    def _():
        own = dot(r.regions[...].astype(F32).astype(BF16), r.spread[...])
        for n in range(STRIPS - 1):
            put_labels(r, n, own[n * WIN + SHIFT : (n + 1) * WIN + SHIFT])
        below = dot(r.regions_halo[...], r.spread[...])
        put_labels(r, STRIPS - 1, jnp.concatenate([own[COLS - (WIN - SHIFT) :], below], 0))
        build_bias(r.table[...], r.entries, r.by_head, r.bias_t)
        r.logit_sums[...] = jnp.zeros_like(r.logit_sums)
        one = (lane_ids((TOTAL, 128)) == 0).astype(F32).astype(BF16)
        r.first_all[:, D:] = one
        r.second_all[:, D:] = one
        r.sums[...] = jnp.zeros_like(r.sums)
        run(forward_stage(s, r))

    @pl.when((s > 0) & (s < STRIPS))
    def _():
        run(backward_stage(s - 1, r), forward_stage(s, r))

    @pl.when(s == STRIPS)
    def _():
        run(backward_stage(s - 1, r))
        finish(r)


def output_strip(active, resid, w_down, b_down, scatter):
    result = resid[...] + b_down[...] + dot(active[...], w_down[...])
    return dot(scatter[...], result.astype(BF16)).astype(BF16)


def image_strip(d_qkv, d_resid, tokens, w_qkv, gain, scatter):
    normal, recip_dev = normalize(tokens[...].astype(F32))
    d_first = dot_nt(d_qkv[...], w_qkv[...])
    grad = d_resid[...] + norm_backward(d_first, normal, recip_dev, gain[...])
    return dot(scatter[...], grad.astype(BF16)).astype(BF16)


there = pl.BlockSpec(memory_space=pl.ANY)


def whole(shape):
    return pl.BlockSpec(shape, lambda s: (0,) * len(shape))


def strips(shape):
    return pl.BlockSpec(shape, lambda s: (s,) + (0,) * (len(shape) - 1))


def struct(shape, dtype):
    return jax.ShapeDtypeStruct(shape, dtype)


def params(mebibytes):
    return pltpu.CompilerParams(
        vmem_limit_bytes=mebibytes * 1024 * 1024, dimension_semantics=("arbitrary",)
    )


def pack_kernel(image, cot, regions, rows, labels):
    rows[0:SHIFT] = image[...]
    rows[SHIFT:] = cot[...]
    labels[...] = regions[0:SHIFT].astype(F32).astype(BF16)


def pack_first_rows(image, cot, regions):
    return pl.pallas_call(
        pack_kernel,
        grid=(1,),
        in_specs=[whole((SHIFT, COLS, D)), whole((SHIFT, COLS, D)), whole(regions.shape)],
        out_specs=[whole((2 * SHIFT, COLS, D)), whole((SHIFT, COLS))],
        out_shape=[pltpu.VMEM((2 * SHIFT, COLS, D), BF16), pltpu.VMEM((SHIFT, COLS), BF16)],
        compiler_params=params(62),
        name="pack_first_rows",
    )(image, cot, regions)


def run_grads(*args):
    early = lambda s: (jnp.minimum(s, STRIPS - 1), 0)
    late = lambda s: (jnp.maximum(s - 1, 0), 0)
    return pl.pallas_call(
        grads_kernel,
        grid=(STRIPS + 1,),
        in_specs=[whole(a.shape) for a in args],
        out_specs=[
            pl.BlockSpec(memory_space=pl.ANY),
            pl.BlockSpec(memory_space=pl.ANY),
            pl.BlockSpec((STRIP, D), early),
            pl.BlockSpec((STRIP, D), late),
            pl.BlockSpec((STRIP, MLP), late),
            pl.BlockSpec((STRIP, D), late),
            pl.BlockSpec((STRIP, 3 * D), late),
        ],
        out_shape=[
            pltpu.VMEM((HALF, D), F32),
            pltpu.VMEM((HALF, D), BF16),
            pltpu.VMEM((TOTAL, D), BF16),
            pltpu.VMEM((TOTAL, D), F32),
            pltpu.VMEM((TOTAL, MLP), BF16),
            pltpu.VMEM((TOTAL, D), F32),
            pltpu.VMEM((TOTAL, 3 * D), BF16),
        ],
        scratch_shapes=[
            pltpu.VMEM((STRIPS, 8, 128), F32),
            pltpu.VMEM((HEADS, 8, 128), F32),
            pltpu.VMEM((PAD, HEADS * LANES), F32),
            pltpu.VMEM((PAD, HEADS * LANES), F32),
            pltpu.VMEM((2, WINDOWS, LANES, 3 * D), BF16),
            pltpu.VMEM((2, WINDOWS, LANES, HEADS * LANES), BF16),
            pltpu.VMEM((2, STRIP, D), F32),
            pltpu.VMEM((8, D), F32),
            pltpu.VMEM((TOTAL, D + 128), BF16),
            pltpu.VMEM((TOTAL, D), BF16),
            pltpu.VMEM((TOTAL, D), BF16),
            pltpu.VMEM((TOTAL, D + 128), BF16),
            pltpu.VMEM((TOTAL, MLP), BF16),
            pltpu.VMEM((TOTAL, MLP), BF16),
            pltpu.VMEM((TOTAL, D), BF16),
            pltpu.VMEM((TOTAL, 3 * D), BF16),
            pltpu.VMEM((2 * HALF, D), F32),
            pltpu.VMEM((2 * HALF, D), BF16),
            pltpu.SemaphoreType.DMA((5,)),
        ],
        compiler_params=params(48),
        cost_estimate=pl.CostEstimate(
            flops=2 * TOTAL * 10 * D * MLP, bytes_accessed=20_000_000, transcendentals=0
        ),
        name="all_gradients",
    )(*args)


def run_field(strip, name, which, blocks, others, field=None, tails=None):
    lower = field is None
    first = FIELD_STEPS if lower else 0
    given = [a for a in (field, tails) if a is not None]
    inputs = len(blocks) + len(others)
    shapes = [struct((COLS, COLS, D), BF16)] + [struct((2, SENT, COLS, D), BF16)] * lower

    def kernel(*refs):
        out = refs[inputs + len(given)]
        below = refs[inputs + len(given) + 1] if lower else None
        put_rows(strip(*refs[:inputs]), first, which, out, below, *refs[-2:])

    return pl.pallas_call(
        kernel,
        grid=(FIELD_STEPS,),
        in_specs=[pl.BlockSpec((STRIP, a.shape[1]), lambda t: (first + t, 0)) for a in blocks]
        + [whole(a.shape) for a in others]
        + [there] * len(given),
        out_specs=[there] * len(shapes),
        out_shape=shapes,
        scratch_shapes=[pltpu.VMEM((2, WIN, COLS, D), BF16), pltpu.SemaphoreType.DMA((3,))],
        input_output_aliases={inputs: 1 if lower else 0} if given else {},
        compiler_params=params(40),
        cost_estimate=pl.CostEstimate(
            flops=2 * TOTAL * 4 * D * D, bytes_accessed=9_000_000, transcendentals=0
        ),
        name=name,
    )(*blocks, *others, *given)


def unpack_half(half, rows, w_up, w_down, w_proj, w_qkv, stage, sems):
    def down(first):
        for n in range(2):
            stage[n * D : (n + 1) * D, :D] = rows[first + n * D : first + (n + 1) * D].astype(F32).T
        at = pl.ds(half * 2 * D, 2 * D)
        return pltpu.make_async_copy(stage.at[pl.ds(0, 2 * D), pl.ds(0, D)], w_down.at[at], sems.at[0])

    def wide(out, first, count, at, sem):
        for n in range(count):
            part = rows[first + n * D : first + (n + 1) * D].astype(F32)
            stage[at : at + D, n * D : (n + 1) * D] = part
        return pltpu.make_async_copy(stage.at[pl.ds(at, D), pl.ds(0, count * D)], out, sems.at[sem])

    copies = []
    if half == 0:
        copies.append(wide(w_up, UP, MLP // D, 2 * D, 1))
        copies[-1].start()
        copies.append(down(DOWN[0]))
        copies[-1].start()
    else:
        copies.append(wide(w_qkv, QKV - HALF, 3, 2 * D, 1))
        copies[-1].start()
        copies.append(wide(w_proj, PROJ - HALF, 1, 3 * D, 2))
        copies[-1].start()
        copies.append(down(DOWN[1] - HALF))
        copies[-1].start()
    for copy in copies:
        copy.wait()


def unpack_first_kernel(own, *refs):
    core = lax.rem(lax.axis_index("dp"), 2)
    for half in range(2):

        @pl.when(core == half)
        def _():
            unpack_half(half, own, *refs)


def unpack_second_kernel(
    other, own, in_up, in_down, in_proj, in_qkv, w_up, w_down, w_proj, w_qkv,
    gain_one, bias_one, b_query, b_value, table, b_proj, gain_two, bias_two, b_up, b_down, stage, sems,
):
    core = lax.rem(lax.axis_index("dp"), 2)
    for half in range(2):

        @pl.when(core != half)
        def _():
            unpack_half(half, other, w_up, w_down, w_proj, w_qkv, stage, sems)

    small = slice(SMALL_ONE, HALF)
    mine, others = own[small].astype(F32), other[small].astype(F32)
    first = jnp.where(core == 0, mine, others)
    second = jnp.where(core == 0, others, mine)
    for n, out in enumerate((gain_two, bias_two, b_proj, b_down)):
        out[...] = first[n : n + 1]
    for n in range(MLP // D):
        b_up[:, n * D : (n + 1) * D] = first[4 + n : 5 + n]
    table[...] = second[:HEADS, :ENTRIES]
    for n, out in enumerate((b_query, b_value, gain_one, bias_one)):
        out[...] = second[HEADS + n : HEADS + n + 1]


LARGE = ((D, MLP), (MLP, D), (D, D), (D, 3 * D))
UNPACK_SCRATCH = [pltpu.VMEM((4 * D, MLP), F32), pltpu.SemaphoreType.DMA((3,))]
def unpack_first(own):
    return pl.pallas_call(
        unpack_first_kernel,
        grid=(1,),
        in_specs=[whole(own.shape)],
        out_specs=[there] * 4,
        out_shape=[struct(shape, F32) for shape in LARGE],
        scratch_shapes=UNPACK_SCRATCH,
        compiler_params=params(24),
        cost_estimate=pl.CostEstimate(flops=0, bytes_accessed=2_400_000, transcendentals=0),
        name="unpack_own_half",
    )(own)


def unpack_second(other, own, large):
    one, four = (1, D), (1, MLP)
    shapes = [one, one, one, one, (HEADS, ENTRIES), one, one, one, four, one]
    out = pl.pallas_call(
        unpack_second_kernel,
        grid=(1,),
        in_specs=[whole(other.shape), whole(own.shape)] + [there] * 4,
        out_specs=[there] * 4 + [whole(shape) for shape in shapes],
        out_shape=[struct(shape, F32) for shape in LARGE] + [struct(shape, F32) for shape in shapes],
        scratch_shapes=UNPACK_SCRATCH,
        input_output_aliases={2: 0, 3: 1, 4: 2, 5: 3},
        compiler_params=params(24),
        name="unpack_other_half",
    )(other, own, *large)
    w_up, w_down, w_proj, w_qkv = out[:4]
    gain_one, bias_one, b_query, b_value, table, b_proj, gain_two, bias_two, b_up, b_down = out[4:]
    return (
        gain_one[0], bias_one[0], w_qkv, b_query[0], b_value[0], table.T, w_proj, b_proj[0],
        gain_two[0], bias_two[0], w_up, b_up[0], w_down, b_down[0],
    )


def coords(index):
    dp, space = divmod(index, 32)
    return {"c": dp % 2, "y": dp // 2 + 2 * ((space // 4) % 2), "x": space % 4, "z": space // 8}


def index_of(c, y, x, z):
    return ((y % 2) * 2 + c) * 32 + z * 8 + (y // 2) * 4 + x


DISTANCES = (2, 1, 3)
STAGES = (("y", "x"), ("x", "z"), ("z", "y"))


def other_core():
    return [(i, index_of(**(coords(i) | {"c": 1 - i // 32 % 2}))) for i in range(128)]


def around(stage, distance):
    out = []
    for i in range(128):
        at = coords(i)
        axis = stage[at["c"]]
        out.append((i, index_of(**(at | {axis: (at[axis] + distance) % 4}))))
    return out


def take(rows, start, count):
    return lax.dynamic_slice_in_dim(rows, start, count, 0)


def sum_everywhere(mine, got_core, at, pieces):
    made = {}
    left = list(pieces)

    def exchange(stage, sends, own):
        nonlocal made
        ahead, beside = left.pop(0)
        early = ahead(made)
        got = [lax.ppermute(sends[d], AXES, around(stage, d)) for d in DISTANCES]
        made, own = lax.optimization_barrier((made, own))
        made = made | beside(made)
        got, made, early, own = lax.optimization_barrier((got, made, early, own))
        made = made | early
        return dict(zip(DISTANCES, got)), own

    def place(stage):
        return jnp.where(at["c"] == 0, at[stage[0]], at[stage[1]])

    stage = STAGES[0]
    here = place(stage)
    count = mine.shape[0] // 4

    def part(which):
        start = which * count
        return take(mine, start, count) + take(got_core, start, count).astype(F32)

    sends = {d: part((here + d) % 4).astype(BF16) for d in DISTANCES}
    got, rows = exchange(stage, sends, part(here))
    for d in DISTANCES:
        rows = rows + got[d].astype(F32)
    low = rows.astype(BF16)
    for stage in STAGES[1:]:
        got, low = exchange(stage, {d: low for d in DISTANCES}, low)
        pairs = low.astype(F32) + got[2].astype(F32), got[1].astype(F32) + got[3].astype(F32)
        low = (pairs[0] + pairs[1]).astype(BF16)
    got, low = exchange(STAGES[0], {d: low for d in DISTANCES}, low)
    whole_half = jnp.zeros((4 * count, D), BF16)
    for d, rows in [(0, low), *got.items()]:
        whole_half = lax.dynamic_update_slice(whole_half, rows, ((here - d) % 4 * count, 0))
    return whole_half, made


def body(
    image_in, cotangent, regions, first_gain, first_bias, qkv_weight, query_bias, value_bias,
    position_table, proj_weight, proj_bias, second_gain, second_bias, up_weight, up_bias,
    down_weight, down_bias,
):
    many = lax.axis_size("dp") * lax.axis_size("space") == 128
    me = lax.axis_index(AXES)
    at = coords(me)
    first_rows = pack_first_rows(image_in, cotangent, regions)
    halo, regions_halo = from_behind(first_rows, "space", -1)
    gather = gather_matrix()
    spread, spread_rows = label_matrices()
    entries = jnp.asarray(entry_matrix(), BF16)
    mask = jnp.asarray(head_mask(), BF16)
    scatter = jnp.asarray(gather.T, BF16)
    mine, send, tokens, resid, active, d_resid, d_qkv = run_grads(
        image_in, cotangent, halo, regions, regions_halo,
        jnp.asarray(spread, BF16), jnp.asarray(spread_rows), jnp.asarray(gather, BF16),
        mask, entries, position_table.T, first_gain[None], first_bias[None], qkv_weight, query_bias[None],
        value_bias[None], proj_weight, proj_bias[None], second_gain[None], second_bias[None],
        up_weight, up_bias[None], down_weight,
    )
    if many:
        got = lax.ppermute(send, AXES, other_core())

    def block_output(*given):
        others = (down_weight, down_bias[None], scatter)
        return run_field(output_strip, "block_output", 0, (active, resid), others, *given)

    def image_gradient(*given):
        others = (qkv_weight, first_gain[None], scatter)
        return run_field(image_strip, "image_gradient", 1, (d_qkv, d_resid, tokens), others, *given)

    def lower_strips(made):
        out, tails = block_output()
        image, tails = image_gradient(None, tails)
        return {"out": out, "image": image, "tails": tails}

    def upper_out(made):
        return made | {"out": block_output(made["out"])[0]}

    def return_rows(made):
        return {"returned": from_behind(made["tails"], "space", 1)}

    def upper_image(made):
        return made | {"image": image_gradient(made["image"])[0]}

    def nothing(made):
        return {}

    def fields(made):
        first, at = made["returned"][:, SENT - SHIFT :], (0, 0, 0)
        return {
            "out": lax.dynamic_update_slice(made["out"], first[0], at),
            "image": lax.dynamic_update_slice(made["image"], first[1], at),
        }

    pieces = [(nothing, lower_strips), (nothing, upper_out), (return_rows, upper_image), (nothing, fields)]
    if many:
        own, made = sum_everywhere(mine, got, at, pieces)
        other = lax.ppermute(own, AXES, other_core())
        large = unpack_first(own)
        other, large = lax.optimization_barrier((other, large))
    else:
        made = {}
        for ahead, beside in pieces:
            made = made | ahead(made) | beside(made)
        own, other = mine.astype(BF16), send
        large = unpack_first(own)
    return (made["out"], made["image"]) + unpack_second(other, own, large)


def solution(mesh):
    tokens = P(AXES, None, None)
    return jax.shard_map(
        body,
        mesh=mesh,
        in_specs=(tokens, tokens, P(AXES, None)) + (P(),) * 14,
        out_specs=(tokens, tokens) + (P(),) * 14,
        check_vma=False,
    )
```

```python
import functools
import math

import jax
import jax.numpy as jnp
import numpy as np
from jax import lax
from jax.experimental import pallas as pl
from jax.experimental.pallas import tpu as pltpu
from jax.sharding import PartitionSpec as P

WIN = 7
SHIFT = 3
HEADS = 8
TOKENS = WIN * WIN
PAD = 56
LANES = 64
ENTRIES = (2 * WIN - 1) * (2 * WIN - 1)
COLS = 42
WINDOWS = COLS // WIN
STRIP = WINDOWS * PAD
STRIPS = COLS // WIN
SENT = 5
FIELD_STEPS = STRIPS // 2
TOTAL = STRIPS * STRIP
ROW = 48
D = 256
MLP = 1024
BF16 = jnp.bfloat16
F32 = jnp.float32
epsilon = 1e-05
neg = -1000000000.0
AXES = ("dp", "space")
SCALE = 1.0 / math.sqrt(D // HEADS)
LOG2E = 1.4426950408889634
UP = 0
DOWN = (MLP, MLP + 2 * D + 32)
SMALL_ONE = MLP + 2 * D
HALF = SMALL_ONE + 32
PROJ = HALF + 2 * D
QKV = PROJ + D
SMALL_TWO = QKV + 3 * D
assert SMALL_TWO + 32 == 2 * HALF


def from_behind(block, axis, distance):
    devices = range(lax.axis_size(axis))
    route = [((i - distance) % len(devices), i) for i in devices]
    return lax.ppermute(block, axis, route)


def place(i, j):
    return 8 * i + j


def gather_matrix():
    out = np.zeros((STRIP, WIN * ROW), np.float32)
    for w in range(WINDOWS):
        for i in range(WIN):
            for j in range(WIN):
                out[w * PAD + place(i, j), i * ROW + (w * WIN + j + SHIFT) % COLS] = 1.0
    return out


def label_matrices():
    spread = np.zeros((COLS, WINDOWS * 2 * LANES), np.float32)
    rows = np.zeros((WIN, WINDOWS * 2 * LANES), np.float32)
    for w in range(WINDOWS):
        for copy in range(2):
            for i in range(WIN):
                for j in range(WIN):
                    col = (w * 2 + copy) * LANES + place(i, j)
                    spread[(w * WIN + j + SHIFT) % COLS, col] = 1.0
                    rows[i, col] = 1.0
    return spread, rows


def entry_matrix():
    out = np.zeros((WIN * 128, D), np.float32)
    for kj in range(WIN):
        for di in range(1 - WIN, WIN):
            for qj in range(WIN):
                entry = (di + WIN - 1) * (2 * WIN - 1) + qj - kj + WIN - 1
                out[kj * 128 + (8 * di + qj) % 128, entry] = 1.0
    return out


def head_mask():
    return (np.arange(4 * LANES)[:, None] // LANES == np.arange(128)[None] // 32).astype(np.float32)


def dot(a, b):
    return jnp.dot(a, b, preferred_element_type=F32)


def dot_nt(a, b):
    return lax.dot_general(a, b, (((1,), (1,)), ((), ())), preferred_element_type=F32)


def dot_tn(a, b):
    return lax.dot_general(a, b, (((0,), (0,)), ((), ())), preferred_element_type=F32)


def normalize(values):
    center = values - jnp.mean(values, -1, keepdims=True)
    variance = jnp.mean(center * center, -1, keepdims=True)
    recip_dev = lax.rsqrt(variance + epsilon)
    return center * recip_dev, recip_dev


def norm_backward(upstream, normal_part, recip_dev, gain):
    scaled = upstream * gain
    inner_mean = jnp.mean(scaled, -1, keepdims=True)
    cross_mean = jnp.mean(scaled * normal_part, -1, keepdims=True)
    return recip_dev * (scaled - inner_mean - normal_part * cross_mean)


def col_sum(values):
    return jnp.sum(values, 0, keepdims=True)


def raster_rows(ref, halo, first, s):
    last = s == STRIPS - 1
    blank = jnp.zeros((ROW - COLS, D), BF16)
    rows = []
    for i in range(WIN):
        g = s * WIN + i + SHIFT
        if i < WIN - SHIFT:
            value = ref[g]
        else:
            value = jnp.where(
                last, halo[first + i - (WIN - SHIFT)], ref[jnp.minimum(g, COLS - 1)]
            )
        rows += [value, blank]
    return jnp.concatenate(rows, 0)


def put_rows(raster, first, which, out, tails, stage, sems):
    t = pl.program_id(0)
    slot = lax.rem(t, 2)

    def whole_strip(n):
        return pltpu.make_async_copy(
            stage.at[lax.rem(n, 2)], out.at[pl.ds((first + n) * WIN + SHIFT, WIN)], sems.at[lax.rem(n, 2)]
        )

    @pl.when(t >= 2)
    def _():
        whole_strip(t - 2).wait()

    for i in range(WIN):
        stage[slot, i] = raster[i * ROW : i * ROW + COLS]

    @pl.when(first + t < STRIPS - 1)
    def _():
        whole_strip(t).start()

    @pl.when(t == FIELD_STEPS - 1)
    def _():
        if tails is None:
            whole_strip(t - 1).wait()
            whole_strip(t).wait()
        else:
            own = pltpu.make_async_copy(
                stage.at[slot, 0 : WIN - SHIFT], out.at[COLS - (WIN - SHIFT) : COLS], sems.at[slot]
            )
            below = pltpu.make_async_copy(stage.at[slot, WIN - SENT : WIN], tails.at[which], sems.at[2])
            own.start()
            below.start()
            whole_strip(t - 1).wait()
            own.wait()
            below.wait()


def pad_rows(values):
    return jnp.concatenate([values, jnp.zeros((LANES - PAD,) + values.shape[1:], values.dtype)], 0)


def head_blocks(low, mask):
    return [jnp.concatenate([low[:, g : g + 128]] * 4, 0) * mask[...] for g in (0, 128)]


def turn_pair(values):
    turned = values.T
    return jnp.concatenate([turned[:LANES], turned[LANES:]], 1)


def three_parts(values):
    high = values.astype(BF16)
    rest = values - high.astype(F32)
    middle = rest.astype(BF16)
    return high, middle, (rest - middle.astype(F32)).astype(BF16)


def lane_ids(shape):
    return lax.broadcasted_iota(jnp.int32, shape, 1)


def build_bias(table, entries, by_head, bias_t):
    parts = three_parts(table * LOG2E)
    for kj in range(WIN):
        one = entries[kj * 128 : (kj + 1) * 128, :ENTRIES]
        by_head[:, kj, :] = dot_nt(parts[0], one) + dot_nt(parts[1], one) + dot_nt(parts[2], one)
    by_head[:, WIN, :] = jnp.full((HEADS, 128), neg, F32)
    lane = lane_ids((8, 128))
    for pair in range(HEADS // 2):
        for ki in range(WIN):
            first = pltpu.roll(by_head[2 * pair], 8 * ki, 1)
            second = pltpu.roll(by_head[2 * pair + 1], (8 * ki + LANES) % 128, 1)
            bias_t[8 * ki : 8 * ki + 8, 128 * pair : 128 * pair + 128] = jnp.where(
                lane < LANES, first, second
            )


def table_gradient(logit_sums, entries, by_head):
    lane = lane_ids((8, 128))
    for pair in range(HEADS // 2):
        for half in range(2):
            total = jnp.zeros((8, 128), F32)
            for ki in range(WIN):
                block = logit_sums[8 * ki : 8 * ki + 8, 128 * pair : 128 * pair + 128]
                own = jnp.where((lane < LANES) == (half == 0), block, 0.0)
                total = total + pltpu.roll(own, (128 - 8 * ki - LANES * half) % 128, 1)
            by_head[2 * pair + half] = total
    out = jnp.zeros((HEADS, D), F32)
    for kj in range(WIN):
        one = entries[kj * 128 : (kj + 1) * 128]
        for part in three_parts(by_head[:, kj, :]):
            out = out + dot(part, one)
    return out


def spans():
    return [slice(w * PAD, (w + 1) * PAD) for w in range(WINDOWS)]


def forward_stage(s, r):
    rows = pl.ds(pl.multiple_of(s * STRIP, 16), STRIP)
    slot = lax.rem(s, 2)
    tokens = dot(r.gather[...], raster_rows(r.image, r.halo, 0, s))
    r.tokens_all[rows] = tokens.astype(BF16)
    yield
    r.cot_all[rows] = dot(r.gather[...], raster_rows(r.cot, r.halo, SHIFT, s)).astype(BF16)
    yield
    normal_one, _ = normalize(tokens)
    first_low = (normal_one * r.gain_one[...] + r.bias_one[...]).astype(BF16)
    r.first_all[rows, :D] = first_low
    yield
    query = dot(first_low, r.w_qkv[:, :D]) + r.b_query[...]
    key = dot(first_low, r.w_qkv[:, D : 2 * D])
    value = dot(first_low, r.w_qkv[:, 2 * D :]) + r.b_value[...]
    yield
    key_labels = r.lane_labels[s].T
    logits = []
    for w, span in enumerate(spans()):
        query_low = pad_rows(query[span]).astype(BF16)
        key_low = pad_rows(key[span]).astype(BF16)
        value_low = pad_rows(value[span]).astype(BF16)
        r.qkv_win[slot, w, :, :D] = query_low
        r.qkv_win[slot, w, :, D : 2 * D] = key_low
        r.qkv_win[slot, w, :, 2 * D :] = value_low
        blocks = head_blocks(query_low, r.mask)
        logits.append(
            [dot_nt(key_low[:, 128 * g : 128 * g + 128], blocks[g])[:PAD] for g in range(2)]
        )
        yield
    turned = []
    for w in range(WINDOWS):
        same = key_labels[:PAD, w : w + 1] == r.lane_labels[s, w : w + 1, :]
        turned.append([])
        for pair in range(HEADS // 2):
            cols = slice(128 * pair, 128 * pair + 128)
            part = logits[w][pair // 2][:, 128 * (pair % 2) : 128 * (pair % 2) + 128]
            part = jnp.where(same, part * (SCALE * LOG2E) + r.bias_t[:, cols], neg)
            powers = jnp.exp2(part - jnp.max(part, 0, keepdims=True))
            attend = powers * (1.0 / jnp.sum(powers, 0, keepdims=True))
            attend_low = pad_rows(attend).astype(BF16)
            r.attend_win[slot, w, :, cols] = attend_low
            turned[w].append(turn_pair(attend_low))
        yield
    mixed_parts = []
    for w in range(WINDOWS):
        blocks = head_blocks(r.qkv_win[slot, w, :, 2 * D :], r.mask)
        mixed_parts.append(
            jnp.concatenate(
                [
                    dot(jnp.concatenate(turned[w][2 * g : 2 * g + 2], 1), blocks[g])[:PAD]
                    for g in range(2)
                ],
                1,
            )
        )
        yield
    mixed_low = jnp.concatenate(mixed_parts, 0).astype(BF16)
    r.mixed_all[rows] = mixed_low
    resid = tokens + dot(mixed_low, r.w_proj[...]) + r.b_proj[...]
    r.resid_all[rows] = resid
    for copy in early_copies(r, s):
        copy.start()
    yield


def strip_copies(s, sems, pairs):
    rows = pl.ds(pl.multiple_of(s * STRIP, 16), STRIP)
    return [pltpu.make_async_copy(a.at[rows], b.at[rows], sems.at[s, n]) for n, (a, b) in enumerate(pairs)]


def early_copies(r, s):
    return strip_copies(s, r.early_sems, ((r.tokens_all, r.tokens_out), (r.resid_all, r.resid_out)))


def late_copies(r, s):
    pairs = (r.active_all, r.active_out), (r.d_branch_all, r.d_branch_out), (r.d_qkv_all, r.d_qkv_out)
    return strip_copies(s, r.late_sems, pairs)


def backward_stage(s, r):
    rows = pl.ds(pl.multiple_of(s * STRIP, 16), STRIP)
    slot = lax.rem(s, 2)
    sums = r.sums
    resid = r.resid_all[rows]
    normal_two, recip_two = normalize(resid)
    second_low = (normal_two * r.gain_two[...] + r.bias_two[...]).astype(BF16)
    r.second_all[rows, :D] = second_low
    yield
    cot_low = r.cot_all[rows]
    d_second = jnp.zeros((STRIP, D), F32)
    for n in range(MLP // D):
        cols = slice(n * D, (n + 1) * D)
        inner = dot(second_low, r.w_up[:, cols]) + r.b_up[:, cols]
        cumulative = 0.5 * lax.erf(inner * 0.7071067811865476) + 0.5
        active_low = (inner * cumulative).astype(BF16)
        r.active_all[rows, cols] = active_low
        yield
        gauss = jnp.exp2(inner * inner * (-0.5 * LOG2E))
        slope = cumulative + inner * gauss * 0.3989422804014327
        d_inner = (dot_nt(cot_low, r.w_down[cols]) * slope).astype(BF16)
        r.d_inner_all[rows, cols] = d_inner
        yield
        d_second = d_second + dot_nt(d_inner, r.w_up[:, cols])
        yield
    cot_f32 = cot_low.astype(F32)
    d_resid = cot_f32 + norm_backward(d_second, normal_two, recip_two, r.gain_two[...])
    d_branch = d_resid.astype(BF16)
    r.d_branch_all[rows] = d_branch
    yield
    d_mixed = dot_nt(d_branch, r.w_proj[...])
    yield
    sums[0:1] += col_sum(d_second * normal_two)
    sums[1:2] += col_sum(d_second)
    sums[2:3] += col_sum(d_resid)
    sums[3:4] += col_sum(cot_f32)
    yield
    mixed_blocks = []
    d_attends = []
    for w, span in enumerate(spans()):
        blocks = head_blocks(pad_rows(d_mixed[span]).astype(BF16), r.mask)
        mixed_blocks.append(blocks)
        value_low = r.qkv_win[slot, w, :, 2 * D :]
        d_attends.append(
            [dot_nt(value_low[:, 128 * g : 128 * g + 128], blocks[g])[:PAD] for g in range(2)]
        )
        yield
    d_logits = []
    turned = []
    for w in range(WINDOWS):
        d_logits.append([])
        turned.append([])
        for pair in range(HEADS // 2):
            cols = slice(128 * pair, 128 * pair + 128)
            part = d_attends[w][pair // 2][:, 128 * (pair % 2) : 128 * (pair % 2) + 128]
            attend = r.attend_win[slot, w, :, cols].astype(F32)[:PAD]
            cross = jnp.sum(part * attend, 0, keepdims=True)
            part = attend * (part - cross)
            r.logit_sums[:, cols] += part
            low = pad_rows(part).astype(BF16)
            d_logits[w].append(low)
            turned[w].append(turn_pair(low))
        yield
    parts = []
    for w in range(WINDOWS):
        query_blocks = head_blocks(r.qkv_win[slot, w, :, :D], r.mask)
        key_blocks = head_blocks(r.qkv_win[slot, w, :, D : 2 * D], r.mask)
        d_query, d_key, d_value = [], [], []
        for g in range(2):
            two = slice(2 * g, 2 * g + 2)
            attend_low = r.attend_win[slot, w, :, 256 * g : 256 * g + 256]
            d_value.append(dot(attend_low, mixed_blocks[w][g])[:PAD])
            d_key.append(dot(jnp.concatenate(d_logits[w][two], 1), query_blocks[g])[:PAD] * SCALE)
            d_query.append(dot(jnp.concatenate(turned[w][two], 1), key_blocks[g])[:PAD] * SCALE)
        parts.append(jnp.concatenate(d_query + d_key + d_value, 1))
        yield
    d_qkv = jnp.concatenate(parts, 0).astype(BF16)
    r.d_qkv_all[rows] = d_qkv
    for copy in late_copies(r, s):
        copy.start()
    yield


WEAVE = (-0.03, 0.144, 0.165, 0.354, 0.445)


def run(*stages):
    order = []
    for n, stage in enumerate(stages):
        count = PIECES[stage.__name__]
        places = (np.arange(count) + 0.5) / count
        if n:
            places = np.interp(places, np.linspace(0.0, 1.0, len(WEAVE)), WEAVE)
        order += [(place, n) for place in places]
    for _, n in sorted(order):
        next(stages[n])
    for stage in stages:
        assert next(stage, None) is None


PIECES = {"forward_stage": 5 + 3 * WINDOWS, "backward_stage": 1 + 3 * (MLP // D) + 3 + 3 * WINDOWS + 1}


def down_rows(n):
    return DOWN[n // 2] + (n % 2) * D


def finish(r):
    core = lax.rem(lax.axis_index("dp"), 2)
    grads = r.grads

    def put(start, rows):
        grads[start : start + rows.shape[0]] = rows
        r.grads_low[start : start + rows.shape[0]] = rows.astype(BF16)

    def sends(n, start, count):
        half, at = divmod(start, HALF)
        span = pl.ds(at, count)
        keep = pltpu.make_async_copy(grads.at[pl.ds(start, count)], r.keep.at[span], r.sems.at[n])
        send = pltpu.make_async_copy(r.grads_low.at[pl.ds(start, count)], r.send.at[span], r.sems.at[n])
        return half, keep, send

    def begin(half, keep, send):
        @pl.when(core == half)
        def _():
            keep.start()

        @pl.when(core != half)
        def _():
            send.start()

    def end(half, keep, send):
        @pl.when(core == half)
        def _():
            keep.wait()

        @pl.when(core != half)
        def _():
            send.wait()

    small = SMALL_TWO
    put(small, table_gradient(r.logit_sums, r.entries, r.by_head))
    product = dot_tn(r.first_all[:, : D + 8], r.d_qkv_all[...])
    sums = product[D : D + 8]
    for n in range(3):
        put(QKV + n * D, product[:D, n * D : (n + 1) * D])
    bias_grad = jnp.zeros((8, D), F32)
    for part in three_parts(sums):
        bias_grad = bias_grad + dot_nt(part, r.w_qkv[...])
    cross = jnp.zeros((8, D), F32)
    for part in three_parts(product[:D] * r.w_qkv[...].astype(F32)):
        cross = cross + dot_nt(jnp.ones((8, 3 * D), BF16), part)
    gain_grad = (cross[0:1] - r.bias_one[...] * bias_grad[0:1]) / r.gain_one[...]
    put(
        small + 8,
        jnp.concatenate(
            [sums[0:1, :D], sums[0:1, 2 * D :], gain_grad, bias_grad[0:1], jnp.zeros((20, D), F32)], 0
        ),
    )
    copies = [sends(0, QKV, 3 * D + 32)]
    begin(*copies[-1])
    product = dot_tn(r.second_all[:, : D + 8], r.d_inner_all[...])
    for n in range(MLP // D):
        put(UP + n * D, product[:D, n * D : (n + 1) * D])
    ups = [product[D : D + 1, n * D : (n + 1) * D] for n in range(MLP // D)]
    put(SMALL_ONE, jnp.concatenate([r.sums[0:4]] + ups + [jnp.zeros((24, D), F32)], 0))
    copies += [sends(1, UP, MLP), sends(2, SMALL_ONE, 32)]
    begin(*copies[-2])
    begin(*copies[-1])
    product = dot_tn(r.cot_all[...], r.active_all[...])
    for n in range(MLP // D):
        put(down_rows(n), product[:, n * D : (n + 1) * D])
    copies += [sends(3, DOWN[0], 2 * D), sends(4, DOWN[1], 2 * D)]
    begin(*copies[-2])
    begin(*copies[-1])
    put(PROJ, dot_tn(r.mixed_all[...], r.d_branch_all[...]))
    copies += [sends(5, PROJ, D)]
    begin(*copies[-1])
    for copy in copies:
        end(*copy)
    for n in range(STRIPS):
        for copy in early_copies(r, n) + late_copies(r, n):
            copy.wait()


class Refs:
    def __init__(self, names, refs):
        self.__dict__.update(zip(names, refs))


INPUTS = [
    "image", "cot", "gather", "mask", "entries", "w_qkv", "w_proj", "w_up", "w_down",
    "halo", "regions", "regions_halo", "spread", "spread_rows", "table",
    "gain_one", "bias_one", "b_query", "b_value", "b_proj", "gain_two", "bias_two", "b_up",
]
NAMES = [name + "_in" for name in INPUTS] + [
    "keep", "send", "tokens_out", "resid_out", "active_out", "d_branch_out", "d_qkv_out",
    "lane_labels", "by_head", "bias_t", "logit_sums", "qkv_win", "attend_win", "sums",
    "first_all", "cot_all", "mixed_all", "second_all", "active_all", "d_inner_all", "d_branch_all", "d_qkv_all",
    "tokens_all", "resid_all", "grads", "grads_low", "sems", "in_sems", "early_sems", "late_sems",
] + INPUTS


def input_copies(r):
    top = WIN + SHIFT
    last = [("w_up", None), ("w_down", None), ("image", slice(top, COLS)), ("cot", slice(top, COLS))]
    large = ["entries", "gather", "image", "w_qkv", "mask", "cot", "w_proj"]
    names = [name for name in INPUTS if name not in large + ["w_up", "w_down"]] + large
    first = [(name, slice(0, top) if name in ("image", "cot") else None) for name in names]
    copies = []
    for n, (name, rows) in enumerate(first + last):
        source, place = getattr(r, name + "_in"), getattr(r, name)
        if rows is not None:
            source, place = source.at[rows], place.at[rows]
        copies.append(pltpu.make_async_copy(source, place, r.in_sems.at[n]))
    return copies[: len(first)], copies[len(first) :]


def put_labels(r, n, part):
    row = jnp.sum(part * r.spread_rows[...], 0, keepdims=True)
    windows = [row[:, 128 * w : 128 * w + 128] for w in range(WINDOWS)]
    r.lane_labels[n] = jnp.concatenate(windows + [jnp.zeros((2, 128), F32)], 0)


def grads_kernel(*refs):
    r = Refs(NAMES, refs)
    s = pl.program_id(0)

    @pl.when(s == 0)
    def _():
        first, later = input_copies(r)
        for copy in first:
            copy.start()
        for copy in first:
            copy.wait()
        for copy in later:
            copy.start()
        own = dot(r.regions[...].astype(F32).astype(BF16), r.spread[...])
        for n in range(STRIPS - 1):
            put_labels(r, n, own[n * WIN + SHIFT : (n + 1) * WIN + SHIFT])
        below = dot(r.regions_halo[...], r.spread[...])
        put_labels(r, STRIPS - 1, jnp.concatenate([own[COLS - (WIN - SHIFT) :], below], 0))
        build_bias(r.table[...], r.entries, r.by_head, r.bias_t)
        r.logit_sums[...] = jnp.zeros_like(r.logit_sums)
        one = (lane_ids((TOTAL, 128)) == 0).astype(F32).astype(BF16)
        r.first_all[:, D:] = one
        r.second_all[:, D:] = one
        r.sums[...] = jnp.zeros_like(r.sums)
        run(forward_stage(s, r))
        for copy in later:
            copy.wait()

    @pl.when((s > 0) & (s < STRIPS))
    def _():
        run(backward_stage(s - 1, r), forward_stage(s, r))

    @pl.when(s == STRIPS)
    def _():
        run(backward_stage(s - 1, r))
        finish(r)


def output_strip(active, resid, w_down, b_down, scatter):
    result = resid[...] + b_down[...] + dot(active[...], w_down[...])
    return dot(scatter[...], result.astype(BF16)).astype(BF16)


def image_strip(d_qkv, d_branch, tokens, w_qkv, gain, scatter):
    normal, recip_dev = normalize(tokens[...].astype(F32))
    d_first = dot_nt(d_qkv[...], w_qkv[...])
    grad = d_branch[...].astype(F32) + norm_backward(d_first, normal, recip_dev, gain[...])
    return dot(scatter[...], grad.astype(BF16)).astype(BF16)


there = pl.BlockSpec(memory_space=pl.ANY)


def whole(shape):
    return pl.BlockSpec(shape, lambda s: (0,) * len(shape))


def once(shape):
    return pl.BlockSpec(shape, lambda s: (0,) * len(shape), pipeline_mode=pl.Buffered(1))


def strips(shape):
    return pl.BlockSpec(shape, lambda s: (s,) + (0,) * (len(shape) - 1))


def struct(shape, dtype):
    return jax.ShapeDtypeStruct(shape, dtype)


def params(mebibytes):
    return pltpu.CompilerParams(
        vmem_limit_bytes=mebibytes * 1024 * 1024, dimension_semantics=("arbitrary",)
    )


def pack_kernel(image, cot, regions, rows, labels):
    rows[0:SHIFT] = image[...]
    rows[SHIFT:] = cot[...]
    labels[...] = regions[0:SHIFT].astype(F32).astype(BF16)


def pack_first_rows(image, cot, regions):
    return pl.pallas_call(
        pack_kernel,
        grid=(1,),
        in_specs=[whole((SHIFT, COLS, D)), whole((SHIFT, COLS, D)), whole(regions.shape)],
        out_specs=[whole((2 * SHIFT, COLS, D)), whole((SHIFT, COLS))],
        out_shape=[pltpu.VMEM((2 * SHIFT, COLS, D), BF16), pltpu.VMEM((SHIFT, COLS), BF16)],
        compiler_params=params(62),
        name="pack_first_rows",
    )(image, cot, regions)


def run_grads(*args):
    return pl.pallas_call(
        grads_kernel,
        grid=(STRIPS + 1,),
        in_specs=[there] * len(args),
        out_specs=[there] * 7,
        out_shape=[
            pltpu.VMEM((HALF, D), F32),
            pltpu.VMEM((HALF, D), BF16),
            struct((TOTAL, D), BF16),
            struct((TOTAL, D), F32),
            struct((TOTAL, MLP), BF16),
            struct((TOTAL, D), BF16),
            struct((TOTAL, 3 * D), BF16),
        ],
        scratch_shapes=[
            pltpu.VMEM((STRIPS, 8, 128), F32),
            pltpu.VMEM((HEADS, 8, 128), F32),
            pltpu.VMEM((PAD, HEADS * LANES), F32),
            pltpu.VMEM((PAD, HEADS * LANES), F32),
            pltpu.VMEM((2, WINDOWS, LANES, 3 * D), BF16),
            pltpu.VMEM((2, WINDOWS, LANES, HEADS * LANES), BF16),
            pltpu.VMEM((8, D), F32),
            pltpu.VMEM((TOTAL, D + 128), BF16),
            pltpu.VMEM((TOTAL, D), BF16),
            pltpu.VMEM((TOTAL, D), BF16),
            pltpu.VMEM((TOTAL, D + 128), BF16),
            pltpu.VMEM((TOTAL, MLP), BF16),
            pltpu.VMEM((TOTAL, MLP), BF16),
            pltpu.VMEM((TOTAL, D), BF16),
            pltpu.VMEM((TOTAL, 3 * D), BF16),
            pltpu.VMEM((TOTAL, D), BF16),
            pltpu.VMEM((TOTAL, D), F32),
            pltpu.VMEM((2 * HALF, D), F32),
            pltpu.VMEM((2 * HALF, D), BF16),
            pltpu.SemaphoreType.DMA((6,)),
            pltpu.SemaphoreType.DMA((len(INPUTS) + 2,)),
            pltpu.SemaphoreType.DMA((STRIPS, 2)),
            pltpu.SemaphoreType.DMA((STRIPS, 3)),
        ]
        + [pltpu.VMEM(a.shape, a.dtype) for a in args],
        compiler_params=params(58),
        cost_estimate=pl.CostEstimate(
            flops=2 * TOTAL * 10 * D * MLP, bytes_accessed=20_000_000, transcendentals=0
        ),
        name="all_gradients",
    )(*args)


def run_field(strip, name, which, blocks, others, field=None, tails=None):
    lower = field is None
    first = FIELD_STEPS if lower else 0
    given = [a for a in (field, tails) if a is not None]
    inputs = len(blocks) + len(others)
    shapes = [struct((COLS, COLS, D), BF16)] + [struct((2, SENT, COLS, D), BF16)] * lower

    def kernel(*refs):
        out = refs[inputs + len(given)]
        below = refs[inputs + len(given) + 1] if lower else None
        put_rows(strip(*refs[:inputs]), first, which, out, below, *refs[-2:])

    return pl.pallas_call(
        kernel,
        grid=(FIELD_STEPS,),
        in_specs=[pl.BlockSpec((STRIP, a.shape[1]), lambda t: (first + t, 0)) for a in blocks]
        + [whole(a.shape) for a in others]
        + [there] * len(given),
        out_specs=[there] * len(shapes),
        out_shape=shapes,
        scratch_shapes=[pltpu.VMEM((2, WIN, COLS, D), BF16), pltpu.SemaphoreType.DMA((3,))],
        input_output_aliases={inputs: 1 if lower else 0} if given else {},
        compiler_params=params(60),
        cost_estimate=pl.CostEstimate(
            flops=2 * TOTAL * 4 * D * D, bytes_accessed=9_000_000, transcendentals=0
        ),
        name=name,
    )(*blocks, *others, *given)


def unpack_half(half, rows, w_up, w_down, w_proj, w_qkv, stage, sems):
    def down(first):
        for n in range(2):
            stage[n * D : (n + 1) * D, :D] = rows[first + n * D : first + (n + 1) * D].astype(F32).T
        at = pl.ds(half * 2 * D, 2 * D)
        return pltpu.make_async_copy(stage.at[pl.ds(0, 2 * D), pl.ds(0, D)], w_down.at[at], sems.at[0])

    def wide(out, first, count, at, sem):
        for n in range(count):
            part = rows[first + n * D : first + (n + 1) * D].astype(F32)
            stage[at : at + D, n * D : (n + 1) * D] = part
        return pltpu.make_async_copy(stage.at[pl.ds(at, D), pl.ds(0, count * D)], out, sems.at[sem])

    copies = []
    if half == 0:
        copies.append(wide(w_up, UP, MLP // D, 2 * D, 1))
        copies[-1].start()
        copies.append(down(DOWN[0]))
        copies[-1].start()
    else:
        copies.append(wide(w_qkv, QKV - HALF, 3, 2 * D, 1))
        copies[-1].start()
        copies.append(wide(w_proj, PROJ - HALF, 1, 3 * D, 2))
        copies[-1].start()
        copies.append(down(DOWN[1] - HALF))
        copies[-1].start()
    for copy in copies:
        copy.wait()


def unpack_first_kernel(own, *refs):
    core = lax.rem(lax.axis_index("dp"), 2)
    for half in range(2):

        @pl.when(core == half)
        def _():
            unpack_half(half, own, *refs)


def unpack_second_kernel(
    other, own, in_up, in_down, in_proj, in_qkv, w_up, w_down, w_proj, w_qkv,
    gain_one, bias_one, b_query, b_value, table, b_proj, gain_two, bias_two, b_up, b_down, stage, sems,
):
    core = lax.rem(lax.axis_index("dp"), 2)
    for half in range(2):

        @pl.when(core != half)
        def _():
            unpack_half(half, other, w_up, w_down, w_proj, w_qkv, stage, sems)

    small = slice(SMALL_ONE, HALF)
    mine, others = own[small].astype(F32), other[small].astype(F32)
    first = jnp.where(core == 0, mine, others)
    second = jnp.where(core == 0, others, mine)
    for n, out in enumerate((gain_two, bias_two, b_proj, b_down)):
        out[...] = first[n : n + 1]
    for n in range(MLP // D):
        b_up[:, n * D : (n + 1) * D] = first[4 + n : 5 + n]
    table[...] = second[:HEADS, :ENTRIES]
    for n, out in enumerate((b_query, b_value, gain_one, bias_one)):
        out[...] = second[HEADS + n : HEADS + n + 1]


LARGE = ((D, MLP), (MLP, D), (D, D), (D, 3 * D))
UNPACK_SCRATCH = [pltpu.VMEM((4 * D, MLP), F32), pltpu.SemaphoreType.DMA((3,))]
def unpack_first(own):
    return pl.pallas_call(
        unpack_first_kernel,
        grid=(1,),
        in_specs=[whole(own.shape)],
        out_specs=[there] * 4,
        out_shape=[struct(shape, F32) for shape in LARGE],
        scratch_shapes=UNPACK_SCRATCH,
        compiler_params=params(24),
        cost_estimate=pl.CostEstimate(flops=0, bytes_accessed=2_400_000, transcendentals=0),
        name="unpack_own_half",
    )(own)


def unpack_second(other, own, large):
    one, four = (1, D), (1, MLP)
    shapes = [one, one, one, one, (HEADS, ENTRIES), one, one, one, four, one]
    out = pl.pallas_call(
        unpack_second_kernel,
        grid=(1,),
        in_specs=[whole(other.shape), whole(own.shape)] + [there] * 4,
        out_specs=[there] * 4 + [whole(shape) for shape in shapes],
        out_shape=[struct(shape, F32) for shape in LARGE] + [struct(shape, F32) for shape in shapes],
        scratch_shapes=UNPACK_SCRATCH,
        input_output_aliases={2: 0, 3: 1, 4: 2, 5: 3},
        compiler_params=params(24),
        name="unpack_other_half",
    )(other, own, *large)
    w_up, w_down, w_proj, w_qkv = out[:4]
    gain_one, bias_one, b_query, b_value, table, b_proj, gain_two, bias_two, b_up, b_down = out[4:]
    return (
        gain_one[0], bias_one[0], w_qkv, b_query[0], b_value[0], table.T, w_proj, b_proj[0],
        gain_two[0], bias_two[0], w_up, b_up[0], w_down, b_down[0],
    )


def coords(index):
    dp, space = divmod(index, 32)
    return {"c": dp % 2, "y": dp // 2 + 2 * ((space // 4) % 2), "x": space % 4, "z": space // 8}


def index_of(c, y, x, z):
    return ((y % 2) * 2 + c) * 32 + z * 8 + (y // 2) * 4 + x


DISTANCES = (2, 1, 3)
STAGES = (("y", "x"), ("x", "z"), ("z", "y"))


def other_core():
    return [(i, index_of(**(coords(i) | {"c": 1 - i // 32 % 2}))) for i in range(128)]


def around(stage, distance):
    out = []
    for i in range(128):
        at = coords(i)
        axis = stage[at["c"]]
        out.append((i, index_of(**(at | {axis: (at[axis] + distance) % 4}))))
    return out


def take(rows, start, count):
    return lax.dynamic_slice_in_dim(rows, start, count, 0)


def sum_everywhere(mine, got_core, at, pieces):
    made = {}
    left = list(pieces)

    def exchange(stage, sends, own):
        nonlocal made
        ahead, beside = left.pop(0)
        early = ahead(made)
        got = [lax.ppermute(sends[d], AXES, around(stage, d)) for d in DISTANCES]
        made, own = lax.optimization_barrier((made, own))
        made = made | beside(made)
        got, made, early, own = lax.optimization_barrier((got, made, early, own))
        made = made | early
        return dict(zip(DISTANCES, got)), own

    def place(stage):
        return jnp.where(at["c"] == 0, at[stage[0]], at[stage[1]])

    stage = STAGES[0]
    here = place(stage)
    count = mine.shape[0] // 4

    def part(which):
        start = which * count
        return take(mine, start, count) + take(got_core, start, count).astype(F32)

    sends = {d: part((here + d) % 4).astype(BF16) for d in DISTANCES}
    got, rows = exchange(stage, sends, part(here))
    for d in DISTANCES:
        rows = rows + got[d].astype(F32)
    low = rows.astype(BF16)
    for stage in STAGES[1:]:
        got, low = exchange(stage, {d: low for d in DISTANCES}, low)
        pairs = low.astype(F32) + got[2].astype(F32), got[1].astype(F32) + got[3].astype(F32)
        low = (pairs[0] + pairs[1]).astype(BF16)
    got, low = exchange(STAGES[0], {d: low for d in DISTANCES}, low)
    whole_half = jnp.zeros((4 * count, D), BF16)
    for d, rows in [(0, low), *got.items()]:
        whole_half = lax.dynamic_update_slice(whole_half, rows, ((here - d) % 4 * count, 0))
    return whole_half, made


def body(
    image_in, cotangent, regions, first_gain, first_bias, qkv_weight, query_bias, value_bias,
    position_table, proj_weight, proj_bias, second_gain, second_bias, up_weight, up_bias,
    down_weight, down_bias,
):
    many = lax.axis_size("dp") * lax.axis_size("space") == 128
    me = lax.axis_index(AXES)
    at = coords(me)
    first_rows = pack_first_rows(image_in, cotangent, regions)
    halo, regions_halo = from_behind(first_rows, "space", -1)
    gather = gather_matrix()
    spread, spread_rows = label_matrices()
    entries = jnp.asarray(entry_matrix(), BF16)
    mask = jnp.asarray(head_mask(), BF16)
    scatter = jnp.asarray(gather.T, BF16)
    mine, send, tokens, resid, active, d_branch, d_qkv = run_grads(
        image_in, cotangent, jnp.asarray(gather, BF16), mask, entries, qkv_weight, proj_weight, up_weight, down_weight,
        halo, regions, regions_halo, jnp.asarray(spread, BF16), jnp.asarray(spread_rows), position_table.T,
        first_gain[None], first_bias[None], query_bias[None], value_bias[None], proj_bias[None],
        second_gain[None], second_bias[None], up_bias[None],
    )
    if many:
        got = lax.ppermute(send, AXES, other_core())

    def block_output(*given):
        others = (down_weight, down_bias[None], scatter)
        return run_field(output_strip, "block_output", 0, (active, resid), others, *given)

    def image_gradient(*given):
        others = (qkv_weight, first_gain[None], scatter)
        return run_field(image_strip, "image_gradient", 1, (d_qkv, d_branch, tokens), others, *given)

    def lower_out(made):
        out, tails = block_output()
        return {"out": out, "tails": tails}

    def lower_image(made):
        image, tails = image_gradient(None, made["tails"])
        return {"image": image, "tails": tails}

    def upper_out(made):
        return made | {"out": block_output(made["out"])[0]}

    def return_rows(made):
        return {"returned": from_behind(made["tails"], "space", 1)}

    def upper_image(made):
        return made | {"image": image_gradient(made["image"])[0]}

    def nothing(made):
        return {}

    def fields(made):
        first, at = made["returned"][:, SENT - SHIFT :], (0, 0, 0)
        return {
            "out": lax.dynamic_update_slice(made["out"], first[0], at),
            "image": lax.dynamic_update_slice(made["image"], first[1], at),
        }

    def upper_image_and_out(made):
        made = made | upper_image(made)
        return made | fields(made)

    pieces = [(nothing, lower_out), (nothing, lower_image), (return_rows, upper_out), (nothing, upper_image_and_out)]
    if many:
        own, made = sum_everywhere(mine, got, at, pieces)
        other = lax.ppermute(own, AXES, other_core())
        large = unpack_first(own)
        other, large = lax.optimization_barrier((other, large))
    else:
        made = {}
        for ahead, beside in pieces:
            made = made | ahead(made) | beside(made)
        own, other = mine.astype(BF16), send
        large = unpack_first(own)
    return (made["out"], made["image"]) + unpack_second(other, own, large)


def solution(mesh):
    tokens = P(AXES, None, None)
    return jax.shard_map(
        body,
        mesh=mesh,
        in_specs=(tokens, tokens, P(AXES, None)) + (P(),) * 14,
        out_specs=(tokens, tokens) + (P(),) * 14,
        check_vma=False,
    )
```

```python
import functools
import math

import jax
import jax.numpy as jnp
import numpy as np
from jax import lax
from jax.experimental import pallas as pl
from jax.experimental.pallas import tpu as pltpu
from jax.sharding import PartitionSpec as P

WIN = 7
SHIFT = 3
HEADS = 8
TOKENS = WIN * WIN
PAD = 56
LANES = 64
ENTRIES = (2 * WIN - 1) * (2 * WIN - 1)
COLS = 42
WINDOWS = COLS // WIN
STRIP = WINDOWS * PAD
STRIPS = COLS // WIN
SENT = 5
FIELD_STEPS = STRIPS // 2
TOTAL = STRIPS * STRIP
ROW = 48
D = 256
MLP = 1024
BF16 = jnp.bfloat16
F32 = jnp.float32
epsilon = 1e-05
neg = -1000000000.0
AXES = ("dp", "space")
SCALE = 1.0 / math.sqrt(D // HEADS)
LOG2E = 1.4426950408889634
UP = 0
HALF = MLP + 2 * D + 32
PROJ = HALF
QKV = PROJ + D
DOWN = (MLP, HALF + MLP)
SMALL_ONE = MLP + 2 * D
SMALL_TWO = HALF + SMALL_ONE
assert QKV + 3 * D == DOWN[1]


def from_behind(block, axis, distance):
    devices = range(lax.axis_size(axis))
    route = [((i - distance) % len(devices), i) for i in devices]
    return lax.ppermute(block, axis, route)


def place(i, j):
    return 8 * i + j


def gather_matrix():
    out = np.zeros((STRIP, WIN * ROW), np.float32)
    for w in range(WINDOWS):
        for i in range(WIN):
            for j in range(WIN):
                out[w * PAD + place(i, j), i * ROW + (w * WIN + j + SHIFT) % COLS] = 1.0
    return out


def label_matrices():
    spread = np.zeros((COLS, WINDOWS * 2 * LANES), np.float32)
    rows = np.zeros((WIN, WINDOWS * 2 * LANES), np.float32)
    for w in range(WINDOWS):
        for copy in range(2):
            for i in range(WIN):
                for j in range(WIN):
                    col = (w * 2 + copy) * LANES + place(i, j)
                    spread[(w * WIN + j + SHIFT) % COLS, col] = 1.0
                    rows[i, col] = 1.0
    return spread, rows


def entry_matrix():
    out = np.zeros((WIN * 128, D), np.float32)
    for kj in range(WIN):
        for di in range(1 - WIN, WIN):
            for qj in range(WIN):
                entry = (di + WIN - 1) * (2 * WIN - 1) + qj - kj + WIN - 1
                out[kj * 128 + (8 * di + qj) % 128, entry] = 1.0
    return out


def head_mask():
    return (np.arange(4 * LANES)[:, None] // LANES == np.arange(128)[None] // 32).astype(np.float32)


def dot(a, b):
    return jnp.dot(a, b, preferred_element_type=F32)


def dot_nt(a, b):
    return lax.dot_general(a, b, (((1,), (1,)), ((), ())), preferred_element_type=F32)


def dot_tn(a, b):
    return lax.dot_general(a, b, (((0,), (0,)), ((), ())), preferred_element_type=F32)


def normalize(values):
    center = values - jnp.mean(values, -1, keepdims=True)
    variance = jnp.mean(center * center, -1, keepdims=True)
    recip_dev = lax.rsqrt(variance + epsilon)
    return center * recip_dev, recip_dev


def norm_backward(upstream, normal_part, recip_dev, gain):
    scaled = upstream * gain
    inner_mean = jnp.mean(scaled, -1, keepdims=True)
    cross_mean = jnp.mean(scaled * normal_part, -1, keepdims=True)
    return recip_dev * (scaled - inner_mean - normal_part * cross_mean)


def col_sum(values):
    return jnp.sum(values, 0, keepdims=True)


def raster_rows(ref, halo, first, s):
    last = s == STRIPS - 1
    blank = jnp.zeros((ROW - COLS, D), BF16)
    rows = []
    for i in range(WIN):
        g = s * WIN + i + SHIFT
        if i < WIN - SHIFT:
            value = ref[g]
        else:
            value = jnp.where(
                last, halo[first + i - (WIN - SHIFT)], ref[jnp.minimum(g, COLS - 1)]
            )
        rows += [value, blank]
    return jnp.concatenate(rows, 0)


def put_rows(raster, first, which, out, tails, stage, sems):
    t = pl.program_id(0)
    slot = lax.rem(t, 2)

    def whole_strip(n):
        return pltpu.make_async_copy(
            stage.at[lax.rem(n, 2)], out.at[pl.ds((first + n) * WIN + SHIFT, WIN)], sems.at[lax.rem(n, 2)]
        )

    @pl.when(t >= 2)
    def _():
        whole_strip(t - 2).wait()

    for i in range(WIN):
        stage[slot, i] = raster[i * ROW : i * ROW + COLS]

    @pl.when(first + t < STRIPS - 1)
    def _():
        whole_strip(t).start()

    @pl.when(t == FIELD_STEPS - 1)
    def _():
        if tails is None:
            whole_strip(t - 1).wait()
            whole_strip(t).wait()
        else:
            own = pltpu.make_async_copy(
                stage.at[slot, 0 : WIN - SHIFT], out.at[COLS - (WIN - SHIFT) : COLS], sems.at[slot]
            )
            below = pltpu.make_async_copy(stage.at[slot, WIN - SENT : WIN], tails.at[which], sems.at[2])
            own.start()
            below.start()
            whole_strip(t - 1).wait()
            own.wait()
            below.wait()


def pad_rows(values):
    return jnp.concatenate([values, jnp.zeros((LANES - PAD,) + values.shape[1:], values.dtype)], 0)


def head_blocks(low, mask):
    return [jnp.concatenate([low[:, g : g + 128]] * 4, 0) * mask[...] for g in (0, 128)]


def turn_pair(values):
    turned = values.T
    return jnp.concatenate([turned[:LANES], turned[LANES:]], 1)


def three_parts(values):
    high = values.astype(BF16)
    rest = values - high.astype(F32)
    middle = rest.astype(BF16)
    return high, middle, (rest - middle.astype(F32)).astype(BF16)


def lane_ids(shape):
    return lax.broadcasted_iota(jnp.int32, shape, 1)


def build_bias(table, entries, by_head, bias_t):
    parts = three_parts(table * LOG2E)
    for kj in range(WIN):
        one = entries[kj * 128 : (kj + 1) * 128, :ENTRIES]
        by_head[:, kj, :] = dot_nt(parts[0], one) + dot_nt(parts[1], one) + dot_nt(parts[2], one)
    by_head[:, WIN, :] = jnp.full((HEADS, 128), neg, F32)
    lane = lane_ids((8, 128))
    for pair in range(HEADS // 2):
        for ki in range(WIN):
            first = pltpu.roll(by_head[2 * pair], 8 * ki, 1)
            second = pltpu.roll(by_head[2 * pair + 1], (8 * ki + LANES) % 128, 1)
            bias_t[8 * ki : 8 * ki + 8, 128 * pair : 128 * pair + 128] = jnp.where(
                lane < LANES, first, second
            )


def table_gradient(logit_sums, entries, by_head):
    lane = lane_ids((8, 128))
    for pair in range(HEADS // 2):
        for half in range(2):
            total = jnp.zeros((8, 128), F32)
            for ki in range(WIN):
                block = logit_sums[8 * ki : 8 * ki + 8, 128 * pair : 128 * pair + 128]
                own = jnp.where((lane < LANES) == (half == 0), block, 0.0)
                total = total + pltpu.roll(own, (128 - 8 * ki - LANES * half) % 128, 1)
            by_head[2 * pair + half] = total
    out = jnp.zeros((HEADS, D), F32)
    for kj in range(WIN):
        one = entries[kj * 128 : (kj + 1) * 128]
        for part in three_parts(by_head[:, kj, :]):
            out = out + dot(part, one)
    return out


def spans():
    return [slice(w * PAD, (w + 1) * PAD) for w in range(WINDOWS)]


def forward_stage(s, r):
    rows = pl.ds(pl.multiple_of(s * STRIP, 16), STRIP)
    slot = lax.rem(s, 2)
    tokens = dot(r.gather[...], raster_rows(r.image, r.halo, 0, s))
    r.tokens_all[rows] = tokens.astype(BF16)
    yield
    r.cot_all[rows] = dot(r.gather[...], raster_rows(r.cot, r.halo, SHIFT, s)).astype(BF16)
    yield
    normal_one, _ = normalize(tokens)
    first_low = (normal_one * r.gain_one[...] + r.bias_one[...]).astype(BF16)
    r.first_all[rows, :D] = first_low
    yield
    query = dot(first_low, r.w_qkv[:, :D]) + r.b_query[...]
    key = dot(first_low, r.w_qkv[:, D : 2 * D])
    value = dot(first_low, r.w_qkv[:, 2 * D :]) + r.b_value[...]
    yield
    key_labels = r.lane_labels[s].T
    logits = []
    for w, span in enumerate(spans()):
        query_low = pad_rows(query[span]).astype(BF16)
        key_low = pad_rows(key[span]).astype(BF16)
        value_low = pad_rows(value[span]).astype(BF16)
        r.qkv_win[slot, w, :, :D] = query_low
        r.qkv_win[slot, w, :, D : 2 * D] = key_low
        r.qkv_win[slot, w, :, 2 * D :] = value_low
        blocks = head_blocks(query_low, r.mask)
        logits.append(
            [dot_nt(key_low[:, 128 * g : 128 * g + 128], blocks[g])[:PAD] for g in range(2)]
        )
        yield
    turned = []
    for w in range(WINDOWS):
        same = key_labels[:PAD, w : w + 1] == r.lane_labels[s, w : w + 1, :]
        turned.append([])
        for pair in range(HEADS // 2):
            cols = slice(128 * pair, 128 * pair + 128)
            part = logits[w][pair // 2][:, 128 * (pair % 2) : 128 * (pair % 2) + 128]
            part = jnp.where(same, part * (SCALE * LOG2E) + r.bias_t[:, cols], neg)
            powers = jnp.exp2(part - jnp.max(part, 0, keepdims=True))
            attend = powers * (1.0 / jnp.sum(powers, 0, keepdims=True))
            attend_low = pad_rows(attend).astype(BF16)
            r.attend_win[slot, w, :, cols] = attend_low
            turned[w].append(turn_pair(attend_low))
        yield
    mixed_parts = []
    for w in range(WINDOWS):
        blocks = head_blocks(r.qkv_win[slot, w, :, 2 * D :], r.mask)
        mixed_parts.append(
            jnp.concatenate(
                [
                    dot(jnp.concatenate(turned[w][2 * g : 2 * g + 2], 1), blocks[g])[:PAD]
                    for g in range(2)
                ],
                1,
            )
        )
        yield
    mixed_low = jnp.concatenate(mixed_parts, 0).astype(BF16)
    r.mixed_all[rows] = mixed_low
    resid = tokens + dot(mixed_low, r.w_proj[...]) + r.b_proj[...]
    r.resid_all[rows] = resid
    for copy in early_copies(r, s):
        copy.start()
    yield


def strip_copies(s, sems, pairs):
    rows = pl.ds(pl.multiple_of(s * STRIP, 16), STRIP)
    return [pltpu.make_async_copy(a.at[rows], b.at[rows], sems.at[s, n]) for n, (a, b) in enumerate(pairs)]


def early_copies(r, s):
    return strip_copies(s, r.early_sems, ((r.tokens_all, r.tokens_out), (r.resid_all, r.resid_out)))


def late_copies(r, s):
    pairs = (r.active_all, r.active_out), (r.d_branch_all, r.d_branch_out), (r.d_qkv_all, r.d_qkv_out)
    return strip_copies(s, r.late_sems, pairs)


def backward_stage(s, r):
    rows = pl.ds(pl.multiple_of(s * STRIP, 16), STRIP)
    slot = lax.rem(s, 2)
    sums = r.sums
    resid = r.resid_all[rows]
    normal_two, recip_two = normalize(resid)
    second_low = (normal_two * r.gain_two[...] + r.bias_two[...]).astype(BF16)
    r.second_all[rows, :D] = second_low
    yield
    cot_low = r.cot_all[rows]
    d_second = jnp.zeros((STRIP, D), F32)
    for n in range(MLP // D):
        cols = slice(n * D, (n + 1) * D)
        inner = dot(second_low, r.w_up[:, cols]) + r.b_up[:, cols]
        cumulative = 0.5 * lax.erf(inner * 0.7071067811865476) + 0.5
        active_low = (inner * cumulative).astype(BF16)
        r.active_all[rows, cols] = active_low
        yield
        gauss = jnp.exp2(inner * inner * (-0.5 * LOG2E))
        slope = cumulative + inner * gauss * 0.3989422804014327
        d_inner = (dot_nt(cot_low, r.w_down[cols]) * slope).astype(BF16)
        r.d_inner_all[rows, cols] = d_inner
        yield
        d_second = d_second + dot_nt(d_inner, r.w_up[:, cols])
        yield
    cot_f32 = cot_low.astype(F32)
    d_resid = cot_f32 + norm_backward(d_second, normal_two, recip_two, r.gain_two[...])
    d_branch = d_resid.astype(BF16)
    r.d_branch_all[rows] = d_branch
    yield
    d_mixed = dot_nt(d_branch, r.w_proj[...])
    yield
    sums[0:1] += col_sum(d_second * normal_two)
    sums[1:2] += col_sum(d_second)
    sums[2:3] += col_sum(d_resid)
    sums[3:4] += col_sum(cot_f32)
    yield
    mixed_blocks = []
    d_attends = []
    for w, span in enumerate(spans()):
        blocks = head_blocks(pad_rows(d_mixed[span]).astype(BF16), r.mask)
        mixed_blocks.append(blocks)
        value_low = r.qkv_win[slot, w, :, 2 * D :]
        d_attends.append(
            [dot_nt(value_low[:, 128 * g : 128 * g + 128], blocks[g])[:PAD] for g in range(2)]
        )
        yield
    d_logits = []
    turned = []
    for w in range(WINDOWS):
        d_logits.append([])
        turned.append([])
        for pair in range(HEADS // 2):
            cols = slice(128 * pair, 128 * pair + 128)
            part = d_attends[w][pair // 2][:, 128 * (pair % 2) : 128 * (pair % 2) + 128]
            attend = r.attend_win[slot, w, :, cols].astype(F32)[:PAD]
            cross = jnp.sum(part * attend, 0, keepdims=True)
            part = attend * (part - cross)
            r.logit_sums[:, cols] += part
            low = pad_rows(part).astype(BF16)
            d_logits[w].append(low)
            turned[w].append(turn_pair(low))
        yield
    parts = []
    for w in range(WINDOWS):
        query_blocks = head_blocks(r.qkv_win[slot, w, :, :D], r.mask)
        key_blocks = head_blocks(r.qkv_win[slot, w, :, D : 2 * D], r.mask)
        d_query, d_key, d_value = [], [], []
        for g in range(2):
            two = slice(2 * g, 2 * g + 2)
            attend_low = r.attend_win[slot, w, :, 256 * g : 256 * g + 256]
            d_value.append(dot(attend_low, mixed_blocks[w][g])[:PAD])
            d_key.append(dot(jnp.concatenate(d_logits[w][two], 1), query_blocks[g])[:PAD] * SCALE)
            d_query.append(dot(jnp.concatenate(turned[w][two], 1), key_blocks[g])[:PAD] * SCALE)
        parts.append(jnp.concatenate(d_query + d_key + d_value, 1))
        yield
    d_qkv = jnp.concatenate(parts, 0).astype(BF16)
    r.d_qkv_all[rows] = d_qkv
    for copy in late_copies(r, s):
        copy.start()
    yield


WEAVE = (-0.03, 0.144, 0.165, 0.354, 0.445)


def run(*stages):
    order = []
    for n, stage in enumerate(stages):
        count = PIECES[stage.__name__]
        places = (np.arange(count) + 0.5) / count
        if n:
            places = np.interp(places, np.linspace(0.0, 1.0, len(WEAVE)), WEAVE)
        order += [(place, n) for place in places]
    for _, n in sorted(order):
        next(stages[n])
    for stage in stages:
        assert next(stage, None) is None


PIECES = {"forward_stage": 5 + 3 * WINDOWS, "backward_stage": 1 + 3 * (MLP // D) + 3 + 3 * WINDOWS + 1}


def down_rows(n):
    return DOWN[n // 2] + (n % 2) * D


def finish(r):
    core = lax.rem(lax.axis_index("dp"), 2)
    grads = r.grads

    def put(start, rows):
        grads[start : start + rows.shape[0]] = rows
        r.grads_low[start : start + rows.shape[0]] = rows.astype(BF16)

    def hand_over(n, start, count):
        span = pl.ds(start, count)
        kept = pl.ds(pl.multiple_of(core * HALF + start, 16), count)
        sent = pl.ds(pl.multiple_of((1 - core) * HALF + start, 16), count)
        copies = [
            pltpu.make_async_copy(grads.at[kept], r.keep.at[span], r.sems.at[2 * n]),
            pltpu.make_async_copy(r.grads_low.at[sent], r.send.at[span], r.sems.at[2 * n + 1]),
        ]
        for copy in copies:
            copy.start()
        return copies

    product = dot_tn(r.first_all[:, : D + 8], r.d_qkv_all[...])
    sums = product[D : D + 8]
    for n in range(3):
        put(QKV + n * D, product[:D, n * D : (n + 1) * D])
    put(PROJ, dot_tn(r.mixed_all[...], r.d_branch_all[...]))
    bias_parts = dot_nt(jnp.concatenate(three_parts(sums), 0), r.w_qkv[...])
    bias_grad = bias_parts[0:1] + bias_parts[8:9] + bias_parts[16:17]
    cross = jnp.zeros((D, 128), F32)
    for n in range(0, 3 * D, 128):
        cross = cross + product[:D, n : n + 128] * r.w_qkv[:, n : n + 128].astype(F32)
    gain_grad = (col_sum(cross.T) - r.bias_one[...] * bias_grad) / r.gain_one[...]
    small = [sums[0:1, :D], sums[0:1, 2 * D :], gain_grad, bias_grad, jnp.zeros((20, D), F32)]
    product = dot_tn(r.second_all[:, : D + 8], r.d_inner_all[...])
    for n in range(MLP // D):
        put(UP + n * D, product[:D, n * D : (n + 1) * D])
    ups = [product[D : D + 1, n * D : (n + 1) * D] for n in range(MLP // D)]
    put(SMALL_ONE, jnp.concatenate([r.sums[0:4]] + ups + [jnp.zeros((24, D), F32)], 0))
    put(SMALL_TWO, jnp.concatenate([table_gradient(r.logit_sums, r.entries, r.by_head)] + small, 0))
    copies = hand_over(0, UP, MLP) + hand_over(1, SMALL_ONE, 32)
    product = dot_tn(r.cot_all[...], r.active_all[...])
    for n in range(MLP // D):
        put(down_rows(n), product[:, n * D : (n + 1) * D])
    copies += hand_over(2, DOWN[0], 2 * D)
    for n in range(STRIPS):
        copies += early_copies(r, n) + late_copies(r, n)
    for copy in copies:
        copy.wait()


class Refs:
    def __init__(self, names, refs):
        self.__dict__.update(zip(names, refs))


INPUTS = [
    "image", "cot", "gather", "mask", "entries", "w_qkv", "w_proj", "w_up", "w_down",
    "halo", "regions", "regions_halo", "spread", "spread_rows", "table",
    "gain_one", "bias_one", "b_query", "b_value", "b_proj", "gain_two", "bias_two", "b_up",
]
NAMES = [name + "_in" for name in INPUTS] + [
    "keep", "send", "tokens_out", "resid_out", "active_out", "d_branch_out", "d_qkv_out",
    "lane_labels", "by_head", "bias_t", "logit_sums", "qkv_win", "attend_win", "sums",
    "first_all", "cot_all", "mixed_all", "second_all", "active_all", "d_inner_all", "d_branch_all", "d_qkv_all",
    "tokens_all", "resid_all", "grads", "grads_low", "sems", "in_sems", "early_sems", "late_sems",
] + INPUTS


LATE_WAITS = 8


def input_copies(r):
    top = WIN + SHIFT
    last = [("w_up", None), ("w_down", None), ("image", slice(top, COLS)), ("cot", slice(top, COLS))]
    large = ["entries", "gather", "image", "w_qkv", "mask", "cot", "w_proj", "halo"]
    names = [name for name in INPUTS if name not in large + ["w_up", "w_down"]] + large
    first = [(name, slice(0, top) if name in ("image", "cot") else None) for name in names]
    copies = []
    for n, (name, rows) in enumerate(first + last):
        source, place = getattr(r, name + "_in"), getattr(r, name)
        if rows is not None:
            source, place = source.at[rows], place.at[rows]
        copies.append(pltpu.make_async_copy(source, place, r.in_sems.at[n]))
    return copies[: len(first)], copies[len(first) :]


def put_labels(r, n, part):
    row = jnp.sum(part * r.spread_rows[...], 0, keepdims=True)
    windows = [row[:, 128 * w : 128 * w + 128] for w in range(WINDOWS)]
    r.lane_labels[n] = jnp.concatenate(windows + [jnp.zeros((2, 128), F32)], 0)


def grads_kernel(*refs):
    r = Refs(NAMES, refs)
    s = pl.program_id(0)

    @pl.when(s == 0)
    def _():
        first, later = input_copies(r)
        for copy in first:
            copy.start()
        r.logit_sums[...] = jnp.zeros_like(r.logit_sums)
        r.sums[...] = jnp.zeros_like(r.sums)
        one = (lane_ids((TOTAL, 128)) == 0).astype(F32).astype(BF16)
        r.first_all[:, D:] = one
        r.second_all[:, D:] = one
        for copy in first[: 1 - LATE_WAITS]:
            copy.wait()
        own = dot(r.regions[...].astype(F32).astype(BF16), r.spread[...])
        for n in range(STRIPS - 1):
            put_labels(r, n, own[n * WIN + SHIFT : (n + 1) * WIN + SHIFT])
        below = dot(r.regions_halo[...], r.spread[...])
        put_labels(r, STRIPS - 1, jnp.concatenate([own[COLS - (WIN - SHIFT) :], below], 0))
        build_bias(r.table[...], r.entries, r.by_head, r.bias_t)
        for copy in first[1 - LATE_WAITS :]:
            copy.wait()
        for copy in later:
            copy.start()
        run(forward_stage(s, r))
        for copy in later:
            copy.wait()

    @pl.when((s > 0) & (s < STRIPS))
    def _():
        run(backward_stage(s - 1, r), forward_stage(s, r))

    @pl.when(s == STRIPS)
    def _():
        run(backward_stage(s - 1, r))
        finish(r)


def output_strip(active, resid, w_down, b_down, scatter):
    result = resid[...] + b_down[...] + dot(active[...], w_down[...])
    return dot(scatter[...], result.astype(BF16)).astype(BF16)


def image_strip(d_qkv, d_branch, tokens, w_qkv, gain, scatter):
    normal, recip_dev = normalize(tokens[...].astype(F32))
    d_first = dot_nt(d_qkv[...], w_qkv[...])
    grad = d_branch[...].astype(F32) + norm_backward(d_first, normal, recip_dev, gain[...])
    return dot(scatter[...], grad.astype(BF16)).astype(BF16)


there = pl.BlockSpec(memory_space=pl.ANY)


def whole(shape):
    return pl.BlockSpec(shape, lambda s: (0,) * len(shape))


def once(shape):
    return pl.BlockSpec(shape, lambda s: (0,) * len(shape), pipeline_mode=pl.Buffered(1))


def strips(shape):
    return pl.BlockSpec(shape, lambda s: (s,) + (0,) * (len(shape) - 1))


def struct(shape, dtype):
    return jax.ShapeDtypeStruct(shape, dtype)


def params(mebibytes):
    return pltpu.CompilerParams(
        vmem_limit_bytes=mebibytes * 1024 * 1024, dimension_semantics=("arbitrary",)
    )


def pack_kernel(image, cot, regions, rows, labels):
    rows[0:SHIFT] = image[...]
    rows[SHIFT:] = cot[...]
    labels[...] = regions[0:SHIFT].astype(F32).astype(BF16)


def pack_first_rows(image, cot, regions):
    return pl.pallas_call(
        pack_kernel,
        grid=(1,),
        in_specs=[whole((SHIFT, COLS, D)), whole((SHIFT, COLS, D)), whole(regions.shape)],
        out_specs=[whole((2 * SHIFT, COLS, D)), whole((SHIFT, COLS))],
        out_shape=[pltpu.VMEM((2 * SHIFT, COLS, D), BF16), pltpu.VMEM((SHIFT, COLS), BF16)],
        compiler_params=params(62),
        name="pack_first_rows",
    )(image, cot, regions)


def run_grads(*args):
    return pl.pallas_call(
        grads_kernel,
        grid=(STRIPS + 1,),
        in_specs=[there] * len(args),
        out_specs=[there] * 7,
        out_shape=[
            pltpu.VMEM((HALF, D), F32),
            pltpu.VMEM((HALF, D), BF16),
            struct((TOTAL, D), BF16),
            struct((TOTAL, D), F32),
            struct((TOTAL, MLP), BF16),
            struct((TOTAL, D), BF16),
            struct((TOTAL, 3 * D), BF16),
        ],
        scratch_shapes=[
            pltpu.VMEM((STRIPS, 8, 128), F32),
            pltpu.VMEM((HEADS, 8, 128), F32),
            pltpu.VMEM((PAD, HEADS * LANES), F32),
            pltpu.VMEM((PAD, HEADS * LANES), F32),
            pltpu.VMEM((2, WINDOWS, LANES, 3 * D), BF16),
            pltpu.VMEM((2, WINDOWS, LANES, HEADS * LANES), BF16),
            pltpu.VMEM((8, D), F32),
            pltpu.VMEM((TOTAL, D + 128), BF16),
            pltpu.VMEM((TOTAL, D), BF16),
            pltpu.VMEM((TOTAL, D), BF16),
            pltpu.VMEM((TOTAL, D + 128), BF16),
            pltpu.VMEM((TOTAL, MLP), BF16),
            pltpu.VMEM((TOTAL, MLP), BF16),
            pltpu.VMEM((TOTAL, D), BF16),
            pltpu.VMEM((TOTAL, 3 * D), BF16),
            pltpu.VMEM((TOTAL, D), BF16),
            pltpu.VMEM((TOTAL, D), F32),
            pltpu.VMEM((2 * HALF, D), F32),
            pltpu.VMEM((2 * HALF, D), BF16),
            pltpu.SemaphoreType.DMA((6,)),
            pltpu.SemaphoreType.DMA((len(INPUTS) + 2,)),
            pltpu.SemaphoreType.DMA((STRIPS, 2)),
            pltpu.SemaphoreType.DMA((STRIPS, 3)),
        ]
        + [pltpu.VMEM(a.shape, a.dtype) for a in args],
        compiler_params=params(58),
        cost_estimate=pl.CostEstimate(
            flops=2 * TOTAL * 10 * D * MLP, bytes_accessed=20_000_000, transcendentals=0
        ),
        name="all_gradients",
    )(*args)


def run_field(strip, name, which, blocks, others, field=None, tails=None):
    lower = field is None
    first = FIELD_STEPS if lower else 0
    given = [a for a in (field, tails) if a is not None]
    inputs = len(blocks) + len(others)
    shapes = [struct((COLS, COLS, D), BF16)] + [struct((2, SENT, COLS, D), BF16)] * lower

    def kernel(*refs):
        out = refs[inputs + len(given)]
        below = refs[inputs + len(given) + 1] if lower else None
        put_rows(strip(*refs[:inputs]), first, which, out, below, *refs[-2:])

    return pl.pallas_call(
        kernel,
        grid=(FIELD_STEPS,),
        in_specs=[pl.BlockSpec((STRIP, a.shape[1]), lambda t: (first + t, 0)) for a in blocks]
        + [whole(a.shape) for a in others]
        + [there] * len(given),
        out_specs=[there] * len(shapes),
        out_shape=shapes,
        scratch_shapes=[pltpu.VMEM((2, WIN, COLS, D), BF16), pltpu.SemaphoreType.DMA((3,))],
        input_output_aliases={inputs: 1 if lower else 0} if given else {},
        compiler_params=params(60),
        cost_estimate=pl.CostEstimate(
            flops=2 * TOTAL * 4 * D * D, bytes_accessed=9_000_000, transcendentals=0
        ),
        name=name,
    )(*blocks, *others, *given)


def unpack_half(half, rows, w_up, w_down, w_proj, w_qkv, stage, sems):
    def down(first):
        for n in range(2):
            stage[n * D : (n + 1) * D, :D] = rows[first + n * D : first + (n + 1) * D].astype(F32).T
        at = pl.ds(half * 2 * D, 2 * D)
        return pltpu.make_async_copy(stage.at[pl.ds(0, 2 * D), pl.ds(0, D)], w_down.at[at], sems.at[0])

    def wide(out, first, count, at, sem):
        for n in range(count):
            part = rows[first + n * D : first + (n + 1) * D].astype(F32)
            stage[at : at + D, n * D : (n + 1) * D] = part
        return pltpu.make_async_copy(stage.at[pl.ds(at, D), pl.ds(0, count * D)], out, sems.at[sem])

    copies = []
    if half == 0:
        copies.append(wide(w_up, UP, MLP // D, 2 * D, 1))
        copies[-1].start()
        copies.append(down(DOWN[0]))
        copies[-1].start()
    else:
        copies.append(wide(w_qkv, QKV - HALF, 3, 2 * D, 1))
        copies[-1].start()
        copies.append(wide(w_proj, PROJ - HALF, 1, 3 * D, 2))
        copies[-1].start()
        copies.append(down(DOWN[1] - HALF))
        copies[-1].start()
    for copy in copies:
        copy.wait()


def unpack_first_kernel(own, *refs):
    core = lax.rem(lax.axis_index("dp"), 2)
    for half in range(2):

        @pl.when(core == half)
        def _():
            unpack_half(half, own, *refs)


def unpack_second_kernel(
    other, own, in_up, in_down, in_proj, in_qkv, w_up, w_down, w_proj, w_qkv,
    gain_one, bias_one, b_query, b_value, table, b_proj, gain_two, bias_two, b_up, b_down, stage, sems,
):
    core = lax.rem(lax.axis_index("dp"), 2)
    for half in range(2):

        @pl.when(core != half)
        def _():
            unpack_half(half, other, w_up, w_down, w_proj, w_qkv, stage, sems)

    small = slice(SMALL_ONE, HALF)
    mine, others = own[small].astype(F32), other[small].astype(F32)
    first = jnp.where(core == 0, mine, others)
    second = jnp.where(core == 0, others, mine)
    for n, out in enumerate((gain_two, bias_two, b_proj, b_down)):
        out[...] = first[n : n + 1]
    for n in range(MLP // D):
        b_up[:, n * D : (n + 1) * D] = first[4 + n : 5 + n]
    table[...] = second[:HEADS, :ENTRIES]
    for n, out in enumerate((b_query, b_value, gain_one, bias_one)):
        out[...] = second[HEADS + n : HEADS + n + 1]


LARGE = ((D, MLP), (MLP, D), (D, D), (D, 3 * D))
UNPACK_SCRATCH = [pltpu.VMEM((4 * D, MLP), F32), pltpu.SemaphoreType.DMA((3,))]
def unpack_first(own):
    return pl.pallas_call(
        unpack_first_kernel,
        grid=(1,),
        in_specs=[whole(own.shape)],
        out_specs=[there] * 4,
        out_shape=[struct(shape, F32) for shape in LARGE],
        scratch_shapes=UNPACK_SCRATCH,
        compiler_params=params(24),
        cost_estimate=pl.CostEstimate(flops=0, bytes_accessed=2_400_000, transcendentals=0),
        name="unpack_own_half",
    )(own)


def unpack_second(other, own, large):
    one, four = (1, D), (1, MLP)
    shapes = [one, one, one, one, (HEADS, ENTRIES), one, one, one, four, one]
    out = pl.pallas_call(
        unpack_second_kernel,
        grid=(1,),
        in_specs=[whole(other.shape), whole(own.shape)] + [there] * 4,
        out_specs=[there] * 4 + [whole(shape) for shape in shapes],
        out_shape=[struct(shape, F32) for shape in LARGE] + [struct(shape, F32) for shape in shapes],
        scratch_shapes=UNPACK_SCRATCH,
        input_output_aliases={2: 0, 3: 1, 4: 2, 5: 3},
        compiler_params=params(24),
        name="unpack_other_half",
    )(other, own, *large)
    w_up, w_down, w_proj, w_qkv = out[:4]
    gain_one, bias_one, b_query, b_value, table, b_proj, gain_two, bias_two, b_up, b_down = out[4:]
    return (
        gain_one[0], bias_one[0], w_qkv, b_query[0], b_value[0], table.T, w_proj, b_proj[0],
        gain_two[0], bias_two[0], w_up, b_up[0], w_down, b_down[0],
    )


def coords(index):
    dp, space = divmod(index, 32)
    return {"c": dp % 2, "y": dp // 2 + 2 * ((space // 4) % 2), "x": space % 4, "z": space // 8}


def index_of(c, y, x, z):
    return ((y % 2) * 2 + c) * 32 + z * 8 + (y // 2) * 4 + x


DISTANCES = (2, 1, 3)
STAGES = (("y", "x"), ("x", "z"), ("z", "y"))


def other_core():
    return [(i, index_of(**(coords(i) | {"c": 1 - i // 32 % 2}))) for i in range(128)]


def around(stage, distance):
    out = []
    for i in range(128):
        at = coords(i)
        axis = stage[at["c"]]
        out.append((i, index_of(**(at | {axis: (at[axis] + distance) % 4}))))
    return out


def take(rows, start, count):
    return lax.dynamic_slice_in_dim(rows, start, count, 0)


def sum_everywhere(mine, got_core, at, pieces):
    made = {}
    left = list(pieces)

    def exchange(stage, sends, own):
        nonlocal made
        ahead, beside = left.pop(0)
        early = ahead(made)
        got = [lax.ppermute(sends[d], AXES, around(stage, d)) for d in DISTANCES]
        made, own = lax.optimization_barrier((made, own))
        made = made | beside(made)
        got, made, early, own = lax.optimization_barrier((got, made, early, own))
        made = made | early
        return dict(zip(DISTANCES, got)), own

    def place(stage):
        return jnp.where(at["c"] == 0, at[stage[0]], at[stage[1]])

    stage = STAGES[0]
    here = place(stage)
    count = mine.shape[0] // 4

    def part(which):
        start = which * count
        return take(mine, start, count) + take(got_core, start, count).astype(F32)

    sends = {d: part((here + d) % 4).astype(BF16) for d in DISTANCES}
    got, rows = exchange(stage, sends, part(here))
    for d in DISTANCES:
        rows = rows + got[d].astype(F32)
    low = rows.astype(BF16)
    for stage in STAGES[1:]:
        got, low = exchange(stage, {d: low for d in DISTANCES}, low)
        pairs = low.astype(F32) + got[2].astype(F32), got[1].astype(F32) + got[3].astype(F32)
        low = (pairs[0] + pairs[1]).astype(BF16)
    ahead, beside = left.pop(0)
    parts = {0: low} | {d: lax.ppermute(low, AXES, around(STAGES[0], d)) for d in (1, 2, 3)}
    others = {d: lax.ppermute(rows, AXES, other_core()) for d, rows in parts.items()}
    made = made | beside(made)

    def assemble(parts, here):
        out = jnp.zeros((4 * count, D), BF16)
        for d, rows in parts.items():
            out = lax.dynamic_update_slice(out, rows, ((here - d) % 4 * count, 0))
        return out

    there_axis = jnp.where(at["c"] == 0, at[STAGES[0][1]], at[STAGES[0][0]])
    own = assemble(parts, here)
    large = unpack_first(own)
    others, large, made = lax.optimization_barrier((others, large, made))
    return own, assemble(others, there_axis), large, made


def body(
    image_in, cotangent, regions, first_gain, first_bias, qkv_weight, query_bias, value_bias,
    position_table, proj_weight, proj_bias, second_gain, second_bias, up_weight, up_bias,
    down_weight, down_bias,
):
    many = lax.axis_size("dp") * lax.axis_size("space") == 128
    me = lax.axis_index(AXES)
    at = coords(me)
    first_rows = pack_first_rows(image_in, cotangent, regions)
    halo, regions_halo = from_behind(first_rows, "space", -1)
    gather = gather_matrix()
    spread, spread_rows = label_matrices()
    entries = jnp.asarray(entry_matrix(), BF16)
    mask = jnp.asarray(head_mask(), BF16)
    scatter = jnp.asarray(gather.T, BF16)
    mine, send, tokens, resid, active, d_branch, d_qkv = run_grads(
        image_in, cotangent, jnp.asarray(gather, BF16), mask, entries, qkv_weight, proj_weight, up_weight, down_weight,
        halo, regions, regions_halo, jnp.asarray(spread, BF16), jnp.asarray(spread_rows), position_table.T,
        first_gain[None], first_bias[None], query_bias[None], value_bias[None], proj_bias[None],
        second_gain[None], second_bias[None], up_bias[None],
    )
    if many:
        got = lax.ppermute(send, AXES, other_core())

    def block_output(*given):
        others = (down_weight, down_bias[None], scatter)
        return run_field(output_strip, "block_output", 0, (active, resid), others, *given)

    def image_gradient(*given):
        others = (qkv_weight, first_gain[None], scatter)
        return run_field(image_strip, "image_gradient", 1, (d_qkv, d_branch, tokens), others, *given)

    def lower_out(made):
        out, tails = block_output()
        return {"out": out, "tails": tails}

    def lower_image(made):
        image, tails = image_gradient(None, made["tails"])
        return {"image": image, "tails": tails}

    def upper_out(made):
        return made | {"out": block_output(made["out"])[0]}

    def return_rows(made):
        return {"returned": from_behind(made["tails"], "space", 1)}

    def upper_image(made):
        return made | {"image": image_gradient(made["image"])[0]}

    def nothing(made):
        return {}

    def fields(made):
        first, at = made["returned"][:, SENT - SHIFT :], (0, 0, 0)
        return {
            "out": lax.dynamic_update_slice(made["out"], first[0], at),
            "image": lax.dynamic_update_slice(made["image"], first[1], at),
        }

    def upper_image_and_out(made):
        made = made | upper_image(made)
        return made | fields(made)

    pieces = [(nothing, lower_out), (nothing, lower_image), (return_rows, upper_out), (nothing, upper_image_and_out)]
    if many:
        own, other, large, made = sum_everywhere(mine, got, at, pieces)
    else:
        made = {}
        for ahead, beside in pieces:
            made = made | ahead(made) | beside(made)
        own, other = mine.astype(BF16), send
        large = unpack_first(own)
    return (made["out"], made["image"]) + unpack_second(other, own, large)


def solution(mesh):
    tokens = P(AXES, None, None)
    return jax.shard_map(
        body,
        mesh=mesh,
        in_specs=(tokens, tokens, P(AXES, None)) + (P(),) * 14,
        out_specs=(tokens, tokens) + (P(),) * 14,
        check_vma=False,
    )
```

```python
import functools
import math

import jax
import jax.numpy as jnp
import numpy as np
from jax import lax
from jax.experimental import pallas as pl
from jax.experimental.pallas import tpu as pltpu
from jax.sharding import PartitionSpec as P

WIN = 7
SHIFT = 3
HEADS = 8
TOKENS = WIN * WIN
PAD = 56
LANES = 64
ENTRIES = (2 * WIN - 1) * (2 * WIN - 1)
COLS = 42
WINDOWS = COLS // WIN
STRIP = WINDOWS * PAD
STRIPS = COLS // WIN
SENT = 5
FIELD_STEPS = STRIPS // 2
TOTAL = STRIPS * STRIP
ROW = 48
D = 256
MLP = 1024
BF16 = jnp.bfloat16
F32 = jnp.float32
epsilon = 1e-05
neg = -1000000000.0
AXES = ("dp", "space")
SCALE = 1.0 / math.sqrt(D // HEADS)
LOG2E = 1.4426950408889634
UP = 0
HALF = MLP + 2 * D + 32
PROJ = HALF
QKV = PROJ + D
DOWN = (MLP, HALF + MLP)
SMALL_ONE = MLP + 2 * D
SMALL_TWO = HALF + SMALL_ONE
assert QKV + 3 * D == DOWN[1]


def from_behind(block, axis, distance):
    devices = range(lax.axis_size(axis))
    route = [((i - distance) % len(devices), i) for i in devices]
    return lax.ppermute(block, axis, route)


def place(i, j):
    return 8 * i + j


def gather_matrix():
    out = np.zeros((STRIP, WIN * ROW), np.float32)
    for w in range(WINDOWS):
        for i in range(WIN):
            for j in range(WIN):
                out[w * PAD + place(i, j), i * ROW + (w * WIN + j + SHIFT) % COLS] = 1.0
    return out


def label_matrices():
    spread = np.zeros((COLS, WINDOWS * 2 * LANES), np.float32)
    rows = np.zeros((WIN, WINDOWS * 2 * LANES), np.float32)
    for w in range(WINDOWS):
        for copy in range(2):
            for i in range(WIN):
                for j in range(WIN):
                    col = (w * 2 + copy) * LANES + place(i, j)
                    spread[(w * WIN + j + SHIFT) % COLS, col] = 1.0
                    rows[i, col] = 1.0
    return spread, rows


def entry_matrix():
    out = np.zeros((WIN * 128, D), np.float32)
    for kj in range(WIN):
        for di in range(1 - WIN, WIN):
            for qj in range(WIN):
                entry = (di + WIN - 1) * (2 * WIN - 1) + qj - kj + WIN - 1
                out[kj * 128 + (8 * di + qj) % 128, entry] = 1.0
    return out


def head_mask():
    return (np.arange(4 * LANES)[:, None] // LANES == np.arange(128)[None] // 32).astype(np.float32)


def dot(a, b):
    return jnp.dot(a, b, preferred_element_type=F32)


def dot_nt(a, b):
    return lax.dot_general(a, b, (((1,), (1,)), ((), ())), preferred_element_type=F32)


def dot_tn(a, b):
    return lax.dot_general(a, b, (((0,), (0,)), ((), ())), preferred_element_type=F32)


def normalize(values):
    center = values - jnp.mean(values, -1, keepdims=True)
    variance = jnp.mean(center * center, -1, keepdims=True)
    recip_dev = lax.rsqrt(variance + epsilon)
    return center * recip_dev, recip_dev


def norm_backward(upstream, normal_part, recip_dev, gain):
    scaled = upstream * gain
    inner_mean = jnp.mean(scaled, -1, keepdims=True)
    cross_mean = jnp.mean(scaled * normal_part, -1, keepdims=True)
    return recip_dev * (scaled - inner_mean - normal_part * cross_mean)


def col_sum(values):
    return jnp.sum(values, 0, keepdims=True)


def raster_rows(ref, halo, first, s):
    last = s == STRIPS - 1
    blank = jnp.zeros((ROW - COLS, D), BF16)
    rows = []
    for i in range(WIN):
        g = s * WIN + i + SHIFT
        if i < WIN - SHIFT:
            value = ref[g]
        else:
            value = jnp.where(
                last, halo[first + i - (WIN - SHIFT)], ref[jnp.minimum(g, COLS - 1)]
            )
        rows += [value, blank]
    return jnp.concatenate(rows, 0)


def put_rows(raster, first, which, out, tails, stage, sems):
    t = pl.program_id(0)
    slot = lax.rem(t, 2)

    def whole_strip(n):
        return pltpu.make_async_copy(
            stage.at[lax.rem(n, 2)], out.at[pl.ds((first + n) * WIN + SHIFT, WIN)], sems.at[lax.rem(n, 2)]
        )

    @pl.when(t >= 2)
    def _():
        whole_strip(t - 2).wait()

    for i in range(WIN):
        stage[slot, i] = raster[i * ROW : i * ROW + COLS]

    @pl.when(first + t < STRIPS - 1)
    def _():
        whole_strip(t).start()

    @pl.when(t == FIELD_STEPS - 1)
    def _():
        if tails is None:
            whole_strip(t - 1).wait()
            whole_strip(t).wait()
        else:
            own = pltpu.make_async_copy(
                stage.at[slot, 0 : WIN - SHIFT], out.at[COLS - (WIN - SHIFT) : COLS], sems.at[slot]
            )
            below = pltpu.make_async_copy(stage.at[slot, WIN - SENT : WIN], tails.at[which], sems.at[2])
            own.start()
            below.start()
            whole_strip(t - 1).wait()
            own.wait()
            below.wait()


def pad_rows(values):
    return jnp.concatenate([values, jnp.zeros((LANES - PAD,) + values.shape[1:], values.dtype)], 0)


def head_blocks(low, mask):
    return [jnp.concatenate([low[:, g : g + 128]] * 4, 0) * mask[...] for g in (0, 128)]


def turn_pair(values):
    turned = values.T
    return jnp.concatenate([turned[:LANES], turned[LANES:]], 1)


def three_parts(values):
    high = values.astype(BF16)
    rest = values - high.astype(F32)
    middle = rest.astype(BF16)
    return high, middle, (rest - middle.astype(F32)).astype(BF16)


def lane_ids(shape):
    return lax.broadcasted_iota(jnp.int32, shape, 1)


def build_bias(table, entries, by_head, bias_t):
    parts = three_parts(table * LOG2E)
    for kj in range(WIN):
        one = entries[kj * 128 : (kj + 1) * 128, :ENTRIES]
        by_head[:, kj, :] = dot_nt(parts[0], one) + dot_nt(parts[1], one) + dot_nt(parts[2], one)
    by_head[:, WIN, :] = jnp.full((HEADS, 128), neg, F32)
    lane = lane_ids((8, 128))
    for pair in range(HEADS // 2):
        for ki in range(WIN):
            first = pltpu.roll(by_head[2 * pair], 8 * ki, 1)
            second = pltpu.roll(by_head[2 * pair + 1], (8 * ki + LANES) % 128, 1)
            bias_t[8 * ki : 8 * ki + 8, 128 * pair : 128 * pair + 128] = jnp.where(
                lane < LANES, first, second
            )


def table_gradient(logit_sums, entries, by_head):
    lane = lane_ids((8, 128))
    for pair in range(HEADS // 2):
        for half in range(2):
            total = jnp.zeros((8, 128), F32)
            for ki in range(WIN):
                block = logit_sums[8 * ki : 8 * ki + 8, 128 * pair : 128 * pair + 128]
                own = jnp.where((lane < LANES) == (half == 0), block, 0.0)
                total = total + pltpu.roll(own, (128 - 8 * ki - LANES * half) % 128, 1)
            by_head[2 * pair + half] = total
    out = jnp.zeros((HEADS, D), F32)
    for kj in range(WIN):
        one = entries[kj * 128 : (kj + 1) * 128]
        for part in three_parts(by_head[:, kj, :]):
            out = out + dot(part, one)
    return out


def spans():
    return [slice(w * PAD, (w + 1) * PAD) for w in range(WINDOWS)]


def forward_stage(s, r):
    rows = pl.ds(pl.multiple_of(s * STRIP, 16), STRIP)
    slot = lax.rem(s, 2)
    tokens = dot(r.gather[...], raster_rows(r.image, r.halo, 0, s))
    r.tokens_all[rows] = tokens.astype(BF16)
    yield
    r.cot_all[rows] = dot(r.gather[...], raster_rows(r.cot, r.halo, SHIFT, s)).astype(BF16)
    yield
    normal_one, _ = normalize(tokens)
    first_low = (normal_one * r.gain_one[...] + r.bias_one[...]).astype(BF16)
    r.first_all[rows, :D] = first_low
    yield
    query = dot(first_low, r.w_qkv[:, :D]) + r.b_query[...]
    key = dot(first_low, r.w_qkv[:, D : 2 * D])
    value = dot(first_low, r.w_qkv[:, 2 * D :]) + r.b_value[...]
    yield
    key_labels = r.lane_labels[s].T
    logits = []
    for w, span in enumerate(spans()):
        query_low = pad_rows(query[span]).astype(BF16)
        key_low = pad_rows(key[span]).astype(BF16)
        value_low = pad_rows(value[span]).astype(BF16)
        r.qkv_win[slot, w, :, :D] = query_low
        r.qkv_win[slot, w, :, D : 2 * D] = key_low
        r.qkv_win[slot, w, :, 2 * D :] = value_low
        blocks = head_blocks(query_low, r.mask)
        logits.append(
            [dot_nt(key_low[:, 128 * g : 128 * g + 128], blocks[g])[:PAD] for g in range(2)]
        )
        yield
    turned = []
    for w in range(WINDOWS):
        same = key_labels[:PAD, w : w + 1] == r.lane_labels[s, w : w + 1, :]
        turned.append([])
        for pair in range(HEADS // 2):
            cols = slice(128 * pair, 128 * pair + 128)
            part = logits[w][pair // 2][:, 128 * (pair % 2) : 128 * (pair % 2) + 128]
            part = jnp.where(same, part * (SCALE * LOG2E) + r.bias_t[:, cols], neg)
            powers = jnp.exp2(part - jnp.max(part, 0, keepdims=True))
            attend = powers * (1.0 / jnp.sum(powers, 0, keepdims=True))
            attend_low = pad_rows(attend).astype(BF16)
            r.attend_win[slot, w, :, cols] = attend_low
            turned[w].append(turn_pair(attend_low))
        yield
    mixed_parts = []
    for w in range(WINDOWS):
        blocks = head_blocks(r.qkv_win[slot, w, :, 2 * D :], r.mask)
        mixed_parts.append(
            jnp.concatenate(
                [
                    dot(jnp.concatenate(turned[w][2 * g : 2 * g + 2], 1), blocks[g])[:PAD]
                    for g in range(2)
                ],
                1,
            )
        )
        yield
    mixed_low = jnp.concatenate(mixed_parts, 0).astype(BF16)
    r.mixed_all[rows] = mixed_low
    resid = tokens + dot(mixed_low, r.w_proj[...]) + r.b_proj[...]
    r.resid_all[rows] = resid
    for copy in early_copies(r, s):
        copy.start()
    yield


def strip_copies(s, sems, pairs):
    rows = pl.ds(pl.multiple_of(s * STRIP, 16), STRIP)
    return [pltpu.make_async_copy(a.at[rows], b.at[rows], sems.at[s, n]) for n, (a, b) in enumerate(pairs)]


def early_copies(r, s):
    return strip_copies(s, r.early_sems, ((r.tokens_all, r.tokens_out), (r.resid_all, r.resid_out)))


def late_copies(r, s):
    pairs = (r.active_all, r.active_out), (r.d_branch_all, r.d_branch_out), (r.d_qkv_all, r.d_qkv_out)
    return strip_copies(s, r.late_sems, pairs)


def backward_stage(s, r):
    rows = pl.ds(pl.multiple_of(s * STRIP, 16), STRIP)
    slot = lax.rem(s, 2)
    sums = r.sums
    resid = r.resid_all[rows]
    normal_two, recip_two = normalize(resid)
    second_low = (normal_two * r.gain_two[...] + r.bias_two[...]).astype(BF16)
    r.second_all[rows, :D] = second_low
    yield
    cot_low = r.cot_all[rows]
    d_second = jnp.zeros((STRIP, D), F32)
    for n in range(MLP // D):
        cols = slice(n * D, (n + 1) * D)
        inner = dot(second_low, r.w_up[:, cols]) + r.b_up[:, cols]
        cumulative = lax.erf(inner * 0.7071067811865476) + 1.0
        active_low = (inner * cumulative).astype(BF16)
        r.active_all[rows, cols] = active_low
        yield
        gauss = jnp.exp2(inner * inner * (-0.5 * LOG2E))
        slope = cumulative + inner * gauss * 0.7978845608028654
        d_inner = (dot_nt(cot_low, r.w_down[cols]) * slope).astype(BF16)
        r.d_inner_all[rows, cols] = d_inner
        yield
        d_second = d_second + dot_nt(d_inner, r.w_up[:, cols])
        yield
    cot_f32 = cot_low.astype(F32)
    d_resid = cot_f32 + norm_backward(d_second, normal_two, recip_two, r.gain_two[...])
    d_branch = d_resid.astype(BF16)
    r.d_branch_all[rows] = d_branch
    yield
    d_mixed = dot_nt(d_branch, r.w_proj[...])
    yield
    sums[0:1] += col_sum(d_second * normal_two)
    sums[1:2] += col_sum(d_second)
    sums[2:3] += col_sum(d_resid)
    sums[3:4] += col_sum(cot_f32)
    yield
    mixed_blocks = []
    d_attends = []
    for w, span in enumerate(spans()):
        blocks = head_blocks(pad_rows(d_mixed[span]).astype(BF16), r.mask)
        mixed_blocks.append(blocks)
        value_low = r.qkv_win[slot, w, :, 2 * D :]
        d_attends.append(
            [dot_nt(value_low[:, 128 * g : 128 * g + 128], blocks[g])[:PAD] for g in range(2)]
        )
        yield
    d_logits = []
    turned = []
    for w in range(WINDOWS):
        d_logits.append([])
        turned.append([])
        for pair in range(HEADS // 2):
            cols = slice(128 * pair, 128 * pair + 128)
            part = d_attends[w][pair // 2][:, 128 * (pair % 2) : 128 * (pair % 2) + 128]
            attend = r.attend_win[slot, w, :, cols].astype(F32)[:PAD]
            cross = jnp.sum(part * attend, 0, keepdims=True)
            part = attend * (part - cross)
            r.logit_sums[:, cols] += part
            low = pad_rows(part).astype(BF16)
            d_logits[w].append(low)
            turned[w].append(turn_pair(low))
        yield
    parts = []
    for w in range(WINDOWS):
        query_blocks = head_blocks(r.qkv_win[slot, w, :, :D], r.mask)
        key_blocks = head_blocks(r.qkv_win[slot, w, :, D : 2 * D], r.mask)
        d_query, d_key, d_value = [], [], []
        for g in range(2):
            two = slice(2 * g, 2 * g + 2)
            attend_low = r.attend_win[slot, w, :, 256 * g : 256 * g + 256]
            d_value.append(dot(attend_low, mixed_blocks[w][g])[:PAD])
            d_key.append(dot(jnp.concatenate(d_logits[w][two], 1), query_blocks[g])[:PAD] * SCALE)
            d_query.append(dot(jnp.concatenate(turned[w][two], 1), key_blocks[g])[:PAD] * SCALE)
        parts.append(jnp.concatenate(d_query + d_key + d_value, 1))
        yield
    d_qkv = jnp.concatenate(parts, 0).astype(BF16)
    r.d_qkv_all[rows] = d_qkv
    for copy in late_copies(r, s):
        copy.start()
    yield


WEAVE = (-0.005, 0.145, 0.197, 0.403, 0.447)


def run(*stages):
    order = []
    for n, stage in enumerate(stages):
        count = PIECES[stage.__name__]
        places = (np.arange(count) + 0.5) / count
        if n:
            places = np.interp(places, np.linspace(0.0, 1.0, len(WEAVE)), WEAVE)
        order += [(place, n) for place in places]
    for _, n in sorted(order):
        next(stages[n])
    for stage in stages:
        assert next(stage, None) is None


PIECES = {"forward_stage": 5 + 3 * WINDOWS, "backward_stage": 1 + 3 * (MLP // D) + 3 + 3 * WINDOWS + 1}


def down_rows(n):
    return DOWN[n // 2] + (n % 2) * D


def finish(r):
    core = lax.rem(lax.axis_index("dp"), 2)
    grads = r.grads

    def put(start, rows):
        grads[start : start + rows.shape[0]] = rows
        r.grads_low[start : start + rows.shape[0]] = rows.astype(BF16)

    def hand_over(n, start, count):
        span = pl.ds(start, count)
        kept = pl.ds(pl.multiple_of(core * HALF + start, 16), count)
        sent = pl.ds(pl.multiple_of((1 - core) * HALF + start, 16), count)
        copies = [
            pltpu.make_async_copy(grads.at[kept], r.keep.at[span], r.sems.at[2 * n]),
            pltpu.make_async_copy(r.grads_low.at[sent], r.send.at[span], r.sems.at[2 * n + 1]),
        ]
        for copy in copies:
            copy.start()
        return copies

    product = dot_tn(r.first_all[:, : D + 8], r.d_qkv_all[...])
    sums = product[D : D + 8]
    for n in range(3):
        put(QKV + n * D, product[:D, n * D : (n + 1) * D])
    put(PROJ, dot_tn(r.mixed_all[...], r.d_branch_all[...]))
    bias_parts = dot_nt(jnp.concatenate(three_parts(sums), 0), r.w_qkv[...])
    bias_grad = bias_parts[0:1] + bias_parts[8:9] + bias_parts[16:17]
    cross = jnp.zeros((D, 128), F32)
    for n in range(0, 3 * D, 128):
        cross = cross + product[:D, n : n + 128] * r.w_qkv[:, n : n + 128].astype(F32)
    gain_grad = (col_sum(cross.T) - r.bias_one[...] * bias_grad) / r.gain_one[...]
    small = [sums[0:1, :D], sums[0:1, 2 * D :], gain_grad, bias_grad, jnp.zeros((20, D), F32)]
    product = dot_tn(r.second_all[:, : D + 8], r.d_inner_all[...])
    for n in range(MLP // D):
        put(UP + n * D, product[:D, n * D : (n + 1) * D])
    ups = [product[D : D + 1, n * D : (n + 1) * D] for n in range(MLP // D)]
    put(SMALL_ONE, jnp.concatenate([r.sums[0:4]] + ups + [jnp.zeros((24, D), F32)], 0))
    put(SMALL_TWO, jnp.concatenate([table_gradient(r.logit_sums, r.entries, r.by_head)] + small, 0))
    copies = hand_over(0, UP, MLP) + hand_over(1, SMALL_ONE, 32)
    product = dot_tn(r.cot_all[...], r.active_all[...])
    for n in range(MLP // D):
        put(down_rows(n), 0.5 * product[:, n * D : (n + 1) * D])
    copies += hand_over(2, DOWN[0], 2 * D)
    for n in range(STRIPS):
        copies += early_copies(r, n) + late_copies(r, n)
    for copy in copies:
        copy.wait()


class Refs:
    def __init__(self, names, refs):
        self.__dict__.update(zip(names, refs))


INPUTS = [
    "image", "cot", "gather", "mask", "entries", "w_qkv", "w_proj", "w_up", "w_down",
    "halo", "regions", "regions_halo", "spread", "spread_rows", "table",
    "gain_one", "bias_one", "b_query", "b_value", "b_proj", "gain_two", "bias_two", "b_up",
]
NAMES = [name + "_in" for name in INPUTS] + [
    "keep", "send", "tokens_out", "resid_out", "active_out", "d_branch_out", "d_qkv_out",
    "lane_labels", "by_head", "bias_t", "logit_sums", "qkv_win", "attend_win", "sums",
    "first_all", "cot_all", "mixed_all", "second_all", "active_all", "d_inner_all", "d_branch_all", "d_qkv_all",
    "tokens_all", "resid_all", "grads", "grads_low", "sems", "in_sems", "early_sems", "late_sems",
] + INPUTS


LATE_WAITS = 8


def input_copies(r):
    top = WIN + SHIFT
    last = [("w_up", None), ("w_down", None), ("image", slice(top, COLS)), ("cot", slice(top, COLS))]
    large = ["entries", "gather", "image", "w_qkv", "mask", "cot", "w_proj", "halo"]
    names = [name for name in INPUTS if name not in large + ["w_up", "w_down"]] + large
    first = [(name, slice(0, top) if name in ("image", "cot") else None) for name in names]
    copies = []
    for n, (name, rows) in enumerate(first + last):
        source, place = getattr(r, name + "_in"), getattr(r, name)
        if rows is not None:
            source, place = source.at[rows], place.at[rows]
        copies.append(pltpu.make_async_copy(source, place, r.in_sems.at[n]))
    return copies[: len(first)], copies[len(first) :]


def put_labels(r, n, part):
    row = jnp.sum(part * r.spread_rows[...], 0, keepdims=True)
    windows = [row[:, 128 * w : 128 * w + 128] for w in range(WINDOWS)]
    r.lane_labels[n] = jnp.concatenate(windows + [jnp.zeros((2, 128), F32)], 0)


def grads_kernel(*refs):
    r = Refs(NAMES, refs)
    s = pl.program_id(0)

    @pl.when(s == 0)
    def _():
        first, later = input_copies(r)
        for copy in first:
            copy.start()
        r.logit_sums[...] = jnp.zeros_like(r.logit_sums)
        r.sums[...] = jnp.zeros_like(r.sums)
        one = (lane_ids((TOTAL, 128)) == 0).astype(F32).astype(BF16)
        r.first_all[:, D:] = one
        r.second_all[:, D:] = one
        for copy in first[: 1 - LATE_WAITS]:
            copy.wait()
        own = dot(r.regions[...].astype(F32).astype(BF16), r.spread[...])
        for n in range(STRIPS - 1):
            put_labels(r, n, own[n * WIN + SHIFT : (n + 1) * WIN + SHIFT])
        below = dot(r.regions_halo[...], r.spread[...])
        put_labels(r, STRIPS - 1, jnp.concatenate([own[COLS - (WIN - SHIFT) :], below], 0))
        build_bias(r.table[...], r.entries, r.by_head, r.bias_t)
        for copy in first[1 - LATE_WAITS :]:
            copy.wait()
        for copy in later:
            copy.start()
        run(forward_stage(s, r))
        for copy in later:
            copy.wait()
        r.w_down[...] = r.w_down[...] * jnp.bfloat16(0.5)

    @pl.when((s > 0) & (s < STRIPS))
    def _():
        run(backward_stage(s - 1, r), forward_stage(s, r))

    @pl.when(s == STRIPS)
    def _():
        run(backward_stage(s - 1, r))
        finish(r)


def output_strip(active, resid, w_down, b_down, scatter):
    result = resid[...] + b_down[...] + 0.5 * dot(active[...], w_down[...])
    return dot(scatter[...], result.astype(BF16)).astype(BF16)


def image_strip(d_qkv, d_branch, tokens, w_qkv, gain, scatter):
    normal, recip_dev = normalize(tokens[...].astype(F32))
    d_first = dot_nt(d_qkv[...], w_qkv[...])
    grad = d_branch[...].astype(F32) + norm_backward(d_first, normal, recip_dev, gain[...])
    return dot(scatter[...], grad.astype(BF16)).astype(BF16)


there = pl.BlockSpec(memory_space=pl.ANY)


def whole(shape):
    return pl.BlockSpec(shape, lambda s: (0,) * len(shape))


def once(shape):
    return pl.BlockSpec(shape, lambda s: (0,) * len(shape), pipeline_mode=pl.Buffered(1))


def strips(shape):
    return pl.BlockSpec(shape, lambda s: (s,) + (0,) * (len(shape) - 1))


def struct(shape, dtype):
    return jax.ShapeDtypeStruct(shape, dtype)


def params(mebibytes):
    return pltpu.CompilerParams(
        vmem_limit_bytes=mebibytes * 1024 * 1024, dimension_semantics=("arbitrary",)
    )


def pack_kernel(image, cot, regions, rows, labels):
    rows[0:SHIFT] = image[...]
    rows[SHIFT:] = cot[...]
    labels[...] = regions[0:SHIFT].astype(F32).astype(BF16)


def pack_first_rows(image, cot, regions):
    return pl.pallas_call(
        pack_kernel,
        grid=(1,),
        in_specs=[whole((SHIFT, COLS, D)), whole((SHIFT, COLS, D)), whole(regions.shape)],
        out_specs=[whole((2 * SHIFT, COLS, D)), whole((SHIFT, COLS))],
        out_shape=[pltpu.VMEM((2 * SHIFT, COLS, D), BF16), pltpu.VMEM((SHIFT, COLS), BF16)],
        compiler_params=params(62),
        name="pack_first_rows",
    )(image, cot, regions)


def run_grads(*args):
    return pl.pallas_call(
        grads_kernel,
        grid=(STRIPS + 1,),
        in_specs=[there] * len(args),
        out_specs=[there] * 7,
        out_shape=[
            pltpu.VMEM((HALF, D), F32),
            pltpu.VMEM((HALF, D), BF16),
            struct((TOTAL, D), BF16),
            struct((TOTAL, D), F32),
            struct((TOTAL, MLP), BF16),
            struct((TOTAL, D), BF16),
            struct((TOTAL, 3 * D), BF16),
        ],
        scratch_shapes=[
            pltpu.VMEM((STRIPS, 8, 128), F32),
            pltpu.VMEM((HEADS, 8, 128), F32),
            pltpu.VMEM((PAD, HEADS * LANES), F32),
            pltpu.VMEM((PAD, HEADS * LANES), F32),
            pltpu.VMEM((2, WINDOWS, LANES, 3 * D), BF16),
            pltpu.VMEM((2, WINDOWS, LANES, HEADS * LANES), BF16),
            pltpu.VMEM((8, D), F32),
            pltpu.VMEM((TOTAL, D + 128), BF16),
            pltpu.VMEM((TOTAL, D), BF16),
            pltpu.VMEM((TOTAL, D), BF16),
            pltpu.VMEM((TOTAL, D + 128), BF16),
            pltpu.VMEM((TOTAL, MLP), BF16),
            pltpu.VMEM((TOTAL, MLP), BF16),
            pltpu.VMEM((TOTAL, D), BF16),
            pltpu.VMEM((TOTAL, 3 * D), BF16),
            pltpu.VMEM((TOTAL, D), BF16),
            pltpu.VMEM((TOTAL, D), F32),
            pltpu.VMEM((2 * HALF, D), F32),
            pltpu.VMEM((2 * HALF, D), BF16),
            pltpu.SemaphoreType.DMA((6,)),
            pltpu.SemaphoreType.DMA((len(INPUTS) + 2,)),
            pltpu.SemaphoreType.DMA((STRIPS, 2)),
            pltpu.SemaphoreType.DMA((STRIPS, 3)),
        ]
        + [pltpu.VMEM(a.shape, a.dtype) for a in args],
        compiler_params=params(58),
        cost_estimate=pl.CostEstimate(
            flops=2 * TOTAL * 10 * D * MLP, bytes_accessed=20_000_000, transcendentals=0
        ),
        name="all_gradients",
    )(*args)


def run_field(strip, name, which, blocks, others, field=None, tails=None):
    lower = field is None
    first = FIELD_STEPS if lower else 0
    given = [a for a in (field, tails) if a is not None]
    inputs = len(blocks) + len(others)
    shapes = [struct((COLS, COLS, D), BF16)] + [struct((2, SENT, COLS, D), BF16)] * lower

    def kernel(*refs):
        out = refs[inputs + len(given)]
        below = refs[inputs + len(given) + 1] if lower else None
        put_rows(strip(*refs[:inputs]), first, which, out, below, *refs[-2:])

    return pl.pallas_call(
        kernel,
        grid=(FIELD_STEPS,),
        in_specs=[pl.BlockSpec((STRIP, a.shape[1]), lambda t: (first + t, 0)) for a in blocks]
        + [whole(a.shape) for a in others]
        + [there] * len(given),
        out_specs=[there] * len(shapes),
        out_shape=shapes,
        scratch_shapes=[pltpu.VMEM((2, WIN, COLS, D), BF16), pltpu.SemaphoreType.DMA((3,))],
        input_output_aliases={inputs: 1 if lower else 0} if given else {},
        compiler_params=params(60),
        cost_estimate=pl.CostEstimate(
            flops=2 * TOTAL * 4 * D * D, bytes_accessed=9_000_000, transcendentals=0
        ),
        name=name,
    )(*blocks, *others, *given)


def unpack_half(half, rows, w_up, w_down, w_proj, w_qkv, stage, sems):
    def down(first):
        for n in range(2):
            stage[n * D : (n + 1) * D, :D] = rows[first + n * D : first + (n + 1) * D].astype(F32).T
        at = pl.ds(half * 2 * D, 2 * D)
        return pltpu.make_async_copy(stage.at[pl.ds(0, 2 * D), pl.ds(0, D)], w_down.at[at], sems.at[0])

    def wide(out, first, count, at, sem):
        for n in range(count):
            part = rows[first + n * D : first + (n + 1) * D].astype(F32)
            stage[at : at + D, n * D : (n + 1) * D] = part
        return pltpu.make_async_copy(stage.at[pl.ds(at, D), pl.ds(0, count * D)], out, sems.at[sem])

    copies = []
    if half == 0:
        copies.append(wide(w_up, UP, MLP // D, 2 * D, 1))
        copies[-1].start()
        copies.append(down(DOWN[0]))
        copies[-1].start()
    else:
        copies.append(wide(w_qkv, QKV - HALF, 3, 2 * D, 1))
        copies[-1].start()
        copies.append(wide(w_proj, PROJ - HALF, 1, 3 * D, 2))
        copies[-1].start()
        copies.append(down(DOWN[1] - HALF))
        copies[-1].start()
    for copy in copies:
        copy.wait()


def unpack_first_kernel(own, *refs):
    core = lax.rem(lax.axis_index("dp"), 2)
    for half in range(2):

        @pl.when(core == half)
        def _():
            unpack_half(half, own, *refs)


def unpack_second_kernel(
    other, own, in_up, in_down, in_proj, in_qkv, w_up, w_down, w_proj, w_qkv,
    gain_one, bias_one, b_query, b_value, table, b_proj, gain_two, bias_two, b_up, b_down, stage, sems,
):
    core = lax.rem(lax.axis_index("dp"), 2)
    for half in range(2):

        @pl.when(core != half)
        def _():
            unpack_half(half, other, w_up, w_down, w_proj, w_qkv, stage, sems)

    mine, others = own[...].astype(F32), other[SMALL_ONE:].astype(F32)
    first = jnp.where(core == 0, mine, others)
    second = jnp.where(core == 0, others, mine)
    for n, out in enumerate((gain_two, bias_two, b_proj, b_down)):
        out[...] = first[n : n + 1]
    for n in range(MLP // D):
        b_up[:, n * D : (n + 1) * D] = first[4 + n : 5 + n]
    table[...] = second[:HEADS, :ENTRIES]
    for n, out in enumerate((b_query, b_value, gain_one, bias_one)):
        out[...] = second[HEADS + n : HEADS + n + 1]


LARGE = ((D, MLP), (MLP, D), (D, D), (D, 3 * D))
UNPACK_SCRATCH = [pltpu.VMEM((4 * D, MLP), F32), pltpu.SemaphoreType.DMA((3,))]
def unpack_first(own):
    return pl.pallas_call(
        unpack_first_kernel,
        grid=(1,),
        in_specs=[whole(own.shape)],
        out_specs=[there] * 4,
        out_shape=[struct(shape, F32) for shape in LARGE],
        scratch_shapes=UNPACK_SCRATCH,
        compiler_params=params(24),
        cost_estimate=pl.CostEstimate(flops=0, bytes_accessed=2_400_000, transcendentals=0),
        name="unpack_own_half",
    )(own)


def unpack_second(other, own, large):
    one, four = (1, D), (1, MLP)
    shapes = [one, one, one, one, (HEADS, ENTRIES), one, one, one, four, one]
    out = pl.pallas_call(
        unpack_second_kernel,
        grid=(1,),
        in_specs=[whole(other.shape), pl.BlockSpec((32, D), lambda s: (SMALL_ONE // 32, 0))] + [there] * 4,
        out_specs=[there] * 4 + [whole(shape) for shape in shapes],
        out_shape=[struct(shape, F32) for shape in LARGE] + [struct(shape, F32) for shape in shapes],
        scratch_shapes=UNPACK_SCRATCH,
        input_output_aliases={2: 0, 3: 1, 4: 2, 5: 3},
        compiler_params=params(24),
        name="unpack_other_half",
    )(other, own, *large)
    w_up, w_down, w_proj, w_qkv = out[:4]
    gain_one, bias_one, b_query, b_value, table, b_proj, gain_two, bias_two, b_up, b_down = out[4:]
    return (
        gain_one[0], bias_one[0], w_qkv, b_query[0], b_value[0], table.T, w_proj, b_proj[0],
        gain_two[0], bias_two[0], w_up, b_up[0], w_down, b_down[0],
    )


def coords(index):
    dp, space = divmod(index, 32)
    return {"c": dp % 2, "y": dp // 2 + 2 * ((space // 4) % 2), "x": space % 4, "z": space // 8}


def index_of(c, y, x, z):
    return ((y % 2) * 2 + c) * 32 + z * 8 + (y // 2) * 4 + x


DISTANCES = (2, 1, 3)
STAGES = (("y", "x"), ("x", "z"), ("z", "y"))


def other_core():
    return [(i, index_of(**(coords(i) | {"c": 1 - i // 32 % 2}))) for i in range(128)]


def around(stage, distance):
    out = []
    for i in range(128):
        at = coords(i)
        axis = stage[at["c"]]
        out.append((i, index_of(**(at | {axis: (at[axis] + distance) % 4}))))
    return out


def take(rows, start, count):
    return lax.dynamic_slice_in_dim(rows, start, count, 0)


def sum_everywhere(mine, got_core, at, pieces):
    made = {}
    left = list(pieces)

    def exchange(stage, sends, own):
        nonlocal made
        ahead, beside = left.pop(0)
        early = ahead(made)
        got = [lax.ppermute(sends[d], AXES, around(stage, d)) for d in DISTANCES]
        made, own = lax.optimization_barrier((made, own))
        made = made | beside(made)
        got, made, early, own = lax.optimization_barrier((got, made, early, own))
        made = made | early
        return dict(zip(DISTANCES, got)), own

    def place(stage):
        return jnp.where(at["c"] == 0, at[stage[0]], at[stage[1]])

    stage = STAGES[0]
    here = place(stage)
    count = mine.shape[0] // 4

    def part(which):
        start = which * count
        return take(mine, start, count) + take(got_core, start, count).astype(F32)

    sends = {d: part((here + d) % 4).astype(BF16) for d in DISTANCES}
    got, rows = exchange(stage, sends, part(here))
    for d in DISTANCES:
        rows = rows + got[d].astype(F32)
    low = rows.astype(BF16)
    for stage in STAGES[1:]:
        got, low = exchange(stage, {d: low for d in DISTANCES}, low)
        pairs = low.astype(F32) + got[2].astype(F32), got[1].astype(F32) + got[3].astype(F32)
        low = (pairs[0] + pairs[1]).astype(BF16)
    ahead, beside = left.pop(0)
    parts = {0: low} | {d: lax.ppermute(low, AXES, around(STAGES[0], d)) for d in (1, 2, 3)}
    others = {d: lax.ppermute(rows, AXES, other_core()) for d, rows in parts.items()}
    made = made | beside(made)

    def assemble(parts, here):
        out = jnp.zeros((4 * count, D), BF16)
        for d, rows in parts.items():
            out = lax.dynamic_update_slice(out, rows, ((here - d) % 4 * count, 0))
        return out

    there_axis = jnp.where(at["c"] == 0, at[STAGES[0][1]], at[STAGES[0][0]])
    own = assemble(parts, here)
    large = unpack_first(own)
    others, large, made = lax.optimization_barrier((others, large, made))
    return own, assemble(others, there_axis), large, made


def body(
    image_in, cotangent, regions, first_gain, first_bias, qkv_weight, query_bias, value_bias,
    position_table, proj_weight, proj_bias, second_gain, second_bias, up_weight, up_bias,
    down_weight, down_bias,
):
    many = lax.axis_size("dp") * lax.axis_size("space") == 128
    me = lax.axis_index(AXES)
    at = coords(me)
    first_rows = pack_first_rows(image_in, cotangent, regions)
    halo, regions_halo = from_behind(first_rows, "space", -1)
    gather = gather_matrix()
    spread, spread_rows = label_matrices()
    entries = jnp.asarray(entry_matrix(), BF16)
    mask = jnp.asarray(head_mask(), BF16)
    scatter = jnp.asarray(gather.T, BF16)
    mine, send, tokens, resid, active, d_branch, d_qkv = run_grads(
        image_in, cotangent, jnp.asarray(gather, BF16), mask, entries, qkv_weight, proj_weight, up_weight, down_weight,
        halo, regions, regions_halo, jnp.asarray(spread, BF16), jnp.asarray(spread_rows), position_table.T,
        first_gain[None], first_bias[None], query_bias[None], value_bias[None], proj_bias[None],
        second_gain[None], second_bias[None], up_bias[None],
    )
    if many:
        got = lax.ppermute(send, AXES, other_core())

    def block_output(*given):
        others = (down_weight, down_bias[None], scatter)
        return run_field(output_strip, "block_output", 0, (active, resid), others, *given)

    def image_gradient(*given):
        others = (qkv_weight, first_gain[None], scatter)
        return run_field(image_strip, "image_gradient", 1, (d_qkv, d_branch, tokens), others, *given)

    def lower_out(made):
        out, tails = block_output()
        return {"out": out, "tails": tails}

    def lower_image(made):
        image, tails = image_gradient(None, made["tails"])
        return {"image": image, "tails": tails}

    def upper_out(made):
        return made | {"out": block_output(made["out"])[0]}

    def return_rows(made):
        return {"returned": from_behind(made["tails"], "space", 1)}

    def upper_image(made):
        return made | {"image": image_gradient(made["image"])[0]}

    def nothing(made):
        return {}

    def fields(made):
        first, at = made["returned"][:, SENT - SHIFT :], (0, 0, 0)
        return {
            "out": lax.dynamic_update_slice(made["out"], first[0], at),
            "image": lax.dynamic_update_slice(made["image"], first[1], at),
        }

    def upper_out_and_fields(made):
        made = made | upper_out(made)
        return made | fields(made)

    pieces = [(nothing, lower_out), (nothing, lower_image), (return_rows, upper_image), (nothing, upper_out_and_fields)]
    if many:
        own, other, large, made = sum_everywhere(mine, got, at, pieces)
    else:
        made = {}
        for ahead, beside in pieces:
            made = made | ahead(made) | beside(made)
        own, other = mine.astype(BF16), send
        large = unpack_first(own)
    return (made["out"], made["image"]) + unpack_second(other, own, large)


def solution(mesh):
    tokens = P(AXES, None, None)
    return jax.shard_map(
        body,
        mesh=mesh,
        in_specs=(tokens, tokens, P(AXES, None)) + (P(),) * 14,
        out_specs=(tokens, tokens) + (P(),) * 14,
        check_vma=False,
    )
```

```python
import functools
import math

import jax
import jax.numpy as jnp
import numpy as np
from jax import lax
from jax.experimental import pallas as pl
from jax.experimental.pallas import tpu as pltpu
from jax.sharding import PartitionSpec as P

WIN = 7
SHIFT = 3
HEADS = 8
TOKENS = WIN * WIN
PAD = 56
LANES = 64
ENTRIES = (2 * WIN - 1) * (2 * WIN - 1)
COLS = 42
WINDOWS = COLS // WIN
STRIP = WINDOWS * PAD
STRIPS = COLS // WIN
SENT = 5
FIELD_STEPS = STRIPS // 2
TOTAL = STRIPS * STRIP
ROW = 48
D = 256
MLP = 1024
BF16 = jnp.bfloat16
F32 = jnp.float32
epsilon = 1e-05
neg = -1000000000.0
AXES = ("dp", "space")
SCALE = 1.0 / math.sqrt(D // HEADS)
LOG2E = 1.4426950408889634
UP = 0
HALF = MLP + 2 * D + 32
PROJ = HALF
QKV = PROJ + D
DOWN = (MLP, HALF + MLP)
SMALL_ONE = MLP + 2 * D
SMALL_TWO = HALF + SMALL_ONE
assert QKV + 3 * D == DOWN[1]


def from_behind(block, axis, distance):
    devices = range(lax.axis_size(axis))
    route = [((i - distance) % len(devices), i) for i in devices]
    return lax.ppermute(block, axis, route)


def place(i, j):
    return 8 * i + j


def gather_matrix():
    out = np.zeros((STRIP, WIN * ROW), np.float32)
    for w in range(WINDOWS):
        for i in range(WIN):
            for j in range(WIN):
                out[w * PAD + place(i, j), i * ROW + (w * WIN + j + SHIFT) % COLS] = 1.0
    return out


def label_matrices():
    spread = np.zeros((COLS, WINDOWS * 2 * LANES), np.float32)
    rows = np.zeros((WIN, WINDOWS * 2 * LANES), np.float32)
    for w in range(WINDOWS):
        for copy in range(2):
            for i in range(WIN):
                for j in range(WIN):
                    col = (w * 2 + copy) * LANES + place(i, j)
                    spread[(w * WIN + j + SHIFT) % COLS, col] = 1.0
                    rows[i, col] = 1.0
    return spread, rows


def entry_matrix():
    out = np.zeros((WIN * 128, D), np.float32)
    for kj in range(WIN):
        for di in range(1 - WIN, WIN):
            for qj in range(WIN):
                entry = (di + WIN - 1) * (2 * WIN - 1) + qj - kj + WIN - 1
                out[kj * 128 + (8 * di + qj) % 128, entry] = 1.0
    return out


def head_mask():
    return (np.arange(4 * LANES)[:, None] // LANES == np.arange(128)[None] // 32).astype(np.float32)


def dot(a, b):
    return jnp.dot(a, b, preferred_element_type=F32)


def dot_nt(a, b):
    return lax.dot_general(a, b, (((1,), (1,)), ((), ())), preferred_element_type=F32)


def dot_tn(a, b):
    return lax.dot_general(a, b, (((0,), (0,)), ((), ())), preferred_element_type=F32)


def normalize(values):
    center = values - jnp.mean(values, -1, keepdims=True)
    variance = jnp.mean(center * center, -1, keepdims=True)
    recip_dev = lax.rsqrt(variance + epsilon)
    return center * recip_dev, recip_dev


def norm_backward(upstream, normal_part, recip_dev, gain):
    scaled = upstream * gain
    inner_mean = jnp.mean(scaled, -1, keepdims=True)
    cross_mean = jnp.mean(scaled * normal_part, -1, keepdims=True)
    return recip_dev * (scaled - inner_mean - normal_part * cross_mean)


def col_sum(values):
    return jnp.sum(values, 0, keepdims=True)


def raster_rows(ref, halo, first, s):
    last = s == STRIPS - 1
    blank = jnp.zeros((ROW - COLS, D), BF16)
    rows = []
    for i in range(WIN):
        g = s * WIN + i + SHIFT
        if i < WIN - SHIFT:
            value = ref[g]
        else:
            value = jnp.where(
                last, halo[first + i - (WIN - SHIFT)], ref[jnp.minimum(g, COLS - 1)]
            )
        rows += [value, blank]
    return jnp.concatenate(rows, 0)


def put_rows(raster, first, which, out, tails, stage, sems):
    t = pl.program_id(0)
    slot = lax.rem(t, 2)

    def whole_strip(n):
        return pltpu.make_async_copy(
            stage.at[lax.rem(n, 2)], out.at[pl.ds((first + n) * WIN + SHIFT, WIN)], sems.at[lax.rem(n, 2)]
        )

    @pl.when(t >= 2)
    def _():
        whole_strip(t - 2).wait()

    for i in range(WIN):
        stage[slot, i] = raster[i * ROW : i * ROW + COLS]

    @pl.when(first + t < STRIPS - 1)
    def _():
        whole_strip(t).start()

    @pl.when(t == FIELD_STEPS - 1)
    def _():
        if tails is None:
            whole_strip(t - 1).wait()
            whole_strip(t).wait()
        else:
            own = pltpu.make_async_copy(
                stage.at[slot, 0 : WIN - SHIFT], out.at[COLS - (WIN - SHIFT) : COLS], sems.at[slot]
            )
            below = pltpu.make_async_copy(stage.at[slot, WIN - SENT : WIN], tails.at[which], sems.at[2])
            own.start()
            below.start()
            whole_strip(t - 1).wait()
            own.wait()
            below.wait()


def pad_rows(values):
    return jnp.concatenate([values, jnp.zeros((LANES - PAD,) + values.shape[1:], values.dtype)], 0)


def head_blocks(low, mask):
    return [jnp.concatenate([low[:, g : g + 128]] * 4, 0) * mask[...] for g in (0, 128)]


def turn_pair(values):
    turned = values.T
    return jnp.concatenate([turned[:LANES], turned[LANES:]], 1)


def three_parts(values):
    high = values.astype(BF16)
    rest = values - high.astype(F32)
    middle = rest.astype(BF16)
    return high, middle, (rest - middle.astype(F32)).astype(BF16)


def lane_ids(shape):
    return lax.broadcasted_iota(jnp.int32, shape, 1)


def build_bias(table, entries, by_head, bias_t):
    parts = three_parts(table * LOG2E)
    for kj in range(WIN):
        one = entries[kj * 128 : (kj + 1) * 128, :ENTRIES]
        by_head[:, kj, :] = dot_nt(parts[0], one) + dot_nt(parts[1], one) + dot_nt(parts[2], one)
    by_head[:, WIN, :] = jnp.full((HEADS, 128), neg, F32)
    lane = lane_ids((8, 128))
    for pair in range(HEADS // 2):
        for ki in range(WIN):
            first = pltpu.roll(by_head[2 * pair], 8 * ki, 1)
            second = pltpu.roll(by_head[2 * pair + 1], (8 * ki + LANES) % 128, 1)
            bias_t[8 * ki : 8 * ki + 8, 128 * pair : 128 * pair + 128] = jnp.where(
                lane < LANES, first, second
            )


def table_gradient(logit_sums, entries, by_head):
    lane = lane_ids((8, 128))
    for pair in range(HEADS // 2):
        for half in range(2):
            total = jnp.zeros((8, 128), F32)
            for ki in range(WIN):
                block = logit_sums[8 * ki : 8 * ki + 8, 128 * pair : 128 * pair + 128]
                own = jnp.where((lane < LANES) == (half == 0), block, 0.0)
                total = total + pltpu.roll(own, (128 - 8 * ki - LANES * half) % 128, 1)
            by_head[2 * pair + half] = total
    out = jnp.zeros((HEADS, D), F32)
    for kj in range(WIN):
        one = entries[kj * 128 : (kj + 1) * 128]
        for part in three_parts(by_head[:, kj, :]):
            out = out + dot(part, one)
    return out


def spans():
    return [slice(w * PAD, (w + 1) * PAD) for w in range(WINDOWS)]


def forward_stage(s, r):
    rows = pl.ds(pl.multiple_of(s * STRIP, 16), STRIP)
    slot = lax.rem(s, 2)
    tokens = dot(r.gather[...], raster_rows(r.image, r.halo, 0, s))
    r.tokens_all[rows] = tokens.astype(BF16)
    yield
    r.cot_all[rows] = dot(r.gather[...], raster_rows(r.cot, r.halo, SHIFT, s)).astype(BF16)
    yield
    normal_one, _ = normalize(tokens)
    first_low = (normal_one * r.gain_one[...] + r.bias_one[...]).astype(BF16)
    r.first_all[rows, :D] = first_low
    yield
    query = dot(first_low, r.w_qkv[:, :D]) + r.b_query[...]
    key = dot(first_low, r.w_qkv[:, D : 2 * D])
    value = dot(first_low, r.w_qkv[:, 2 * D :]) + r.b_value[...]
    yield
    key_labels = r.lane_labels[s].T
    logits = []
    for w, span in enumerate(spans()):
        query_low = pad_rows(query[span]).astype(BF16)
        key_low = pad_rows(key[span]).astype(BF16)
        value_low = pad_rows(value[span]).astype(BF16)
        r.qkv_win[slot, w, :, :D] = query_low
        r.qkv_win[slot, w, :, D : 2 * D] = key_low
        r.qkv_win[slot, w, :, 2 * D :] = value_low
        blocks = head_blocks(query_low, r.mask)
        logits.append(
            [dot_nt(key_low[:, 128 * g : 128 * g + 128], blocks[g])[:PAD] for g in range(2)]
        )
        yield
    turned = []
    for w in range(WINDOWS):
        same = key_labels[:PAD, w : w + 1] == r.lane_labels[s, w : w + 1, :]
        turned.append([])
        for pair in range(HEADS // 2):
            cols = slice(128 * pair, 128 * pair + 128)
            part = logits[w][pair // 2][:, 128 * (pair % 2) : 128 * (pair % 2) + 128]
            part = jnp.where(same, part * (SCALE * LOG2E) + r.bias_t[:, cols], neg)
            powers = jnp.exp2(part - jnp.max(part, 0, keepdims=True))
            attend = powers * (1.0 / jnp.sum(powers, 0, keepdims=True))
            attend_low = pad_rows(attend).astype(BF16)
            r.attend_win[slot, w, :, cols] = attend_low
            turned[w].append(turn_pair(attend_low))
        yield
    mixed_parts = []
    for w in range(WINDOWS):
        blocks = head_blocks(r.qkv_win[slot, w, :, 2 * D :], r.mask)
        mixed_parts.append(
            jnp.concatenate(
                [
                    dot(jnp.concatenate(turned[w][2 * g : 2 * g + 2], 1), blocks[g])[:PAD]
                    for g in range(2)
                ],
                1,
            )
        )
        yield
    mixed_low = jnp.concatenate(mixed_parts, 0).astype(BF16)
    r.mixed_all[rows] = mixed_low
    resid = tokens + dot(mixed_low, r.w_proj[...]) + r.b_proj[...]
    r.resid_all[rows] = resid
    for copy in early_copies(r, s):
        copy.start()
    yield


def strip_copies(s, sems, pairs):
    rows = pl.ds(pl.multiple_of(s * STRIP, 16), STRIP)
    return [pltpu.make_async_copy(a.at[rows], b.at[rows], sems.at[s, n]) for n, (a, b) in enumerate(pairs)]


def early_copies(r, s):
    return strip_copies(s, r.early_sems, ((r.tokens_all, r.tokens_out), (r.resid_all, r.resid_out)))


def late_copies(r, s):
    pairs = (r.active_all, r.active_out), (r.d_branch_all, r.d_branch_out), (r.d_qkv_all, r.d_qkv_out)
    return strip_copies(s, r.late_sems, pairs)


def backward_stage(s, r):
    rows = pl.ds(pl.multiple_of(s * STRIP, 16), STRIP)
    slot = lax.rem(s, 2)
    sums = r.sums
    resid = r.resid_all[rows]
    normal_two, recip_two = normalize(resid)
    second_low = (normal_two * r.gain_two[...] + r.bias_two[...]).astype(BF16)
    r.second_all[rows, :D] = second_low
    yield
    cot_low = r.cot_all[rows]
    d_second = jnp.zeros((STRIP, D), F32)
    for n in range(MLP // D):
        cols = slice(n * D, (n + 1) * D)
        inner = dot(second_low, r.w_up[:, cols]) + r.b_up[:, cols]
        cumulative = lax.erf(inner * 0.7071067811865476) + 1.0
        active_low = (inner * cumulative).astype(BF16)
        r.active_all[rows, cols] = active_low
        yield
        gauss = jnp.exp2(inner * inner * (-0.5 * LOG2E))
        slope = cumulative + inner * gauss * 0.7978845608028654
        d_inner = (dot_nt(cot_low, r.w_down[cols]) * slope).astype(BF16)
        r.d_inner_all[rows, cols] = d_inner
        yield
        d_second = d_second + dot_nt(d_inner, r.w_up[:, cols])
        yield
    cot_f32 = cot_low.astype(F32)
    d_resid = cot_f32 + norm_backward(d_second, normal_two, recip_two, r.gain_two[...])
    d_branch = d_resid.astype(BF16)
    r.d_branch_all[rows] = d_branch
    yield
    d_mixed = dot_nt(d_branch, r.w_proj[...])
    yield
    sums[0:1] += col_sum(d_second * normal_two)
    sums[1:2] += col_sum(d_second)
    sums[2:3] += col_sum(d_resid)
    sums[3:4] += col_sum(cot_f32)
    yield
    mixed_blocks = []
    d_attends = []
    for w, span in enumerate(spans()):
        blocks = head_blocks(pad_rows(d_mixed[span]).astype(BF16), r.mask)
        mixed_blocks.append(blocks)
        value_low = r.qkv_win[slot, w, :, 2 * D :]
        d_attends.append(
            [dot_nt(value_low[:, 128 * g : 128 * g + 128], blocks[g])[:PAD] for g in range(2)]
        )
        yield
    d_logits = []
    turned = []
    for w in range(WINDOWS):
        d_logits.append([])
        turned.append([])
        for pair in range(HEADS // 2):
            cols = slice(128 * pair, 128 * pair + 128)
            part = d_attends[w][pair // 2][:, 128 * (pair % 2) : 128 * (pair % 2) + 128]
            attend = r.attend_win[slot, w, :, cols].astype(F32)[:PAD]
            cross = jnp.sum(part * attend, 0, keepdims=True)
            part = attend * (part - cross)
            r.logit_sums[:, cols] += part
            low = pad_rows(part).astype(BF16)
            d_logits[w].append(low)
            turned[w].append(turn_pair(low))
        yield
    parts = []
    for w in range(WINDOWS):
        query_blocks = head_blocks(r.qkv_win[slot, w, :, :D], r.mask)
        key_blocks = head_blocks(r.qkv_win[slot, w, :, D : 2 * D], r.mask)
        d_query, d_key, d_value = [], [], []
        for g in range(2):
            two = slice(2 * g, 2 * g + 2)
            attend_low = r.attend_win[slot, w, :, 256 * g : 256 * g + 256]
            d_value.append(dot(attend_low, mixed_blocks[w][g])[:PAD])
            d_key.append(dot(jnp.concatenate(d_logits[w][two], 1), query_blocks[g])[:PAD] * SCALE)
            d_query.append(dot(jnp.concatenate(turned[w][two], 1), key_blocks[g])[:PAD] * SCALE)
        parts.append(jnp.concatenate(d_query + d_key + d_value, 1))
        yield
    d_qkv = jnp.concatenate(parts, 0).astype(BF16)
    r.d_qkv_all[rows] = d_qkv
    for copy in late_copies(r, s):
        copy.start()
    yield


WEAVE = (-0.005, 0.145, 0.197, 0.403, 0.447)


def run(*stages):
    order = []
    for n, stage in enumerate(stages):
        count = PIECES[stage.__name__]
        places = (np.arange(count) + 0.5) / count
        if n:
            places = np.interp(places, np.linspace(0.0, 1.0, len(WEAVE)), WEAVE)
        order += [(place, n) for place in places]
    for _, n in sorted(order):
        next(stages[n])
    for stage in stages:
        assert next(stage, None) is None


PIECES = {"forward_stage": 5 + 3 * WINDOWS, "backward_stage": 1 + 3 * (MLP // D) + 3 + 3 * WINDOWS + 1}


def down_rows(n):
    return DOWN[n // 2] + (n % 2) * D


def finish(r):
    core = lax.rem(lax.axis_index("dp"), 2)
    grads = r.grads

    def put(start, rows):
        grads[start : start + rows.shape[0]] = rows
        r.grads_low[start : start + rows.shape[0]] = rows.astype(BF16)

    def hand_over(n, start, count):
        span = pl.ds(start, count)
        kept = pl.ds(pl.multiple_of(core * HALF + start, 16), count)
        sent = pl.ds(pl.multiple_of((1 - core) * HALF + start, 16), count)
        copies = [
            pltpu.make_async_copy(grads.at[kept], r.keep.at[span], r.sems.at[2 * n]),
            pltpu.make_async_copy(r.grads_low.at[sent], r.send.at[span], r.sems.at[2 * n + 1]),
        ]
        for copy in copies:
            copy.start()
        return copies

    product = dot_tn(r.first_all[:, : D + 8], r.d_qkv_all[...])
    sums = product[D : D + 8]
    for n in range(3):
        put(QKV + n * D, product[:D, n * D : (n + 1) * D])
    put(PROJ, dot_tn(r.mixed_all[...], r.d_branch_all[...]))
    bias_parts = dot_nt(jnp.concatenate(three_parts(sums), 0), r.w_qkv[...])
    bias_grad = bias_parts[0:1] + bias_parts[8:9] + bias_parts[16:17]
    cross = jnp.zeros((D, 128), F32)
    for n in range(0, 3 * D, 128):
        cross = cross + product[:D, n : n + 128] * r.w_qkv[:, n : n + 128].astype(F32)
    gain_grad = (col_sum(cross.T) - r.bias_one[...] * bias_grad) / r.gain_one[...]
    small = [sums[0:1, :D], sums[0:1, 2 * D :], gain_grad, bias_grad, jnp.zeros((20, D), F32)]
    product = dot_tn(r.second_all[:, : D + 8], r.d_inner_all[...])
    for n in range(MLP // D):
        put(UP + n * D, product[:D, n * D : (n + 1) * D])
    ups = [product[D : D + 1, n * D : (n + 1) * D] for n in range(MLP // D)]
    put(SMALL_ONE, jnp.concatenate([r.sums[0:4]] + ups + [jnp.zeros((24, D), F32)], 0))
    put(SMALL_TWO, jnp.concatenate([table_gradient(r.logit_sums, r.entries, r.by_head)] + small, 0))
    copies = hand_over(0, UP, MLP) + hand_over(1, SMALL_ONE, 32)
    product = dot_tn(r.cot_all[...], r.active_all[...])
    for n in range(MLP // D):
        put(down_rows(n), 0.5 * product[:, n * D : (n + 1) * D])
    copies += hand_over(2, DOWN[0], 2 * D)
    for n in range(STRIPS):
        copies += early_copies(r, n) + late_copies(r, n)
    for copy in copies:
        copy.wait()


class Refs:
    def __init__(self, names, refs):
        self.__dict__.update(zip(names, refs))


INPUTS = [
    "image", "cot", "gather", "mask", "entries", "w_qkv", "w_proj", "w_up", "w_down",
    "halo", "regions", "regions_halo", "spread", "spread_rows", "table",
    "gain_one", "bias_one", "b_query", "b_value", "b_proj", "gain_two", "bias_two", "b_up",
]
NAMES = [name + "_in" for name in INPUTS] + [
    "keep", "send", "tokens_out", "resid_out", "active_out", "d_branch_out", "d_qkv_out",
    "lane_labels", "by_head", "bias_t", "logit_sums", "qkv_win", "attend_win", "sums",
    "first_all", "cot_all", "mixed_all", "second_all", "active_all", "d_inner_all", "d_branch_all", "d_qkv_all",
    "tokens_all", "resid_all", "grads", "grads_low", "sems", "in_sems", "early_sems", "late_sems",
] + INPUTS


LATE_WAITS = 8


def input_copies(r):
    top = WIN + SHIFT
    last = [("w_up", None), ("w_down", None), ("image", slice(top, COLS)), ("cot", slice(top, COLS))]
    large = ["entries", "gather", "image", "w_qkv", "mask", "cot", "w_proj", "halo"]
    names = [name for name in INPUTS if name not in large + ["w_up", "w_down"]] + large
    first = [(name, slice(0, top) if name in ("image", "cot") else None) for name in names]
    copies = []
    for n, (name, rows) in enumerate(first + last):
        source, place = getattr(r, name + "_in"), getattr(r, name)
        if rows is not None:
            source, place = source.at[rows], place.at[rows]
        copies.append(pltpu.make_async_copy(source, place, r.in_sems.at[n]))
    return copies[: len(first)], copies[len(first) :]


def put_labels(r, n, part):
    row = jnp.sum(part * r.spread_rows[...], 0, keepdims=True)
    windows = [row[:, 128 * w : 128 * w + 128] for w in range(WINDOWS)]
    r.lane_labels[n] = jnp.concatenate(windows + [jnp.zeros((2, 128), F32)], 0)


def grads_kernel(*refs):
    r = Refs(NAMES, refs)
    s = pl.program_id(0)

    @pl.when(s == 0)
    def _():
        first, later = input_copies(r)
        for copy in first:
            copy.start()
        r.logit_sums[...] = jnp.zeros_like(r.logit_sums)
        r.sums[...] = jnp.zeros_like(r.sums)
        one = (lane_ids((TOTAL, 128)) == 0).astype(F32).astype(BF16)
        r.first_all[:, D:] = one
        r.second_all[:, D:] = one
        for copy in first[: 1 - LATE_WAITS]:
            copy.wait()
        own = dot(r.regions[...].astype(F32).astype(BF16), r.spread[...])
        for n in range(STRIPS - 1):
            put_labels(r, n, own[n * WIN + SHIFT : (n + 1) * WIN + SHIFT])
        below = dot(r.regions_halo[...], r.spread[...])
        put_labels(r, STRIPS - 1, jnp.concatenate([own[COLS - (WIN - SHIFT) :], below], 0))
        build_bias(r.table[...], r.entries, r.by_head, r.bias_t)
        for copy in first[1 - LATE_WAITS :]:
            copy.wait()
        for copy in later:
            copy.start()
        run(forward_stage(s, r))
        for copy in later:
            copy.wait()
        r.w_down[...] = r.w_down[...] * jnp.bfloat16(0.5)

    @pl.when((s > 0) & (s < STRIPS))
    def _():
        run(backward_stage(s - 1, r), forward_stage(s, r))

    @pl.when(s == STRIPS)
    def _():
        run(backward_stage(s - 1, r))
        finish(r)


def output_strip(active, resid, w_down, b_down, scatter):
    result = resid[...] + b_down[...] + 0.5 * dot(active[...], w_down[...])
    return dot(scatter[...], result.astype(BF16)).astype(BF16)


def image_strip(d_qkv, d_branch, tokens, w_qkv, gain, scatter):
    normal, recip_dev = normalize(tokens[...].astype(F32))
    d_first = dot_nt(d_qkv[...], w_qkv[...])
    grad = d_branch[...].astype(F32) + norm_backward(d_first, normal, recip_dev, gain[...])
    return dot(scatter[...], grad.astype(BF16)).astype(BF16)


there = pl.BlockSpec(memory_space=pl.ANY)


def whole(shape):
    return pl.BlockSpec(shape, lambda s: (0,) * len(shape))


def once(shape):
    return pl.BlockSpec(shape, lambda s: (0,) * len(shape), pipeline_mode=pl.Buffered(1))


def strips(shape):
    return pl.BlockSpec(shape, lambda s: (s,) + (0,) * (len(shape) - 1))


def struct(shape, dtype):
    return jax.ShapeDtypeStruct(shape, dtype)


def params(mebibytes):
    return pltpu.CompilerParams(
        vmem_limit_bytes=mebibytes * 1024 * 1024, dimension_semantics=("arbitrary",)
    )


def pack_kernel(image, cot, regions, rows, labels):
    rows[0:SHIFT] = image[...]
    rows[SHIFT:] = cot[...]
    labels[...] = regions[0:SHIFT].astype(F32).astype(BF16)


def pack_first_rows(image, cot, regions):
    return pl.pallas_call(
        pack_kernel,
        grid=(1,),
        in_specs=[whole((SHIFT, COLS, D)), whole((SHIFT, COLS, D)), whole(regions.shape)],
        out_specs=[whole((2 * SHIFT, COLS, D)), whole((SHIFT, COLS))],
        out_shape=[pltpu.VMEM((2 * SHIFT, COLS, D), BF16), pltpu.VMEM((SHIFT, COLS), BF16)],
        compiler_params=params(62),
        name="pack_first_rows",
    )(image, cot, regions)


def run_grads(*args):
    return pl.pallas_call(
        grads_kernel,
        grid=(STRIPS + 1,),
        in_specs=[there] * len(args),
        out_specs=[there] * 7,
        out_shape=[
            pltpu.VMEM((HALF, D), F32),
            pltpu.VMEM((HALF, D), BF16),
            struct((TOTAL, D), BF16),
            struct((TOTAL, D), F32),
            struct((TOTAL, MLP), BF16),
            struct((TOTAL, D), BF16),
            struct((TOTAL, 3 * D), BF16),
        ],
        scratch_shapes=[
            pltpu.VMEM((STRIPS, 8, 128), F32),
            pltpu.VMEM((HEADS, 8, 128), F32),
            pltpu.VMEM((PAD, HEADS * LANES), F32),
            pltpu.VMEM((PAD, HEADS * LANES), F32),
            pltpu.VMEM((2, WINDOWS, LANES, 3 * D), BF16),
            pltpu.VMEM((2, WINDOWS, LANES, HEADS * LANES), BF16),
            pltpu.VMEM((8, D), F32),
            pltpu.VMEM((TOTAL, D + 128), BF16),
            pltpu.VMEM((TOTAL, D), BF16),
            pltpu.VMEM((TOTAL, D), BF16),
            pltpu.VMEM((TOTAL, D + 128), BF16),
            pltpu.VMEM((TOTAL, MLP), BF16),
            pltpu.VMEM((TOTAL, MLP), BF16),
            pltpu.VMEM((TOTAL, D), BF16),
            pltpu.VMEM((TOTAL, 3 * D), BF16),
            pltpu.VMEM((TOTAL, D), BF16),
            pltpu.VMEM((TOTAL, D), F32),
            pltpu.VMEM((2 * HALF, D), F32),
            pltpu.VMEM((2 * HALF, D), BF16),
            pltpu.SemaphoreType.DMA((6,)),
            pltpu.SemaphoreType.DMA((len(INPUTS) + 2,)),
            pltpu.SemaphoreType.DMA((STRIPS, 2)),
            pltpu.SemaphoreType.DMA((STRIPS, 3)),
        ]
        + [pltpu.VMEM(a.shape, a.dtype) for a in args],
        compiler_params=params(58),
        cost_estimate=pl.CostEstimate(
            flops=2 * TOTAL * 10 * D * MLP, bytes_accessed=20_000_000, transcendentals=0
        ),
        name="all_gradients",
    )(*args)


def run_field(strip, name, which, blocks, others, field=None, tails=None):
    lower = field is None
    first = FIELD_STEPS if lower else 0
    given = [a for a in (field, tails) if a is not None]
    inputs = len(blocks) + len(others)
    shapes = [struct((COLS, COLS, D), BF16)] + [struct((2, SENT, COLS, D), BF16)] * lower

    def kernel(*refs):
        out = refs[inputs + len(given)]
        below = refs[inputs + len(given) + 1] if lower else None
        put_rows(strip(*refs[:inputs]), first, which, out, below, *refs[-2:])

    return pl.pallas_call(
        kernel,
        grid=(FIELD_STEPS,),
        in_specs=[pl.BlockSpec((STRIP, a.shape[1]), lambda t: (first + t, 0)) for a in blocks]
        + [whole(a.shape) for a in others]
        + [there] * len(given),
        out_specs=[there] * len(shapes),
        out_shape=shapes,
        scratch_shapes=[pltpu.VMEM((2, WIN, COLS, D), BF16), pltpu.SemaphoreType.DMA((3,))],
        input_output_aliases={inputs: 1 if lower else 0} if given else {},
        compiler_params=params(60),
        cost_estimate=pl.CostEstimate(
            flops=2 * TOTAL * 4 * D * D, bytes_accessed=9_000_000, transcendentals=0
        ),
        name=name,
    )(*blocks, *others, *given)


def unpack_half(half, rows, w_up, w_down, w_proj, w_qkv, stage, sems):
    def down(first):
        for n in range(2):
            stage[n * D : (n + 1) * D, :D] = rows[first + n * D : first + (n + 1) * D].astype(F32).T
        at = pl.ds(half * 2 * D, 2 * D)
        return pltpu.make_async_copy(stage.at[pl.ds(0, 2 * D), pl.ds(0, D)], w_down.at[at], sems.at[0])

    def wide(out, first, count, at, sem):
        for n in range(count):
            part = rows[first + n * D : first + (n + 1) * D].astype(F32)
            stage[at : at + D, n * D : (n + 1) * D] = part
        return pltpu.make_async_copy(stage.at[pl.ds(at, D), pl.ds(0, count * D)], out, sems.at[sem])

    copies = []
    if half == 0:
        copies.append(wide(w_up, UP, MLP // D, 2 * D, 1))
        copies[-1].start()
        copies.append(down(DOWN[0]))
        copies[-1].start()
    else:
        copies.append(wide(w_qkv, QKV - HALF, 3, 2 * D, 1))
        copies[-1].start()
        copies.append(wide(w_proj, PROJ - HALF, 1, 3 * D, 2))
        copies[-1].start()
        copies.append(down(DOWN[1] - HALF))
        copies[-1].start()
    for copy in copies:
        copy.wait()


def unpack_first_kernel(own, *refs):
    core = lax.rem(lax.axis_index("dp"), 2)
    for half in range(2):

        @pl.when(core == half)
        def _():
            unpack_half(half, own, *refs)


def unpack_second_kernel(
    other, own, in_up, in_down, in_proj, in_qkv, w_up, w_down, w_proj, w_qkv,
    gain_one, bias_one, b_query, b_value, table, b_proj, gain_two, bias_two, b_up, b_down, stage, sems,
):
    core = lax.rem(lax.axis_index("dp"), 2)
    for half in range(2):

        @pl.when(core != half)
        def _():
            unpack_half(half, other, w_up, w_down, w_proj, w_qkv, stage, sems)

    mine, others = own[...].astype(F32), other[SMALL_ONE:].astype(F32)
    first = jnp.where(core == 0, mine, others)
    second = jnp.where(core == 0, others, mine)
    for n, out in enumerate((gain_two, bias_two, b_proj, b_down)):
        out[...] = first[n : n + 1]
    for n in range(MLP // D):
        b_up[:, n * D : (n + 1) * D] = first[4 + n : 5 + n]
    table[...] = second[:HEADS, :ENTRIES]
    for n, out in enumerate((b_query, b_value, gain_one, bias_one)):
        out[...] = second[HEADS + n : HEADS + n + 1]


LARGE = ((D, MLP), (MLP, D), (D, D), (D, 3 * D))
UNPACK_SCRATCH = [pltpu.VMEM((4 * D, MLP), F32), pltpu.SemaphoreType.DMA((3,))]
def unpack_first(own):
    return pl.pallas_call(
        unpack_first_kernel,
        grid=(1,),
        in_specs=[whole(own.shape)],
        out_specs=[there] * 4,
        out_shape=[struct(shape, F32) for shape in LARGE],
        scratch_shapes=UNPACK_SCRATCH,
        compiler_params=params(24),
        cost_estimate=pl.CostEstimate(flops=0, bytes_accessed=2_400_000, transcendentals=0),
        name="unpack_own_half",
    )(own)


def unpack_second(other, own, large):
    one, four = (1, D), (1, MLP)
    shapes = [one, one, one, one, (HEADS, ENTRIES), one, one, one, four, one]
    out = pl.pallas_call(
        unpack_second_kernel,
        grid=(1,),
        in_specs=[whole(other.shape), pl.BlockSpec((32, D), lambda s: (SMALL_ONE // 32, 0))] + [there] * 4,
        out_specs=[there] * 4 + [whole(shape) for shape in shapes],
        out_shape=[struct(shape, F32) for shape in LARGE] + [struct(shape, F32) for shape in shapes],
        scratch_shapes=UNPACK_SCRATCH,
        input_output_aliases={2: 0, 3: 1, 4: 2, 5: 3},
        compiler_params=params(24),
        name="unpack_other_half",
    )(other, own, *large)
    w_up, w_down, w_proj, w_qkv = out[:4]
    gain_one, bias_one, b_query, b_value, table, b_proj, gain_two, bias_two, b_up, b_down = out[4:]
    return (
        gain_one[0], bias_one[0], w_qkv, b_query[0], b_value[0], table.T, w_proj, b_proj[0],
        gain_two[0], bias_two[0], w_up, b_up[0], w_down, b_down[0],
    )


def coords(index):
    dp, space = divmod(index, 32)
    return {"c": dp % 2, "y": dp // 2 + 2 * ((space // 4) % 2), "x": space % 4, "z": space // 8}


def index_of(c, y, x, z):
    return ((y % 2) * 2 + c) * 32 + z * 8 + (y // 2) * 4 + x


DISTANCES = (2, 1, 3)
STAGES = (("z", "y"), ("y", "x"), ("x", "z"))


def other_core():
    return [(i, index_of(**(coords(i) | {"c": 1 - i // 32 % 2}))) for i in range(128)]


def around(stage, distance):
    out = []
    for i in range(128):
        at = coords(i)
        axis = stage[at["c"]]
        out.append((i, index_of(**(at | {axis: (at[axis] + distance) % 4}))))
    return out


def take(rows, start, count):
    return lax.dynamic_slice_in_dim(rows, start, count, 0)


def sum_everywhere(mine, got_core, at, pieces):
    made = {}
    left = list(pieces)

    def exchange(stage, sends, own):
        nonlocal made
        ahead, beside = left.pop(0)
        early = ahead(made)
        got = [lax.ppermute(sends[d], AXES, around(stage, d)) for d in DISTANCES]
        made, own = lax.optimization_barrier((made, own))
        made = made | beside(made)
        got, made, early, own = lax.optimization_barrier((got, made, early, own))
        made = made | early
        return dict(zip(DISTANCES, got)), own

    def place(stage):
        return jnp.where(at["c"] == 0, at[stage[0]], at[stage[1]])

    stage = STAGES[0]
    here = place(stage)
    count = mine.shape[0] // 4

    def part(which):
        start = which * count
        return take(mine, start, count) + take(got_core, start, count).astype(F32)

    sends = {d: part((here + d) % 4).astype(BF16) for d in DISTANCES}
    got, rows = exchange(stage, sends, part(here))
    for d in DISTANCES:
        rows = rows + got[d].astype(F32)
    low = rows.astype(BF16)
    for stage in STAGES[1:]:
        got, low = exchange(stage, {d: low for d in DISTANCES}, low)
        pairs = low.astype(F32) + got[2].astype(F32), got[1].astype(F32) + got[3].astype(F32)
        low = (pairs[0] + pairs[1]).astype(BF16)
    ahead, beside = left.pop(0)
    parts = {0: low} | {d: lax.ppermute(low, AXES, around(STAGES[0], d)) for d in (1, 2, 3)}
    others = {d: lax.ppermute(rows, AXES, other_core()) for d, rows in parts.items()}
    made = made | beside(made)

    def assemble(parts, here):
        out = jnp.zeros((4 * count, D), BF16)
        for d, rows in parts.items():
            out = lax.dynamic_update_slice(out, rows, ((here - d) % 4 * count, 0))
        return out

    there_axis = jnp.where(at["c"] == 0, at[STAGES[0][1]], at[STAGES[0][0]])
    own = assemble(parts, here)
    large = unpack_first(own)
    others, large, made = lax.optimization_barrier((others, large, made))
    return own, assemble(others, there_axis), large, made


def body(
    image_in, cotangent, regions, first_gain, first_bias, qkv_weight, query_bias, value_bias,
    position_table, proj_weight, proj_bias, second_gain, second_bias, up_weight, up_bias,
    down_weight, down_bias,
):
    many = lax.axis_size("dp") * lax.axis_size("space") == 128
    me = lax.axis_index(AXES)
    at = coords(me)
    first_rows = pack_first_rows(image_in, cotangent, regions)
    halo, regions_halo = from_behind(first_rows, "space", -1)
    gather = gather_matrix()
    spread, spread_rows = label_matrices()
    entries = jnp.asarray(entry_matrix(), BF16)
    mask = jnp.asarray(head_mask(), BF16)
    scatter = jnp.asarray(gather.T, BF16)
    mine, send, tokens, resid, active, d_branch, d_qkv = run_grads(
        image_in, cotangent, jnp.asarray(gather, BF16), mask, entries, qkv_weight, proj_weight, up_weight, down_weight,
        halo, regions, regions_halo, jnp.asarray(spread, BF16), jnp.asarray(spread_rows), position_table.T,
        first_gain[None], first_bias[None], query_bias[None], value_bias[None], proj_bias[None],
        second_gain[None], second_bias[None], up_bias[None],
    )
    if many:
        got = lax.ppermute(send, AXES, other_core())

    def block_output(*given):
        others = (down_weight, down_bias[None], scatter)
        return run_field(output_strip, "block_output", 0, (active, resid), others, *given)

    def image_gradient(*given):
        others = (qkv_weight, first_gain[None], scatter)
        return run_field(image_strip, "image_gradient", 1, (d_qkv, d_branch, tokens), others, *given)

    def lower_out(made):
        out, tails = block_output()
        return {"out": out, "tails": tails}

    def lower_image(made):
        image, tails = image_gradient(None, made["tails"])
        return {"image": image, "tails": tails}

    def upper_out(made):
        return made | {"out": block_output(made["out"])[0]}

    def return_rows(made):
        return {"returned": from_behind(made["tails"], "space", 1)}

    def upper_image(made):
        return made | {"image": image_gradient(made["image"])[0]}

    def nothing(made):
        return {}

    def fields(made):
        first, at = made["returned"][:, SENT - SHIFT :], (0, 0, 0)
        return {
            "out": lax.dynamic_update_slice(made["out"], first[0], at),
            "image": lax.dynamic_update_slice(made["image"], first[1], at),
        }

    def upper_out_and_fields(made):
        made = made | upper_out(made)
        return made | fields(made)

    pieces = [(nothing, lower_out), (nothing, lower_image), (return_rows, upper_image), (nothing, upper_out_and_fields)]
    if many:
        own, other, large, made = sum_everywhere(mine, got, at, pieces)
    else:
        made = {}
        for ahead, beside in pieces:
            made = made | ahead(made) | beside(made)
        own, other = mine.astype(BF16), send
        large = unpack_first(own)
    return (made["out"], made["image"]) + unpack_second(other, own, large)


def solution(mesh):
    tokens = P(AXES, None, None)
    return jax.shard_map(
        body,
        mesh=mesh,
        in_specs=(tokens, tokens, P(AXES, None)) + (P(),) * 14,
        out_specs=(tokens, tokens) + (P(),) * 14,
        check_vma=False,
    )
```
